32 devices in a mesh: dp: 16 (over z, x, core), seq: 2 (over y).
Axes of the slice: x: 2, y: 2, z: 4, core: 2. Of those that a mesh axis runs over, the one named last changes fastest.
Arguments:
- tokens: bfloat16 [8192, 2048], P(('dp', 'seq')), may hold values from -6 to 6
- cotangent: bfloat16 [8192, 2048], P(('dp', 'seq')), may hold values from -6 to 6
- seq_lengths: int32 [16], replicated, may hold values from 257 to 512, as said below
- assignment: int32 [16], replicated, may hold values from 0 to 15, each once
- w_query: bfloat16 [2048, 2048], P(('dp', 'seq')), may hold values from -0.1875 to 0.1875
- w_key: bfloat16 [2048, 2048], P(('dp', 'seq')), may hold values from -0.1875 to 0.1875
- w_value: bfloat16 [2048, 2048], P(('dp', 'seq')), may hold values from -0.125 to 0.125
- w_out: bfloat16 [2048, 2048], P(('dp', 'seq')), may hold values from -0.5 to 0.5
- w_gate: bfloat16 [2048, 8192], P(('dp', 'seq')), may hold values from -0.125 to 0.125
- w_up: bfloat16 [2048, 8192], P(('dp', 'seq')), may hold values from -0.125 to 0.125
- w_down: bfloat16 [8192, 2048], P(('dp', 'seq')), may hold values from -0.0625 to 0.0625
- gain_attn: bfloat16 [2048], P(('dp', 'seq')), may hold values from 0.5 to 1.5
- gain_mlp: bfloat16 [2048], P(('dp', 'seq')), may hold values from 0.5 to 1.5
Outputs:
- output: bfloat16 [8192, 2048], P(('dp', 'seq'))
- grad_input: float32 [8192, 2048], P(('dp', 'seq'))
- grad_w_query: float32 [2048, 2048], P(('dp', 'seq'))
- grad_w_key: float32 [2048, 2048], P(('dp', 'seq'))
- grad_w_value: float32 [2048, 2048], P(('dp', 'seq'))
- grad_w_out: float32 [2048, 2048], P(('dp', 'seq'))
- grad_w_gate: float32 [2048, 8192], P(('dp', 'seq'))
- grad_w_up: float32 [2048, 8192], P(('dp', 'seq'))
- grad_w_down: float32 [8192, 2048], P(('dp', 'seq'))
- grad_gain_attn: float32 [2048], P(('dp', 'seq'))
- grad_gain_mlp: float32 [2048], P(('dp', 'seq'))
The draws below stay inside these ranges and needn't reach their ends.
Inputs may be any that keep to these rules, and one draw needn't show every extreme that they name: `seq_lengths`: each sequence is longer than one device's 256 rows; some sequence has exactly 512.
All inputs are finite; a program needn't handle non-finite values.
Results may differ from the reference program's by a relative error of at most 0.014.
The reference program's roundings to bfloat16 on the way count: a program that leaves them out, or rounds other values in their place, can miss the bound.
Values may be sent and summed in bfloat16 or wider, within the bound.
A program may use at most 512 MiB of HBM per device.

```python
import jax
import jax.numpy as jnp
from jax import lax

D = 2048
FF = 8192
HEADS = 32
HEAD_DIM = 64
TOK_DEV = 256
SEQ_LEN = 512
GROUPS = 16
TOKENS = 8192


def draw_seq_lengths(key, part):
    key = jax.random.fold_in(key, 7)
    first_key, second_key = jax.random.split(key)
    drawn = jax.random.randint(first_key, (GROUPS,), TOK_DEV + 1, SEQ_LEN + 1)
    chosen = jax.random.randint(second_key, (), 0, GROUPS)
    return jnp.where(jnp.arange(GROUPS) == chosen, SEQ_LEN, drawn).astype(jnp.int32)


def levels(stream_key, shape, shards, least, largest):
    level = 1.0
    for axis_at, blocks in shards:
        heights = jax.random.uniform(jax.random.fold_in(jax.random.fold_in(stream_key, 6), axis_at), (blocks,), jnp.float32, least / len(shards), largest / len(shards))
        level = level * jnp.repeat(jnp.exp(heights), shape[axis_at] // blocks).reshape((-1,) + (1,) * (len(shape) - 1 - axis_at))
    return level


def centred(key, extent, deviation, limit, pieces=(), dtype=jnp.bfloat16):
    values = jax.random.normal(key, extent, jnp.float32) * deviation
    if len(pieces) > 0:
        values = levels(key, extent, pieces, -0.22, 0.18) * values
    return jnp.clip(values, min=-limit, max=limit).astype(dtype)


def setup_inputs(seed: int = 0) -> dict:
    key_of = jax.random.split(jax.random.key(seed), 14)
    return {
        "tokens": centred(key_of[0], (TOKENS, D), 1.0, 6.0, ((0, 32),)),
        "cotangent": centred(key_of[1], (TOKENS, D), 1.0, 6.0, ((0, 32),)),
        "seq_lengths": draw_seq_lengths(jax.random.fold_in(key_of[13], 71), 0),
        "assignment": jax.random.permutation(key_of[3], GROUPS).astype(jnp.int32),
        "w_query": centred(key_of[4], (D, D), (D // 2) ** -0.5, 0.1875, ((0, 32),)),
        "w_key": centred(key_of[5], (D, D), (D // 2) ** -0.5, 0.1875, ((0, 32),)),
        "w_value": centred(key_of[6], (D, D), D ** -0.5, 0.125, ((0, 32),)),
        "w_out": centred(key_of[7], (D, D), (D // 16) ** -0.5, 0.5, ((0, 32),)),
        "w_gate": centred(key_of[8], (D, FF), D ** -0.5, 0.125, ((0, 32),)),
        "w_up": centred(key_of[9], (D, FF), D ** -0.5, 0.125, ((0, 32),)),
        "w_down": centred(key_of[10], (FF, D), FF ** -0.5, 0.0625, ((0, 32),)),
        "gain_attn": jnp.clip(1.0 + 0.1 * jax.random.normal(key_of[11], (D,), jnp.float32), 0.5, 1.5).astype(jnp.bfloat16),
        "gain_mlp": jnp.clip(1.0 + 0.1 * jax.random.normal(key_of[12], (D,), jnp.float32), 0.5, 1.5).astype(jnp.bfloat16),
    }


norm_eps = 1e-05
rope_base = 130000.0

@jax.custom_vjp
def low(v):
    return lax.optimization_barrier(v.astype(jnp.bfloat16)).astype(jnp.float32)

@jax.custom_vjp
def low_back(v):
    return v

def low_keep(v):
    return (low(v), None)

def low_pass(kept, grad):
    return (grad,)

def back_keep(v):
    return (v, None)

def back_low(kept, grad):
    return (low(grad),)
low.defvjp(low_keep, low_pass)
low_back.defvjp(back_keep, back_low)

def product(left, right):
    return jnp.dot(left, right, precision=lax.Precision.HIGHEST, preferred_element_type=jnp.float32)

def rms_norm(values, gain):
    factor = lax.rsqrt(lax.optimization_barrier(jnp.mean(values * values, axis=-1, keepdims=True)) + norm_eps)
    return values * factor * gain

def rope_tables(positions, head_size):
    halves = head_size // 2
    frequency = rope_base ** (-(jnp.arange(halves).astype(jnp.float32) * 2.0 / head_size))
    angles = positions.astype(jnp.float32)[:, None] * frequency[None, :]
    cosine = jnp.cos(angles)
    sine = jnp.sin(angles)
    return (jnp.concatenate([cosine, cosine], axis=1), jnp.concatenate([sine, sine], axis=1))

def rotate(values, cosine, sine):
    halves = values.shape[-1] // 2
    turned = jnp.concatenate([-values[..., halves:], values[..., :halves]], axis=-1)
    return values * cosine[:, None, :] + turned * sine[:, None, :]

def group_layer(params, rows_in, length):
    w_query, w_key, w_value, w_out, w_gate, w_up, w_down, gain_attn, gain_mlp = params
    count = rows_in.shape[0]
    positions = jnp.arange(count).astype(jnp.int32)
    valid_rows = (positions < length).astype(jnp.float32)
    normed = low(rms_norm(rows_in, gain_attn))
    cosine, sine = rope_tables(positions, HEAD_DIM)
    q_lin = low_back(product(normed, w_query)).reshape(count, HEADS, HEAD_DIM)
    k_lin = low_back(product(normed, w_key)).reshape(count, HEADS, HEAD_DIM)
    queries = low(rotate(q_lin, cosine, sine))
    keys = low(rotate(k_lin, cosine, sine))
    values = low(low_back(product(normed, w_value))).reshape(count, HEADS, HEAD_DIM)
    scale = HEAD_DIM ** (-0.5)
    scores = low_back(jnp.einsum('qhe,khe->hqk', queries, keys, precision=lax.Precision.HIGHEST) * scale)
    allowed = (positions[None, :] <= positions[:, None]) & (positions[None, :] < length)
    scores = jnp.where(allowed[None], scores, -1e+30)
    row_max = lax.optimization_barrier(jnp.max(scores, axis=-1, keepdims=True))
    weights = jnp.exp(scores - row_max)
    probs = low(weights / lax.optimization_barrier(jnp.sum(weights, axis=-1, keepdims=True)))
    mixed = jnp.einsum('hqk,khe->qhe', probs, values, precision=lax.Precision.HIGHEST)
    mixed = low(low_back(mixed.reshape(count, HEADS * HEAD_DIM)))
    attended = rows_in + low_back(product(mixed, w_out))
    normed2 = low(rms_norm(attended, gain_mlp))
    gate = low_back(product(normed2, w_gate))
    upper = low_back(product(normed2, w_up))
    active = low(jax.nn.silu(gate) * upper)
    result = attended + low_back(product(active, w_down))
    return result * valid_rows[:, None]

def reference(tokens, cotangent, seq_lengths, assignment, w_query, w_key, w_value, w_out, w_gate, w_up, w_down, gain_attn, gain_mlp):
    slot_count = assignment.shape[0]
    slot_lengths = seq_lengths[assignment]
    params = tuple((item.astype(jnp.float32) for item in (w_query, w_key, w_value, w_out, w_gate, w_up, w_down, gain_attn, gain_mlp)))
    inputs = tokens.astype(jnp.float32)

    def forward(rows_in, weights):
        shaped = rows_in.reshape(slot_count, -1, rows_in.shape[1])

        def slot_step(carry, item):
            return (carry, group_layer(weights, item[0], item[1]))
        _, results = lax.scan(jax.checkpoint(slot_step), jnp.zeros((), jnp.float32), (shaped, slot_lengths))
        return results.reshape(rows_in.shape)
    result, pullback = jax.vjp(forward, inputs, params)
    grad_input, grads = pullback(cotangent.astype(jnp.float32))
    return (result.astype(jnp.bfloat16), grad_input, grads[0], grads[1], grads[2], grads[3], grads[4], grads[5], grads[6], grads[7], grads[8])
```

```python
import jax
import jax.numpy as jnp
from jax import lax
from jax.sharding import Mesh, PartitionSpec as P

HEAD_DIM = 64
norm_eps = 1e-05
rope_base = 130000.0
AXES = ("z", "x", "c", "y")
LOW = jnp.bfloat16
FULL = jnp.float32


def swap_x(value):
    return lax.ppermute(value, "x", [(0, 1), (1, 0)])


def swap_y(value):
    return lax.ppermute(value, "y", [(0, 1), (1, 0)])


def swap_plane(value, step):
    return lax.ppermute(value, ("x", "y"), [(at, at ^ step) for at in range(4)])


def plane_gather(value):
    half = value.shape[0] // 2
    top, low = value[:half], value[half:]
    top_y = swap_y(top)
    low_x = swap_x(low)
    top_far = swap_x(jnp.concatenate([top, top_y], axis=0))
    low_far = swap_y(jnp.concatenate([low, low_x], axis=0))
    return jnp.concatenate(
        [top, low, top_y, low_far[:half], top_far[:half], low_x, top_far[half:], low_far[half:]],
        axis=0,
    )


def plane_reduce(value):
    count = value.shape[0] // 4
    half = count // 2
    own, by_y, by_x, by_d = (value[at * count : (at + 1) * count] for at in range(4))
    top_in = swap_x(jnp.concatenate([by_x[:half], by_d[:half]], axis=0).astype(LOW)).astype(FULL)
    low_in = swap_y(jnp.concatenate([by_y[half:], by_d[half:]], axis=0).astype(LOW)).astype(FULL)
    top_last = swap_y((by_y[:half] + top_in[half:]).astype(LOW)).astype(FULL)
    low_last = swap_x((by_x[half:] + low_in[half:]).astype(LOW)).astype(FULL)
    return jnp.concatenate(
        [own[:half] + top_in[:half] + top_last, own[half:] + low_in[:half] + low_last], axis=0
    )


def columns_by_part(weight, deep):
    rows, columns = weight.shape
    if deep:
        parts = weight.reshape(rows, -1, 2, 2, 2, columns // (8 * deep))
        return parts.transpose(2, 4, 0, 1, 3, 5).reshape(4, rows, columns // 4)
    return weight.reshape(rows, 4, columns // 4).transpose(1, 0, 2)


def columns_from_parts(parts, deep):
    _, rows, width = parts.shape
    columns = 4 * width
    if deep:
        apart = parts.reshape(2, 2, rows, deep, 2, columns // (8 * deep))
        return apart.transpose(2, 3, 0, 4, 1, 5).reshape(rows, columns)
    return parts.transpose(1, 0, 2).reshape(rows, columns)


def plane_exchange(parts, mine):
    got = [lax.dynamic_index_in_dim(parts, mine, 0, keepdims=False)]
    for step in (1, 2, 3):
        sent = lax.dynamic_index_in_dim(parts, mine ^ step, 0, keepdims=False)
        got.append(swap_plane(sent, step))
    stacked = jnp.stack(got)
    return jnp.concatenate(
        [lax.dynamic_index_in_dim(stacked, mine ^ at, 0, keepdims=True) for at in range(4)], axis=0
    )


def gather_small(value):
    for axis in ("y", "c", "x"):
        other = lax.ppermute(value, axis, [(0, 1), (1, 0)])
        first = lax.axis_index(axis) == 0
        value = jnp.where(
            first,
            jnp.concatenate([value, other], axis=-1),
            jnp.concatenate([other, value], axis=-1),
        )
    count = lax.axis_size("z")
    step = 1
    while step < count:
        other = lax.ppermute(value, "z", [(at, at ^ step) for at in range(count)])
        first = (lax.axis_index("z") // step) % 2 == 0
        value = jnp.where(
            first,
            jnp.concatenate([value, other], axis=-1),
            jnp.concatenate([other, value], axis=-1),
        )
        step *= 2
    return value


def scatter_small(value):
    total = lax.psum(value, AXES)
    part = value.shape[-1] // (8 * lax.axis_size("z"))
    index = (
        (lax.axis_index("z") * 2 + lax.axis_index("x")) * 2 + lax.axis_index("c")
    ) * 2 + lax.axis_index("y")
    return lax.dynamic_slice_in_dim(total, index * part, part, axis=-1)


def factor_of(values):
    return lax.rsqrt(jnp.mean(values * values, axis=-1, keepdims=True) + norm_eps)


def norm_back(values, gain, grads):
    factor = factor_of(values)
    weighted = grads * gain
    inner = jnp.mean(weighted * values, axis=-1, keepdims=True)
    grad_gain = jnp.sum(grads * values * factor, axis=0)
    return factor * weighted - values * (factor * factor * factor) * inner, grad_gain


def rope_tables(positions):
    halves = HEAD_DIM // 2
    frequency = rope_base ** (-(jnp.arange(halves).astype(FULL) * 2.0 / HEAD_DIM))
    angles = positions.astype(FULL)[:, None] * frequency[None, :]
    cosine = jnp.cos(angles)
    sine = jnp.sin(angles)
    return (
        jnp.concatenate([cosine, cosine], axis=1)[:, None, :],
        jnp.concatenate([sine, sine], axis=1)[:, None, :],
    )


def rotate(values, cosine, sine):
    halves = HEAD_DIM // 2
    turned = jnp.concatenate([-values[..., halves:], values[..., :halves]], axis=-1)
    return values * cosine + turned * sine


def unrotate(grads, cosine, sine):
    halves = HEAD_DIM // 2
    scaled = grads * sine
    turned = jnp.concatenate([scaled[..., halves:], -scaled[..., :halves]], axis=-1)
    return grads * cosine + turned


def dot(left, right):
    return jnp.dot(left, right, preferred_element_type=FULL)


def dot_rows(left, right):
    return lax.dot_general(left, right, (((0,), (0,)), ((), ())), preferred_element_type=FULL)


def dot_through(left, right):
    return lax.dot_general(left, right, (((1,), (1,)), ((), ())), preferred_element_type=FULL)


def body(
    tokens,
    cotangent,
    seq_lengths,
    assignment,
    w_query,
    w_key,
    w_value,
    w_out,
    w_gate,
    w_up,
    w_down,
    gain_attn,
    gain_mlp,
):
    rows, width = tokens.shape
    depth = lax.axis_size("z")
    deep = depth
    at_z, at_x, at_c, at_y = (lax.axis_index(axis) for axis in AXES)
    mine = at_x * 2 + at_y
    whole_heads = w_out.shape[0] % HEAD_DIM == 0
    head_deep = depth if whole_heads else 0
    head_width = width // 4
    unit_width = w_gate.shape[1] // 4
    scale = HEAD_DIM ** (-0.5)

    def to_mixed(values):
        apart = values.reshape(values.shape[0], depth, 2, 2, -1)
        return apart.transpose(0, 1, 3, 2, 4).reshape(values.shape)

    slot_at = [(at_z * 2 + x) * 2 + at_c for x in (at_x, 1 - at_x)]
    slot_length = [seq_lengths[assignment[slot]] for slot in slot_at]
    row = jnp.arange(rows)
    position = jnp.concatenate([at_y * rows + row, (1 - at_y) * rows + row])
    valid_rows = (at_y * rows + row < slot_length[0]).astype(FULL)[:, None]

    gains = gather_small(jnp.stack([gain_attn, gain_mlp])).astype(FULL)
    gain_one, gain_two = gains[0], gains[1]

    qkv_parts = jnp.concatenate(
        [columns_by_part(weight, head_deep) for weight in (w_query, w_key, w_value)], axis=2
    )
    qkv_rows = plane_exchange(qkv_parts, mine).reshape(4 * qkv_parts.shape[1], -1)
    full_qkv = lax.all_gather(qkv_rows, ("z", "c"), axis=0, tiled=True)
    if whole_heads:
        full_out = lax.all_gather(w_out, ("z", "c"), axis=0, tiled=True)
    else:
        every = lax.all_gather(w_out, AXES, axis=0, tiled=True)
        full_out = lax.dynamic_slice_in_dim(every, mine * head_width, head_width, axis=0)
    gu_parts = jnp.concatenate([columns_by_part(weight, deep) for weight in (w_gate, w_up)], axis=2)
    gu_rows = plane_exchange(gu_parts, mine).reshape(4 * gu_parts.shape[1], -1)
    full_gu = lax.all_gather(gu_rows, ("z", "c"), axis=0, tiled=True)
    full_down = lax.all_gather(w_down, ("z", "c"), axis=0, tiled=True)

    inputs = tokens.astype(FULL)
    normed = to_mixed((inputs * factor_of(inputs) * gain_one).astype(LOW))
    normed_all = plane_gather(normed)
    grad_out = cotangent.astype(FULL) * valid_rows
    grad_low = grad_out.astype(LOW)
    grad_low_all = plane_gather(grad_low)

    qkv = dot(normed_all, full_qkv)
    cosine, sine = rope_tables(position)
    cosine = jnp.concatenate([cosine, cosine], axis=0)
    sine = jnp.concatenate([sine, sine], axis=0)
    total_rows = 4 * rows

    def heads_of(values):
        return values.reshape(total_rows, -1, HEAD_DIM)

    queries = rotate(heads_of(qkv[:, :head_width]), cosine, sine).astype(LOW)
    keys = rotate(heads_of(qkv[:, head_width : 2 * head_width]), cosine, sine).astype(LOW)
    values = heads_of(qkv[:, 2 * head_width :]).astype(LOW)

    def by_slot(item):
        return item.reshape(2, 2 * rows, -1, HEAD_DIM).transpose(0, 2, 1, 3)

    queries, keys, values = by_slot(queries), by_slot(keys), by_slot(values)
    causal = position[None, :] <= position[:, None]
    allowed = jnp.stack([causal & (position[None, :] < length) for length in slot_length])[:, None]

    scores = jnp.einsum("shqe,shke->shqk", queries, keys, preferred_element_type=FULL) * scale
    scores = jnp.where(allowed, scores, -1e30)
    row_max = jnp.max(scores, axis=-1, keepdims=True)
    weights = jnp.exp(scores - row_max)
    total = jnp.sum(weights, axis=-1, keepdims=True)
    probs_full = weights / total
    probs = probs_full.astype(LOW)
    mixed = jnp.einsum("shqk,shke->shqe", probs, values, preferred_element_type=FULL)
    mixed = mixed.astype(LOW).transpose(0, 2, 1, 3).reshape(total_rows, head_width)
    attended = inputs + plane_reduce(dot(mixed, full_out))

    normed2 = to_mixed((attended * factor_of(attended) * gain_two).astype(LOW))
    normed2_all = plane_gather(normed2)
    gate = dot(normed2_all, full_gu[:, :unit_width])
    upper = dot(normed2_all, full_gu[:, unit_width:])
    sigmoid = jax.nn.sigmoid(gate)
    silu = gate * sigmoid
    active = (silu * upper).astype(LOW)
    result = attended + plane_reduce(dot(active, full_down))
    output = (result * valid_rows).astype(LOW)

    def scattered(grads):
        return lax.psum_scatter(grads.astype(LOW), ("z", "c"), scatter_dimension=0, tiled=True)

    grad_w_down = scattered(dot_rows(active, grad_low_all)).astype(FULL)
    grad_active = dot_through(grad_low_all, full_down)
    grad_gate = (grad_active * upper * sigmoid * (1.0 + gate * (1.0 - sigmoid))).astype(LOW)
    grad_upper = (grad_active * silu).astype(LOW)
    grad_gu = jnp.concatenate([grad_gate, grad_upper], axis=1)
    grad_gu_rows = scattered(dot_rows(normed2_all, grad_gu))
    grad_normed2 = to_mixed_back(plane_reduce(dot_through(grad_gu, full_gu)), depth)
    from_norm, grad_gain_mlp = norm_back(attended, gain_two, grad_normed2)
    grad_attended = grad_out + from_norm

    grad_branch = plane_gather(grad_attended.astype(LOW))
    grad_w_out = dot_rows(mixed, grad_branch)
    if whole_heads:
        grad_w_out = scattered(grad_w_out).astype(FULL)
    else:
        spread = lax.dynamic_update_slice_in_dim(
            jnp.zeros((width, width), FULL), grad_w_out, mine * head_width, axis=0
        )
        grad_w_out = lax.psum_scatter(spread, AXES, scatter_dimension=0, tiled=True)
    grad_mixed = by_slot(dot_through(grad_branch, full_out).astype(LOW))
    grad_probs = jnp.einsum("shqe,shke->shqk", grad_mixed, values, preferred_element_type=FULL)
    inner = jnp.sum(probs_full * grad_probs, axis=-1, keepdims=True)
    grad_scores = jnp.where(allowed, probs_full * (grad_probs - inner), 0.0).astype(LOW)
    grad_queries = (
        jnp.einsum("shqk,shke->sqhe", grad_scores, keys, preferred_element_type=FULL) * scale
    ).reshape(total_rows, -1, HEAD_DIM)
    grad_keys = (
        jnp.einsum("shqk,shqe->skhe", grad_scores, queries, preferred_element_type=FULL) * scale
    ).reshape(total_rows, -1, HEAD_DIM)
    grad_values = jnp.einsum("shqk,shqe->skhe", probs, grad_mixed, preferred_element_type=FULL)
    grad_qkv = jnp.concatenate(
        [
            unrotate(grad_queries, cosine, sine).astype(LOW).reshape(total_rows, -1),
            unrotate(grad_keys, cosine, sine).astype(LOW).reshape(total_rows, -1),
            grad_values.astype(LOW).reshape(total_rows, -1),
        ],
        axis=1,
    )
    grad_qkv_rows = scattered(dot_rows(normed_all, grad_qkv))
    grad_normed = to_mixed_back(plane_reduce(dot_through(grad_qkv, full_qkv)), depth)
    from_first, grad_gain_attn = norm_back(inputs, gain_one, grad_normed)
    grad_input = grad_attended + from_first

    def to_columns(grads, count, shape):
        back = plane_exchange(grads.reshape(4, -1, grads.shape[1]), mine)
        each = back.shape[2] // count
        return [
            columns_from_parts(back[:, :, at * each : (at + 1) * each], shape).astype(FULL)
            for at in range(count)
        ]

    grad_w_gate, grad_w_up = to_columns(grad_gu_rows, 2, deep)
    grad_w_query, grad_w_key, grad_w_value = to_columns(grad_qkv_rows, 3, head_deep)
    grad_gains = scatter_small(jnp.stack([grad_gain_attn, grad_gain_mlp]))
    return (
        output,
        grad_input,
        grad_w_query,
        grad_w_key,
        grad_w_value,
        grad_w_out,
        grad_w_gate,
        grad_w_up,
        grad_w_down,
        grad_gains[0],
        grad_gains[1],
    )


def to_mixed_back(values, depth):
    apart = values.reshape(values.shape[0], depth, 2, 2, -1)
    return apart.transpose(0, 1, 3, 2, 4).reshape(values.shape)


def solution(mesh):
    shape = (mesh.shape["dp"] // 4, 2, 2, mesh.shape["seq"])
    grid = Mesh(mesh.devices.reshape(shape), AXES)
    split = P(AXES, None)
    part = P(AXES)
    return jax.shard_map(
        body,
        mesh=grid,
        in_specs=(split, split, P(), P()) + (split,) * 7 + (part, part),
        out_specs=(split,) * 9 + (part, part),
        check_vma=False,
    )
```

```python
import functools

import jax
import jax.experimental.pallas as pl
import jax.experimental.pallas.tpu as pltpu
import jax.numpy as jnp
from jax import lax
from jax.sharding import Mesh, PartitionSpec as P

HEAD_DIM = 64
PAIR = 2 * HEAD_DIM
norm_eps = 1e-05
rope_base = 130000.0
AXES = ("z", "x", "c", "y")
LOW = jnp.bfloat16
FULL = jnp.float32


def swap_x(value):
    return lax.ppermute(value, "x", [(0, 1), (1, 0)])


def swap_y(value):
    return lax.ppermute(value, "y", [(0, 1), (1, 0)])


def plane_gather_near(value):
    half = value.shape[0] // 2
    return swap_y(value[:half]), swap_x(value[half:])


def plane_gather_far(value, near):
    half = value.shape[0] // 2
    return (
        swap_x(jnp.concatenate([value[:half], near[0]], axis=0)),
        swap_y(jnp.concatenate([value[half:], near[1]], axis=0)),
    )


def plane_gathered(value, near, far):
    half = value.shape[0] // 2
    top, low = far
    return jnp.concatenate(
        [value, near[0], low[:half], top[:half], near[1], top[half:], low[half:]], axis=0
    )


def plane_blocks(value):
    count = value.shape[0] // 4
    return [value[at * count : (at + 1) * count] for at in range(4)]


def plane_reduce_near(value):
    _, by_y, by_x, by_d = plane_blocks(value)
    half = by_y.shape[0] // 2
    return (
        swap_x(jnp.concatenate([by_x[:half], by_d[:half]], axis=0)),
        swap_y(jnp.concatenate([by_y[half:], by_d[half:]], axis=0)),
    )


def plane_reduce_far(value, near):
    _, by_y, by_x, _ = plane_blocks(value)
    half = by_y.shape[0] // 2
    return (
        swap_y((by_y[:half].astype(FULL) + near[0][half:].astype(FULL)).astype(LOW)),
        swap_x((by_x[half:].astype(FULL) + near[1][half:].astype(FULL)).astype(LOW)),
    )


def plane_reduced(own, near, far):
    half = own.shape[0] // 2
    return own + jnp.concatenate(
        [
            near[0][:half].astype(FULL) + far[0].astype(FULL),
            near[1][:half].astype(FULL) + far[1].astype(FULL),
        ],
        axis=0,
    )


def columns_by_part(weight, deep):
    rows, columns = weight.shape
    if deep:
        parts = weight.reshape(rows, -1, 2, 2, 2, columns // (8 * deep))
        return parts.transpose(2, 4, 0, 1, 3, 5).reshape(4, rows, columns // 4)
    return weight.reshape(rows, 4, columns // 4).transpose(1, 0, 2)


def factor_of(values):
    return lax.rsqrt(jnp.mean(values * values, axis=-1, keepdims=True) + norm_eps)


def rope_tables(positions):
    halves = HEAD_DIM // 2
    frequency = rope_base ** (-(jnp.arange(halves).astype(FULL) * 2.0 / HEAD_DIM))
    angles = positions.astype(FULL)[:, None] * frequency[None, :]
    cosine = jnp.cos(angles)
    sine = jnp.sin(angles)
    return (
        jnp.concatenate([cosine] * 4, axis=1),
        jnp.concatenate([-sine, sine, -sine, sine], axis=1),
    )


def turned(values, low_half):
    lanes = values.shape[1]
    halves = HEAD_DIM // 2
    return jnp.where(
        low_half, pltpu.roll(values, lanes - halves, 1), pltpu.roll(values, halves, 1)
    )


def lane_masks(rows):
    lane = lax.broadcasted_iota(jnp.int32, (rows, PAIR), 1)
    return lane % HEAD_DIM < HEAD_DIM // 2, lane < HEAD_DIM


def diagonal_mask(first, length, rows):
    query = lax.broadcasted_iota(jnp.int32, (rows, rows), 0)
    key = lax.broadcasted_iota(jnp.int32, (rows, rows), 1)
    return (key <= query) & (key + first < length)


def attend_kernel(info, q_ref, k_ref, v_ref, c_ref, s_ref, mixed, lse, q_out, k_out, v_out):
    rows = q_ref.shape[0] // 2
    length = info[1 + pl.program_id(0)]
    scale = HEAD_DIM ** (-0.5)
    low_half, first_head = lane_masks(rows)
    place = [pl.multiple_of(jnp.where(info[0] == at, 0, rows), rows) for at in range(2)]
    queries, keys, values = [], [], []
    for at in range(2):
        span = pl.ds(place[at], rows)
        table = pl.ds(at * rows, rows)
        for source, target, kept in ((q_ref, q_out, queries), (k_ref, k_out, keys)):
            item = source[span, :]
            item = item * c_ref[table, :] + turned(item, low_half) * s_ref[table, :]
            item = item.astype(LOW)
            target[span, :] = item
            kept.append(item)
        item = v_ref[span, :].astype(LOW)
        v_out[span, :] = item
        values.append(item)
    for at in range(2):
        allowed = diagonal_mask(at * rows, length, rows)
        found, logs = [], []
        for head in range(2):
            only = first_head if head == 0 else jnp.logical_not(first_head)
            query = jnp.where(only, queries[at], jnp.zeros_like(queries[at]))
            scores = []
            for block in range(at + 1):
                score = dot_through(query, keys[block]) * scale
                scores.append(jnp.where(allowed, score, -1e30) if block == at else score)
            top = jnp.max(scores[0], axis=1, keepdims=True)
            for score in scores[1:]:
                top = jnp.maximum(top, jnp.max(score, axis=1, keepdims=True))
            weights = [jnp.exp(score - top) for score in scores]
            total = jnp.sum(weights[0], axis=1, keepdims=True)
            for weight in weights[1:]:
                total = total + jnp.sum(weight, axis=1, keepdims=True)
            share = 1.0 / total
            out = dot((weights[0] * share).astype(LOW), values[0])
            for block in range(1, at + 1):
                out = out + dot((weights[block] * share).astype(LOW), values[block])
            found.append(out)
            logs.append(top + jnp.log(total))
        span = pl.ds(place[at], rows)
        mixed[span, :] = jnp.where(first_head, found[0], found[1]).astype(LOW)
        lse[span, :] = jnp.where(first_head, logs[0], logs[1])


def attend_back_kernel(
    info, q_ref, k_ref, v_ref, g_ref, lse_ref, c_ref, s_ref, grad_q, grad_k, grad_v
):
    rows = q_ref.shape[0] // 2
    length = info[1 + pl.program_id(0)]
    scale = HEAD_DIM ** (-0.5)
    low_half, first_head = lane_masks(rows)
    place = [pl.multiple_of(jnp.where(info[0] == at, 0, rows), rows) for at in range(2)]
    spans = [pl.ds(start, rows) for start in place]
    keys = [k_ref[span, :] for span in spans]
    values = [v_ref[span, :] for span in spans]
    key_sums = [[None, None], [None, None]]
    value_sums = [[None, None], [None, None]]

    def unrotated(item, at):
        table = pl.ds(at * rows, rows)
        scaled = item * s_ref[table, :]
        return (item * c_ref[table, :] + turned(scaled, low_half)).astype(LOW)

    def added(old, new):
        return new if old is None else old + new

    for at in range(2):
        allowed = diagonal_mask(at * rows, length, rows)
        query_all, grad_all, logs = q_ref[spans[at], :], g_ref[spans[at], :], lse_ref[spans[at], :]
        found = []
        for head in range(2):
            only = first_head if head == 0 else jnp.logical_not(first_head)
            query = jnp.where(only, query_all, jnp.zeros_like(query_all))
            grad = jnp.where(only, grad_all, jnp.zeros_like(grad_all))
            log = logs[:, head * HEAD_DIM : head * HEAD_DIM + 1]
            probs, grads = [], []
            inner = jnp.zeros((rows, 1), FULL)
            for block in range(at + 1):
                prob = jnp.exp(dot_through(query, keys[block]) * scale - log)
                if block == at:
                    prob = jnp.where(allowed, prob, 0.0)
                grad_prob = dot_through(grad, values[block])
                inner = inner + jnp.sum(prob * grad_prob, axis=1, keepdims=True)
                probs.append(prob)
                grads.append(grad_prob)
            out = None
            for block in range(at + 1):
                grad_score = (probs[block] * (grads[block] - inner)).astype(LOW)
                out = added(out, dot(grad_score, keys[block]))
                key_sums[block][head] = added(key_sums[block][head], dot_rows(grad_score, query_all))
                value_sums[block][head] = added(
                    value_sums[block][head], dot_rows(probs[block].astype(LOW), grad_all)
                )
            found.append(out)
        grad_q[spans[at], :] = unrotated(jnp.where(first_head, found[0], found[1]) * scale, at)
    for at in range(2):
        both = jnp.where(first_head, key_sums[at][0], key_sums[at][1]) * scale
        grad_k[spans[at], :] = unrotated(both, at)
        both = jnp.where(first_head, value_sums[at][0], value_sums[at][1])
        grad_v[spans[at], :] = both.astype(LOW)


def attend(info, qkv, cosine, sine):
    total, width = qkv.shape[0], qkv.shape[1] // 3
    slot_rows, pairs = total // 2, width // PAIR
    block = (slot_rows, PAIR)

    def part(at):
        return pl.BlockSpec(block, lambda slot, pair, info: (slot, pair + at * pairs))

    table = pl.BlockSpec(block, lambda slot, pair, info: (0, 0))
    low = jax.ShapeDtypeStruct((total, width), LOW)
    return pl.pallas_call(
        attend_kernel,
        grid_spec=pltpu.PrefetchScalarGridSpec(
            num_scalar_prefetch=1,
            grid=(2, pairs),
            in_specs=[part(0), part(1), part(2), table, table],
            out_specs=[part(0)] * 5,
        ),
        out_shape=[low, jax.ShapeDtypeStruct((total, width), FULL), low, low, low],
        compiler_params=pltpu.CompilerParams(vmem_limit_bytes=16 * 1024 * 1024),
        cost_estimate=pl.CostEstimate(
            flops=16 * total * slot_rows * width,
            bytes_accessed=total * width * 24,
            transcendentals=total * slot_rows * width // HEAD_DIM,
        ),
    )(info, qkv, qkv, qkv, cosine, sine)


def attend_back(info, queries, keys, values, grads, lse, cosine, sine):
    total, width = queries.shape
    slot_rows, pairs = total // 2, width // PAIR
    block = (slot_rows, PAIR)
    part = pl.BlockSpec(block, lambda slot, pair, info: (slot, pair))
    table = pl.BlockSpec(block, lambda slot, pair, info: (0, 0))
    low = jax.ShapeDtypeStruct((total, width), LOW)
    return pl.pallas_call(
        attend_back_kernel,
        grid_spec=pltpu.PrefetchScalarGridSpec(
            num_scalar_prefetch=1,
            grid=(2, pairs),
            in_specs=[part] * 5 + [table, table],
            out_specs=[part] * 3,
        ),
        out_shape=[low, low, low],
        compiler_params=pltpu.CompilerParams(vmem_limit_bytes=16 * 1024 * 1024),
        cost_estimate=pl.CostEstimate(
            flops=40 * total * slot_rows * width,
            bytes_accessed=total * width * 18,
            transcendentals=total * slot_rows * width // HEAD_DIM,
        ),
    )(info, queries, keys, values, grads, lse, cosine, sine)


def dot(left, right):
    return jnp.dot(left, right, preferred_element_type=FULL)


def dot_rows(left, right):
    return lax.dot_general(left, right, (((0,), (0,)), ((), ())), preferred_element_type=FULL)


def dot_through(left, right):
    return lax.dot_general(left, right, (((1,), (1,)), ((), ())), preferred_element_type=FULL)


AXIS_BLOCK = {"y": 1, "x": 2}
PIECES = 4
FIRST, SECOND = ("x", "y"), ("y", "x")


def peer(*axes):
    return {axis: 1 - lax.axis_index(axis) for axis in axes}


def paired(axis, step):
    index = lax.axis_index(axis)
    return {axis: index + step * (1 - 2 * ((index // step) % 2))}


def beside(step):
    count = lax.axis_size("z")
    return {"z": (lax.axis_index("z") + step + count) % count}


def signal(barrier, device):
    pl.semaphore_signal(barrier, inc=1, device_id=device, device_id_type=pl.DeviceIdType.MESH)


def greet(devices, line=False):
    barrier = pltpu.get_barrier_semaphore()
    count = len(devices)
    for device in devices:
        signal(barrier, device)
    if line:
        index, last = lax.axis_index("z"), lax.axis_size("z") - 1
        for step, there in ((1, index < last), (-1, index > 0)):

            @pl.when(there)
            def _():
                signal(barrier, beside(step))

            count = count + there.astype(jnp.int32)
    pl.semaphore_wait(barrier, count)


class PlaneSum:
    def __init__(self, low, own, first_in, second_out, second_in, send, recv, spread=None):
        self.low, self.own, self.spread = low, own, spread
        self.first_in, self.second_out, self.second_in = first_in, second_out, second_in
        self.send, self.recv = send, recv
        self.rows = own.shape[0]
        self.step = self.rows // (2 * PIECES)
        self.pieces = [(half, at) for at in range(PIECES) for half in range(2)]

    def span(self, block, half, at):
        return pl.ds(block * self.rows + (half * PIECES + at) * self.step, self.step)

    def copy(self, kind, half, at, source, target, axis):
        return pltpu.make_async_remote_copy(
            src_ref=source,
            dst_ref=target,
            send_sem=self.send.at[kind, half, at],
            recv_sem=self.recv.at[kind, half, at],
            device_id=peer(axis),
            device_id_type=pl.DeviceIdType.MESH,
        )

    def first(self, kind, half, at):
        block = (AXIS_BLOCK[FIRST[half]], 3)[kind]
        return self.copy(
            kind,
            half,
            at,
            self.low.at[self.span(block, half, at)],
            self.first_in.at[half, at, kind],
            FIRST[half],
        )

    def second(self, half, at):
        return self.copy(
            2, half, at, self.second_out.at[half, at], self.second_in.at[half, at], SECOND[half]
        )

    def spreading(self, axis, half, at):
        return self.copy(
            2 + AXIS_BLOCK[axis],
            half,
            at,
            self.spread.at[self.span(0, half, at)],
            self.spread.at[self.span(AXIS_BLOCK[axis], half, at)],
            axis,
        )

    def forwarding(self, half, at):
        block = AXIS_BLOCK[SECOND[half]]
        return self.copy(
            5,
            half,
            at,
            self.spread.at[self.span(block, half, at)],
            self.spread.at[self.span(3, half, at)],
            FIRST[half],
        )

    def start(self):
        for half, at in self.pieces:
            self.first(0, half, at).start()
            self.first(1, half, at).start()

    def middle(self, half, at):
        self.first(0, half, at).wait_recv()
        self.first(1, half, at).wait_recv()
        block = AXIS_BLOCK[SECOND[half]]
        total = self.low[self.span(block, half, at), :].astype(FULL)
        total = total + self.first_in[half, at, 1].astype(FULL)
        self.second_out[half, at] = total.astype(LOW)
        self.second(half, at).start()

    def total(self, half, at):
        self.second(half, at).wait_recv()
        total = self.own[self.span(0, half, at), :] + self.first_in[half, at, 0].astype(FULL)
        return total + self.second_in[half, at].astype(FULL)

    def give(self, half, at, rows):
        self.spread[self.span(0, half, at), :] = rows
        self.spreading("x", half, at).start()
        self.spreading("y", half, at).start()

    def forward(self, half, at):
        self.spreading(SECOND[half], half, at).wait_recv()
        self.forwarding(half, at).start()

    def finish(self):
        for half, at in self.pieces:
            self.first(0, half, at).wait_send()
            self.first(1, half, at).wait_send()
            self.second(half, at).wait_send()
            if self.spread is not None:
                self.close_spread(half, at)

    def close_spread(self, half, at):
        self.spreading("x", half, at).wait_send()
        self.spreading("y", half, at).wait_send()
        self.spreading(FIRST[half], half, at).wait_recv()
        self.forwarding(half, at).wait()

    def run(self, each):
        count = len(self.pieces)
        self.start()
        for turn in range(count + 3):
            if turn < count:
                self.middle(*self.pieces[turn])
            if 1 <= turn <= count:
                half, at = self.pieces[turn - 1]
                self.give(half, at, each(self.span(0, half, at), self.total(half, at)))
            if turn >= 3:
                self.forward(*self.pieces[turn - 3])
        self.finish()


def forward_kernel(low, own, tokens, gain, attended, spread, first_in, out, second_in, send, recv):
    greet([peer("x"), peer("y")])
    plane = PlaneSum(low, own, first_in, out, second_in, send, recv, spread)

    def each(span, total):
        values = tokens[span, :].astype(FULL) + total
        attended[span, :] = values
        return mix((values * factor_of(values) * gain[...]).astype(LOW), lax.axis_size("z"))

    plane.run(each)


def norm_back(values, gain, grads):
    factor = factor_of(values)
    weighted = grads * gain
    inner = jnp.mean(weighted * values, axis=-1, keepdims=True)
    grad_gain = jnp.sum(grads * values * factor, axis=0, keepdims=True)
    return factor * weighted - values * (factor * factor * factor) * inner, grad_gain


def backward_kernel(
    low, own, attended, gain, grad_out, grad_attended, grad_gain, spread, first_in, out, second_in,
    send, recv
):
    greet([peer("x"), peer("y")])
    plane = PlaneSum(low, own, first_in, out, second_in, send, recv, spread)
    grad_gain[...] = jnp.zeros_like(grad_gain)

    def each(span, total):
        grads, for_gain = norm_back(attended[span, :], gain[...], mix(total, lax.axis_size("z")))
        grads = grads + grad_out[span, :]
        grad_attended[span, :] = grads
        grad_gain[...] += for_gain
        return grads.astype(LOW)

    plane.run(each)


def mixed_order(depth):
    return [at + step for at in range(0, 4 * depth, 4) for step in (0, 2, 1, 3)]


def blocks_align(width, depth):
    return (width // (4 * depth)) % 128 == 0


def mix(values, depth):
    if not blocks_align(values.shape[1], depth):
        return values
    block = values.shape[1] // (4 * depth)
    return jnp.concatenate(
        [values[:, at * block : (at + 1) * block] for at in mixed_order(depth)], axis=1
    )


class LineSum:
    def __init__(self, parts, sums, line_in, last_in, sems):
        self.parts, self.sums, self.line_in, self.last_in = parts, sums, line_in, last_in
        self.core_send, self.core_recv, self.send, self.right_recv, self.left_recv = sems
        self.depth = parts.shape[0]

    def core(self, at):
        return pltpu.make_async_remote_copy(
            src_ref=self.parts.at[at, 1 - lax.axis_index("c")],
            dst_ref=self.sums.at[at],
            send_sem=self.core_send.at[at],
            recv_sem=self.core_recv.at[at],
            device_id=peer("c"),
            device_id_type=pl.DeviceIdType.MESH,
        )

    def line(self, at, step, last=False):
        sems = self.right_recv if step == 1 else self.left_recv
        return pltpu.make_async_remote_copy(
            src_ref=self.sums.at[at],
            dst_ref=self.last_in if last else self.line_in.at[at],
            send_sem=self.send.at[at],
            recv_sem=sems.at[at],
            device_id=beside(step),
            device_id_type=pl.DeviceIdType.MESH,
        )

    def start(self):
        ends_first = sorted(range(self.depth), key=lambda at: min(at, self.depth - 1 - at))
        for at in ends_first:
            self.core(at).start()

    def both_cores(self, at):
        return self.parts[at, lax.axis_index("c")].astype(FULL) + self.sums[at].astype(FULL)

    def pass_on(self, at, step, first):
        self.core(at).wait_recv()
        total = self.both_cores(at)
        if not first:
            self.line(at, step).wait_recv()
            total = total + self.line_in[at].astype(FULL)
        self.sums[at] = total.astype(LOW)
        if step == 1:
            self.line(at, 1).start()
            return
        ends = at == lax.axis_index("z") - 1

        @pl.when(ends)
        def _():
            self.line(at, -1, True).start()

        @pl.when(jnp.logical_not(ends))
        def _():
            self.line(at, -1).start()

    def from_ends(self):
        index, last = lax.axis_index("z"), self.depth - 1
        for number in range(last):

            @pl.when(index == 0)
            def _():
                self.pass_on(last - number, 1, True)

            @pl.when(index == last)
            def _():
                self.pass_on(number, -1, True)

    def turn(self, time):
        index, last = lax.axis_index("z"), self.depth - 1

        @pl.when((index > 0) & (index <= time))
        def _():
            self.pass_on(index + last - time, 1, False)

        @pl.when((index < last) & (last - index <= time))
        def _():
            self.pass_on(time - (last - index), -1, False)

    def finish(self, total):
        index, last = lax.axis_index("z"), self.depth - 1
        self.core(index).wait_recv()
        total[...] = self.both_cores(index)

        @pl.when(index > 0)
        def _():
            self.line(index, 1).wait_recv()
            total[...] += self.line_in[index].astype(FULL)

        @pl.when(index < last)
        def _():
            self.line(index, -1, True).wait_recv()
            total[...] += self.last_in[...].astype(FULL)

    def close(self):
        index = lax.axis_index("z")
        for at in range(self.depth):
            self.core(at).wait_send()

            @pl.when(index < at)
            def _():
                self.line(at, 1).wait_send()

            @pl.when(index > at)
            def _():
                self.line(at, -1).wait_send()


def line_scratch(shape):
    depth, _, rows, columns = shape
    sems = [pltpu.SemaphoreType.DMA((depth,))] * 5
    return [pltpu.VMEM((depth, rows, columns), LOW)] * 2 + [pltpu.VMEM((rows, columns), LOW)] + sems


def last_kernel(deep, with_out, *refs):
    refs = list(refs)

    def take(count):
        taken, refs[:count] = refs[:count], []
        return taken

    low, own, tokens, gain, grad_attended, grad_gain_mlp, gu_rows, qkv_parts = take(8)
    out_parts = take(1)[0] if with_out else None
    grad_input, gains, grad_gate, grad_up, grad_query, grad_key, grad_value = take(7)
    grad_out = take(1)[0] if with_out else None
    plane_refs = take(5)
    qkv_refs, (qkv_total,) = take(8), take(1)
    if with_out:
        out_refs, (out_total,) = take(8), take(1)
    sent, back, gu_back, back_send, back_recv, gain_in, gain_out, gain_send, gain_recv = take(9)

    depth = qkv_parts.shape[0]
    steps = [("c", 1), ("x", 1), ("y", 1)]
    step = 1
    while step < depth:
        steps.append(("z", step))
        step *= 2
    far = [paired(axis, step) for axis, step in steps if step > 1]
    greet([peer("c"), peer("x"), peer("y"), peer("x", "y")] + far, line=True)

    plane = PlaneSum(low, own, *plane_refs)
    lines = [LineSum(qkv_parts, *qkv_refs[:3], qkv_refs[3:])]
    if with_out:
        lines.append(LineSum(out_parts, *out_refs[:3], out_refs[3:]))
    mine = lax.axis_index("x") * 2 + lax.axis_index("y")
    members = [("y",), ("x",), ("x", "y")]

    def exchange(kind, at):
        there = peer(*members[at])
        theirs = there.get("x", lax.axis_index("x")) * 2 + there.get("y", lax.axis_index("y"))
        source, target = ((sent, back), (gu_rows, gu_back))[kind]
        return pltpu.make_async_remote_copy(
            src_ref=source.at[theirs],
            dst_ref=target.at[mine],
            send_sem=back_send.at[kind, at],
            recv_sem=back_recv.at[kind, at],
            device_id=there,
            device_id_type=pl.DeviceIdType.MESH,
        )

    def spread_columns(target, source, offset, width, in_blocks):
        for part in range(4):
            columns = source[part, :, offset : offset + width].astype(FULL)
            if not in_blocks:
                target[:, part * width : (part + 1) * width] = columns
                continue
            each = width // (2 * depth)
            for at in range(2 * depth):
                place = ((at // 2 * 2 + part // 2) * 2 + at % 2) * 2 + part % 2
                target[:, place * each : (place + 1) * each] = columns[:, at * each : (at + 1) * each]

    for line in lines:
        line.start()
    plane.start()
    for line in lines:
        line.from_ends()
    gu_back[mine] = gu_rows[mine]

    grad_gain = jnp.zeros((1, own.shape[1]), FULL)
    todo = [("middle", 0)]
    for at in range(1, len(plane.pieces)):
        todo += [("middle", at), ("total", at - 1)]
    todo.append(("total", len(plane.pieces) - 1))
    share = -(-len(todo) // max(1, depth - 1))
    for number in range(depth - 1):
        if number:
            lines[0].turn(number)
        if number == (depth - 1) // 2:
            for at in range(3):
                exchange(1, at).start()
        for kind, at in todo[number * share : (number + 1) * share]:
            half, piece = plane.pieces[at]
            if kind == "middle":
                plane.middle(half, piece)
                continue
            span = plane.span(0, half, piece)
            grads, for_gain = norm_back(
                tokens[span, :].astype(FULL), gain[...], mix(plane.total(half, piece), depth)
            )
            grad_input[span, :] = grads + grad_attended[span, :]
            grad_gain = grad_gain + for_gain

    gain_out[0, 0:1, :] = grad_gain
    gain_out[0, 1:2, :] = grad_gain_mlp[...]

    def swap(at):
        axis, step = steps[at]
        return pltpu.make_async_remote_copy(
            src_ref=gain_out.at[at],
            dst_ref=gain_in.at[at],
            send_sem=gain_send.at[at],
            recv_sem=gain_recv.at[at],
            device_id=paired(axis, step),
            device_id_type=pl.DeviceIdType.MESH,
        )

    def swap_on(at):
        swap(at).wait_recv()
        total = gain_out[at] + gain_in[at]
        if at + 1 < len(steps):
            gain_out[at + 1] = total
            swap(at + 1).start()
        else:
            gains[...] = total

    swap(0).start()

    lines[0].finish(qkv_total)
    rows = qkv_parts.shape[2] // 4
    for at in range(4):
        sent[at] = qkv_total[at * rows : (at + 1) * rows, :].astype(LOW)
    for at in range(3):
        exchange(0, at).start()
    back[mine] = sent[mine]
    if with_out:
        for number in range(1, depth - 1):
            lines[1].turn(number)
    swap_on(0)
    for at in range(3):
        exchange(1, at).wait_recv()
    width = gu_back.shape[2] // 2
    spread_columns(grad_gate, gu_back, 0, width, True)
    swap_on(1)
    spread_columns(grad_up, gu_back, width, width, True)
    for at in range(2, len(steps)):
        swap_on(at)
    for at in range(3):
        exchange(0, at).wait_recv()
    width = back.shape[2] // 3
    for number, grad in enumerate((grad_query, grad_key, grad_value)):
        spread_columns(grad, back, number * width, width, deep)
    if with_out:
        lines[1].finish(out_total)
        grad_out[...] = out_total[...]

    for at in range(3):
        exchange(0, at).wait_send()
        exchange(1, at).wait_send()
    for at in range(len(steps)):
        swap(at).wait_send()
    plane.finish()
    for line in lines:
        line.close()


def last_call(deep, depth, rows, width, plane_operands, gu_rows, qkv_parts, out_parts):
    whole = pl.BlockSpec(memory_space=pltpu.VMEM)
    with_out = out_parts is not None
    operands = list(plane_operands) + [gu_rows, qkv_parts] + ([out_parts] if with_out else [])
    part_rows, part_width = qkv_parts.shape[2] // 4, qkv_parts.shape[3]
    outs = [like((rows, width), FULL), like((2, width), FULL)]
    outs += [like((part_rows, 2 * gu_rows.shape[2]), FULL)] * 2
    outs += [like((part_rows, 4 * part_width // 3), FULL)] * 3
    scratch = plane_scratch(rows, width) + line_scratch(qkv_parts.shape)
    scratch.append(pltpu.VMEM(qkv_parts.shape[2:], FULL))
    if with_out:
        outs.append(like(out_parts.shape[2:], FULL))
        scratch += line_scratch(out_parts.shape)
        scratch.append(pltpu.VMEM(out_parts.shape[2:], FULL))
    swaps = 3 + (depth - 1).bit_length()
    scratch += [
        pltpu.VMEM((4, part_rows, part_width), LOW),
        pltpu.VMEM((4, part_rows, part_width), LOW),
        pltpu.VMEM(gu_rows.shape, LOW),
        pltpu.SemaphoreType.DMA((2, 3)),
        pltpu.SemaphoreType.DMA((2, 3)),
        pltpu.VMEM((swaps, 2, width), FULL),
        pltpu.VMEM((swaps, 2, width), FULL),
        pltpu.SemaphoreType.DMA((swaps,)),
        pltpu.SemaphoreType.DMA((swaps,)),
    ]
    return pl.pallas_call(
        functools.partial(last_kernel, deep, with_out),
        out_shape=outs,
        in_specs=[whole] * len(operands),
        out_specs=[whole] * len(outs),
        scratch_shapes=scratch,
        compiler_params=pltpu.CompilerParams(
            collective_id=3, has_side_effects=True, vmem_limit_bytes=50 * 1024 * 1024
        ),
        cost_estimate=pl.CostEstimate(
            flops=rows * width * 100, bytes_accessed=rows * width * 400, transcendentals=0
        ),
    )(*operands)


class LineGather:
    def __init__(self, full, sems):
        self.full = full
        self.right_send, self.right_recv, self.left_send, self.left_recv = sems[:4]
        self.core_send, self.core_recv = sems[4:]
        self.depth = full.shape[0]

    def copy(self, at, send, recv, device):
        place = self.full.at[at, lax.axis_index("c")]
        return pltpu.make_async_remote_copy(
            src_ref=place,
            dst_ref=place,
            send_sem=send.at[at],
            recv_sem=recv.at[at],
            device_id=device,
            device_id_type=pl.DeviceIdType.MESH,
        )

    def right(self, at):
        return self.copy(at, self.right_send, self.right_recv, beside(1))

    def left(self, at):
        return self.copy(at, self.left_send, self.left_recv, beside(-1))

    def core(self, at):
        return self.copy(at, self.core_send, self.core_recv, peer("c"))

    def pass_on(self, number):
        index, last = lax.axis_index("z"), self.depth - 1
        for step, move in ((1, self.right), (-1, self.left)):
            at = index - number * step
            inside = (at >= 0) & (at <= last)

            @pl.when(inside)
            def _():
                if number:
                    move(at).wait_recv()

                @pl.when((index < last) if step == 1 else (index > 0))
                def _():
                    move(at).start()

                if number or step == 1:
                    self.core(at).start()

    def close(self):
        index, last = lax.axis_index("z"), self.depth - 1
        for at in range(self.depth):
            self.core(at).wait()

            @pl.when((index < last) & (at <= index))
            def _():
                self.right(at).wait_send()

            @pl.when((index > 0) & (at >= index))
            def _():
                self.left(at).wait_send()


def first_kernel(with_out, *refs):
    refs = list(refs)

    def take(count):
        taken, refs[:count] = refs[:count], []
        return taken

    qkv_parts, gu_parts, tokens, gain_parts = take(4)
    w_out = take(1)[0] if with_out else None
    full_qkv, gu_rows, spread, gains = take(4)
    full_out = take(1)[0] if with_out else None
    spread_send, spread_recv, gain_all, gain_send, gain_recv = take(5)
    swap_send, swap_recv, local = take(3)
    lines = [LineGather(full_qkv, take(6))]
    if with_out:
        lines.insert(0, LineGather(full_out, take(6)))

    depth = full_qkv.shape[0]
    at_z, at_x, at_c, at_y = (lax.axis_index(axis) for axis in AXES)
    mine = at_x * 2 + at_y
    index = ((at_z * 2 + at_x) * 2 + at_c) * 2 + at_y
    steps = [("y", 1), ("c", 1), ("x", 1)]
    step = 1
    while step < depth:
        steps.append(("z", step))
        step *= 2
    far = [paired(axis, step) for axis, step in steps if step > 1]
    greet([peer("c"), peer("x"), peer("y"), peer("x", "y")] + far, line=True)

    members = [("y",), ("x",), ("x", "y")]
    part_rows = qkv_parts.shape[1]

    def exchange(kind, at):
        there = peer(*members[at])
        theirs = there.get("x", at_x) * 2 + there.get("y", at_y)
        source, target = (
            (qkv_parts, full_qkv.at[at_z, at_c, pl.ds(mine * part_rows, part_rows)]),
            (gu_parts, gu_rows.at[mine]),
        )[kind]
        return pltpu.make_async_remote_copy(
            src_ref=source.at[theirs],
            dst_ref=target,
            send_sem=swap_send.at[kind, at],
            recv_sem=swap_recv.at[kind, at],
            device_id=there,
            device_id_type=pl.DeviceIdType.MESH,
        )

    own_qkv = pltpu.make_async_copy(
        qkv_parts.at[mine],
        full_qkv.at[at_z, at_c, pl.ds(mine * part_rows, part_rows)],
        local.at[0],
    )
    own_gu = pltpu.make_async_copy(gu_parts.at[mine], gu_rows.at[mine], local.at[1])
    for at in (2, 0, 1):
        exchange(0, at).start()
    own_qkv.start()
    if with_out:
        own_out = pltpu.make_async_copy(w_out, full_out.at[at_z, at_c], local.at[2])
        own_out.start()
    own_gu.start()

    def swap(at):
        axis, step = steps[at]
        count = 2**at
        place = gain_all.at[pl.ds((index // count) * count, count)]
        return pltpu.make_async_remote_copy(
            src_ref=place,
            dst_ref=place,
            send_sem=gain_send.at[at],
            recv_sem=gain_recv.at[at],
            device_id=paired(axis, step),
            device_id_type=pl.DeviceIdType.MESH,
        )

    gain_all[index] = gain_parts[0]
    for at in range(len(steps)):
        swap(at).start()
        if at == 1 and with_out:
            own_out.wait()
            lines[0].pass_on(0)
        if at == 2:
            for other in range(3):
                exchange(0, other).wait_recv()
            own_qkv.wait()
            lines[-1].pass_on(0)
            for other in range(3):
                exchange(1, other).start()
        swap(at).wait_recv()
    each = gain_parts.shape[2]
    for at in range(8 * depth):
        gains[:, at * each : (at + 1) * each] = gain_all[at]

    plane = PlaneSum(None, tokens, None, None, None, spread_send, spread_recv, spread)
    gain = gains[0:1, :]
    for half, at in plane.pieces:
        values = tokens[plane.span(0, half, at), :].astype(FULL)
        plane.give(half, at, mix((values * factor_of(values) * gain).astype(LOW), depth))

    todo = list(plane.pieces)
    share = -(-len(todo) // max(1, depth - 1))
    for number in range(1, depth):
        for line in lines:
            line.pass_on(number)
        for half, at in todo[(number - 1) * share : number * share]:
            plane.forward(half, at)
    for half, at in plane.pieces:
        plane.close_spread(half, at)
    own_gu.wait()
    for at in range(3):
        exchange(0, at).wait_send()
        exchange(1, at).wait()
    for at in range(len(steps)):
        swap(at).wait_send()
    for line in lines:
        line.close()


def first_call(depth, qkv_parts, gu_parts, tokens, gain_parts, w_out):
    rows, width = tokens.shape
    whole = pl.BlockSpec(memory_space=pltpu.VMEM)
    there = pl.BlockSpec(memory_space=pl.ANY)
    operands = [qkv_parts, gu_parts, tokens, gain_parts]
    in_specs = [there, there, whole, whole]
    part_rows, part_width = qkv_parts.shape[1:]
    outs = [
        like((depth, 2, 4 * part_rows, part_width), LOW),
        like(gu_parts.shape, LOW),
        like((4 * rows, width), LOW),
        like((2, width), FULL),
    ]
    out_specs = [there, there, whole, whole]
    swaps = 3 + (depth - 1).bit_length()
    scratch = [
        pltpu.SemaphoreType.DMA((6, 2, PIECES)),
        pltpu.SemaphoreType.DMA((6, 2, PIECES)),
        pltpu.VMEM((8 * depth, 2, width // (8 * depth)), FULL),
        pltpu.SemaphoreType.DMA((swaps,)),
        pltpu.SemaphoreType.DMA((swaps,)),
        pltpu.SemaphoreType.DMA((2, 3)),
        pltpu.SemaphoreType.DMA((2, 3)),
        pltpu.SemaphoreType.DMA((3,)),
    ]
    scratch += [pltpu.SemaphoreType.DMA((depth,))] * 6
    if w_out is not None:
        operands.append(w_out)
        in_specs.append(there)
        outs.append(like((depth, 2) + w_out.shape, LOW))
        out_specs.append(there)
        scratch += [pltpu.SemaphoreType.DMA((depth,))] * 6
    return pl.pallas_call(
        functools.partial(first_kernel, w_out is not None),
        out_shape=outs,
        in_specs=in_specs,
        out_specs=out_specs,
        scratch_shapes=scratch,
        compiler_params=pltpu.CompilerParams(
            collective_id=4, has_side_effects=True, vmem_limit_bytes=16 * 1024 * 1024
        ),
        cost_estimate=pl.CostEstimate(
            flops=rows * width * 100, bytes_accessed=rows * width * 200, transcendentals=0
        ),
    )(*operands)


def plane_scratch(rows, width):
    step = rows // (2 * PIECES)
    return [
        pltpu.VMEM((2, PIECES, 2, step, width), LOW),
        pltpu.VMEM((2, PIECES, step, width), LOW),
        pltpu.VMEM((2, PIECES, step, width), LOW),
        pltpu.SemaphoreType.DMA((6, 2, PIECES)),
        pltpu.SemaphoreType.DMA((6, 2, PIECES)),
    ]


def plane_call(kernel, number, rows, width, outs, *operands):
    whole = pl.BlockSpec(memory_space=pltpu.VMEM)
    return pl.pallas_call(
        kernel,
        out_shape=outs,
        in_specs=[whole] * len(operands),
        out_specs=[whole] * len(outs),
        scratch_shapes=plane_scratch(rows, width),
        compiler_params=pltpu.CompilerParams(
            collective_id=number, has_side_effects=True, vmem_limit_bytes=32 * 1024 * 1024
        ),
        cost_estimate=pl.CostEstimate(
            flops=rows * width * 100, bytes_accessed=rows * width * 200, transcendentals=0
        ),
    )(*operands)


like = jax.ShapeDtypeStruct


def body(
    tokens,
    cotangent,
    seq_lengths,
    assignment,
    w_query,
    w_key,
    w_value,
    w_out,
    w_gate,
    w_up,
    w_down,
    gain_attn,
    gain_mlp,
):
    rows, width = tokens.shape
    depth = lax.axis_size("z")
    deep = depth
    at_z, at_x, at_c, at_y = (lax.axis_index(axis) for axis in AXES)
    mine = at_x * 2 + at_y
    whole_heads = w_out.shape[0] % HEAD_DIM == 0
    head_deep = depth if whole_heads else 0
    head_width = width // 4
    unit_width = w_gate.shape[1] // 4

    def in_order(weight):
        if blocks_align(width, depth):
            return weight
        apart = weight.reshape(depth, 2, 2, -1, weight.shape[1])
        return apart.transpose(0, 2, 1, 3, 4).reshape(weight.shape)

    slot_at = [(at_z * 2 + x) * 2 + at_c for x in (at_x, 1 - at_x)]
    slot_length = [seq_lengths[assignment[slot]] for slot in slot_at]
    row = jnp.arange(rows)
    valid_rows = (at_y * rows + row < slot_length[0]).astype(FULL)[:, None]

    qkv_parts = jnp.concatenate(
        [columns_by_part(weight, head_deep) for weight in (w_query, w_key, w_value)], axis=2
    )
    gu_parts = jnp.concatenate([columns_by_part(weight, deep) for weight in (w_gate, w_up)], axis=2)
    full_qkv, gu_rows, normed_all, gains, *rest = first_call(
        depth,
        qkv_parts,
        gu_parts,
        tokens,
        jnp.stack([gain_attn, gain_mlp])[None].astype(FULL),
        w_out if whole_heads else None,
    )
    full_qkv = in_order(full_qkv.reshape(width, -1))
    gain_one, gain_two = gains[0], gains[1]
    full_gu = lax.all_gather(
        gu_rows.reshape(-1, gu_rows.shape[2]), ("z", "c"), axis=0, tiled=True
    )
    full_gu = in_order(full_gu)
    if whole_heads:
        full_out = rest[0].reshape(-1, width)
    else:
        every = lax.all_gather(w_out, AXES, axis=0, tiled=True)
        full_out = lax.dynamic_slice_in_dim(every, mine * head_width, head_width, axis=0)
    w_down, normed_all = lax.optimization_barrier((w_down, normed_all))

    grad_out = cotangent.astype(FULL) * valid_rows
    grad_low = grad_out.astype(LOW)
    normed_all, grad_low = lax.optimization_barrier((normed_all, grad_low))
    near = plane_gather_near(grad_low)
    qkv = dot(normed_all, full_qkv)
    qkv, near = lax.optimization_barrier((qkv, near))
    far = plane_gather_far(grad_low, near)
    cosine, sine = rope_tables(jnp.arange(2 * rows))
    info = jnp.stack([at_y.astype(jnp.int32)] + slot_length)
    heads_out, lse, queries, keys, values = attend(info, qkv, cosine, sine)
    w_down, heads_out, far = lax.optimization_barrier((w_down, heads_out, far))
    grad_low_all = plane_gathered(grad_low, near, far)
    full_down = lax.all_gather(w_down, ("z", "c"), axis=0, tiled=True)
    branch = dot(heads_out, full_out)
    attended, normed2_all = plane_call(
        forward_kernel,
        1,
        rows,
        width,
        [like((rows, width), FULL), like((4 * rows, width), LOW)],
        branch.astype(LOW),
        branch[:rows],
        tokens,
        gain_two[None],
    )
    gate = dot(normed2_all, full_gu[:, :unit_width])
    upper = dot(normed2_all, full_gu[:, unit_width:])
    sigmoid = jax.nn.sigmoid(gate)
    silu = gate * sigmoid
    active = (silu * upper).astype(LOW)

    def scattered(grads):
        return lax.psum_scatter(grads, ("z", "c"), scatter_dimension=0, tiled=True)

    grad_down_part = dot_rows(active, grad_low_all).astype(LOW)
    grad_down_part, grad_low_all, active = lax.optimization_barrier(
        (grad_down_part, grad_low_all, active)
    )
    grad_w_down = scattered(grad_down_part).astype(FULL)
    last = dot(active, full_down)
    last_low, last_own = last.astype(LOW), last[:rows]
    last_low, grad_low_all = lax.optimization_barrier((last_low, grad_low_all))
    near = plane_reduce_near(last_low)
    grad_active = dot_through(grad_low_all, full_down)
    grad_gate = (grad_active * upper * sigmoid * (1.0 + gate * (1.0 - sigmoid))).astype(LOW)
    grad_upper = (grad_active * silu).astype(LOW)
    grad_gu = jnp.concatenate([grad_gate, grad_upper], axis=1)
    grad_gu, near = lax.optimization_barrier((grad_gu, near))
    far = plane_reduce_far(last_low, near)
    grad_gu_part = in_order(dot_rows(normed2_all, grad_gu).astype(LOW))
    grad_gu_part, grad_gu = lax.optimization_barrier((grad_gu_part, grad_gu))
    grad_gu_rows = scattered(grad_gu_part)
    back = dot_through(grad_gu, full_gu)
    back, far = lax.optimization_barrier((back, far))
    result = attended + plane_reduced(last_own, near, far)
    output = (result * valid_rows).astype(LOW)
    grad_attended, grad_gain_mlp, grad_branch = plane_call(
        backward_kernel,
        2,
        rows,
        width,
        [like((rows, width), FULL), like((1, width), FULL), like((4 * rows, width), LOW)],
        back.astype(LOW),
        back[:rows],
        attended,
        gain_two[None],
        grad_out,
    )
    grad_w_down, grad_branch = lax.optimization_barrier((grad_w_down, grad_branch))

    grad_w_out = dot_rows(heads_out, grad_branch)
    out_parts = None
    if whole_heads:
        out_parts = grad_w_out.astype(LOW).reshape(depth, 2, -1, width)
    else:
        spread = lax.dynamic_update_slice_in_dim(
            jnp.zeros((width, width), FULL), grad_w_out, mine * head_width, axis=0
        )
        grad_w_out = lax.psum_scatter(spread, AXES, scatter_dimension=0, tiled=True)
    grad_mixed = dot_through(grad_branch, full_out).astype(LOW)
    grad_qkv = jnp.concatenate(
        attend_back(info, queries, keys, values, grad_mixed, lse, cosine, sine), axis=1
    )
    grad_qkv_part = in_order(dot_rows(normed_all, grad_qkv).astype(LOW))
    back = dot_through(grad_qkv, full_qkv)
    grad_input, grad_gains, *last_weights = last_call(
        head_deep,
        depth,
        rows,
        width,
        [
            back.astype(LOW),
            back[:rows],
            tokens,
            gain_one[None],
            grad_attended,
            grad_gain_mlp,
        ],
        grad_gu_rows.reshape(4, -1, grad_gu_rows.shape[1]),
        grad_qkv_part.reshape(depth, 2, -1, grad_qkv_part.shape[1]),
        out_parts,
    )
    grad_w_gate, grad_w_up, grad_w_query, grad_w_key, grad_w_value = last_weights[:5]
    if whole_heads:
        grad_w_out = last_weights[5]
    index = ((at_z * 2 + at_x) * 2 + at_c) * 2 + at_y
    part = width // (8 * depth)
    grad_gains = lax.dynamic_slice_in_dim(grad_gains, index * part, part, axis=1)
    return (
        output,
        grad_input,
        grad_w_query,
        grad_w_key,
        grad_w_value,
        grad_w_out,
        grad_w_gate,
        grad_w_up,
        grad_w_down,
        grad_gains[0],
        grad_gains[1],
    )


def solution(mesh):
    shape = (mesh.shape["dp"] // 4, 2, 2, mesh.shape["seq"])
    grid = Mesh(mesh.devices.reshape(shape), AXES)
    split = P(AXES, None)
    part = P(AXES)
    return jax.shard_map(
        body,
        mesh=grid,
        in_specs=(split, split, P(), P()) + (split,) * 7 + (part, part),
        out_specs=(split,) * 9 + (part, part),
        check_vma=False,
    )
```

```python
import functools

import jax
import jax.experimental.pallas as pl
import jax.experimental.pallas.tpu as pltpu
import jax.numpy as jnp
from jax import lax
from jax.sharding import Mesh, PartitionSpec as P

HEAD_DIM = 64
PAIR = 2 * HEAD_DIM
norm_eps = 1e-05
rope_base = 130000.0
AXES = ("z", "x", "c", "y")
LOW = jnp.bfloat16
FULL = jnp.float32
like = jax.ShapeDtypeStruct
in_hbm = pltpu.HBM


def hbm(*values):
    return [pltpu.with_memory_space_constraint(value, pltpu.HBM) for value in values]


def swap_x(value):
    return lax.ppermute(value, "x", [(0, 1), (1, 0)])


def swap_y(value):
    return lax.ppermute(value, "y", [(0, 1), (1, 0)])


def swap_c(value):
    return lax.ppermute(value, "c", [(0, 1), (1, 0)])


def plane_gather_near(value):
    half = value.shape[0] // 2
    return swap_y(value[:half]), swap_x(value[half:])


def plane_gather_far(value, near):
    half = value.shape[0] // 2
    return (
        swap_x(jnp.concatenate([value[:half], near[0]], axis=0)),
        swap_y(jnp.concatenate([value[half:], near[1]], axis=0)),
    )


def plane_gathered(value, near, far):
    half = value.shape[0] // 2
    top, low = far
    return jnp.concatenate(
        [value, near[0], low[:half], top[:half], near[1], top[half:], low[half:]], axis=0
    )


def plane_blocks(value):
    count = value.shape[0] // 4
    return [value[at * count : (at + 1) * count] for at in range(4)]


def plane_reduce_near(value):
    _, by_y, by_x, by_d = plane_blocks(value)
    half = by_y.shape[0] // 2
    return (
        swap_x(jnp.concatenate([by_x[:half], by_d[:half]], axis=0)),
        swap_y(jnp.concatenate([by_y[half:], by_d[half:]], axis=0)),
    )


def plane_reduce_far(value, near):
    _, by_y, by_x, _ = plane_blocks(value)
    half = by_y.shape[0] // 2
    return (
        swap_y((by_y[:half].astype(FULL) + near[0][half:].astype(FULL)).astype(LOW)),
        swap_x((by_x[half:].astype(FULL) + near[1][half:].astype(FULL)).astype(LOW)),
    )


def plane_reduced(own, near, far):
    half = own.shape[0] // 2
    return own + jnp.concatenate(
        [
            near[0][:half].astype(FULL) + far[0].astype(FULL),
            near[1][:half].astype(FULL) + far[1].astype(FULL),
        ],
        axis=0,
    )


def part_place(depth, part, block):
    return ((block // 2 * 2 + part // 2) * 2 + block % 2) * 2 + part % 2


def part_columns(width, depth, in_blocks, part, start, count):
    if not in_blocks:
        return [(0, part * (width // 4) + start, count)]
    each = width // (8 * depth)
    length = min(each, count)
    return [
        (
            at,
            part_place(depth, part, (start + at) // each) * each + (start + at) % each,
            length,
        )
        for at in range(0, count, length)
    ]


def factor_of(values):
    return lax.rsqrt(jnp.mean(values * values, axis=-1, keepdims=True) + norm_eps)


def rope_tables(positions):
    halves = HEAD_DIM // 2
    frequency = rope_base ** (-(jnp.arange(halves).astype(FULL) * 2.0 / HEAD_DIM))
    angles = positions.astype(FULL)[:, None] * frequency[None, :]
    cosine = jnp.cos(angles)
    sine = jnp.sin(angles)
    return (
        jnp.concatenate([cosine] * 4, axis=1),
        jnp.concatenate([-sine, sine, -sine, sine], axis=1),
    )


def turned(values, low_half):
    lanes = values.shape[1]
    halves = HEAD_DIM // 2
    return jnp.where(
        low_half, pltpu.roll(values, lanes - halves, 1), pltpu.roll(values, halves, 1)
    )


def lane_masks(rows):
    lane = lax.broadcasted_iota(jnp.int32, (rows, PAIR), 1)
    return lane % HEAD_DIM < HEAD_DIM // 2, lane < HEAD_DIM


def diagonal_mask(first, length, rows):
    query = lax.broadcasted_iota(jnp.int32, (rows, rows), 0)
    key = lax.broadcasted_iota(jnp.int32, (rows, rows), 1)
    return (key <= query) & (key + first < length)


def attend_kernel(info, qkv_ref, c_ref, s_ref, mixed, lse, qkv_out):
    rows = qkv_ref.shape[0] // 2
    length = info[1 + pl.program_id(0)]
    scale = HEAD_DIM ** (-0.5)
    low_half, first_head = lane_masks(rows)
    place = [pl.multiple_of(jnp.where(info[0] == at, 0, rows), rows) for at in range(2)]
    queries, keys, values = [], [], []
    for at in range(2):
        span = pl.ds(place[at], rows)
        table = pl.ds(at * rows, rows)
        for number, kept in enumerate((queries, keys, values)):
            lanes = slice(number * PAIR, (number + 1) * PAIR)
            item = qkv_ref[span, lanes]
            if number < 2:
                item = item * c_ref[table, :] + turned(item, low_half) * s_ref[table, :]
            item = item.astype(LOW)
            qkv_out[span, lanes] = item
            kept.append(item)
    for at in range(2):
        allowed = diagonal_mask(at * rows, length, rows)
        found, logs = [], []
        for head in range(2):
            only = first_head if head == 0 else jnp.logical_not(first_head)
            query = jnp.where(only, queries[at], jnp.zeros_like(queries[at]))
            scores = []
            for block in range(at + 1):
                score = dot_through(query, keys[block]) * scale
                scores.append(jnp.where(allowed, score, -1e30) if block == at else score)
            top = jnp.max(scores[0], axis=1, keepdims=True)
            for score in scores[1:]:
                top = jnp.maximum(top, jnp.max(score, axis=1, keepdims=True))
            weights = [jnp.exp(score - top) for score in scores]
            total = jnp.sum(weights[0], axis=1, keepdims=True)
            for weight in weights[1:]:
                total = total + jnp.sum(weight, axis=1, keepdims=True)
            share = 1.0 / total
            out = dot((weights[0] * share).astype(LOW), values[0])
            for block in range(1, at + 1):
                out = out + dot((weights[block] * share).astype(LOW), values[block])
            found.append(out)
            logs.append(top + jnp.log(total))
        span = pl.ds(place[at], rows)
        mixed[span, :] = jnp.where(first_head, found[0], found[1]).astype(LOW)
        lse[span, :] = jnp.where(first_head, logs[0], logs[1])


def attend_back_kernel(info, qkv_ref, g_ref, lse_ref, c_ref, s_ref, grads_out):
    rows = qkv_ref.shape[0] // 2
    length = info[1 + pl.program_id(0)]
    scale = HEAD_DIM ** (-0.5)
    low_half, first_head = lane_masks(rows)
    place = [pl.multiple_of(jnp.where(info[0] == at, 0, rows), rows) for at in range(2)]
    spans = [pl.ds(start, rows) for start in place]
    keys = [qkv_ref[span, PAIR : 2 * PAIR] for span in spans]
    values = [qkv_ref[span, 2 * PAIR :] for span in spans]
    key_sums = [[None, None], [None, None]]
    value_sums = [[None, None], [None, None]]

    def unrotated(item, at):
        table = pl.ds(at * rows, rows)
        scaled = item * s_ref[table, :]
        return (item * c_ref[table, :] + turned(scaled, low_half)).astype(LOW)

    def added(old, new):
        return new if old is None else old + new

    for at in range(2):
        allowed = diagonal_mask(at * rows, length, rows)
        query_all, grad_all, logs = qkv_ref[spans[at], :PAIR], g_ref[spans[at], :], lse_ref[spans[at], :]
        found = []
        for head in range(2):
            only = first_head if head == 0 else jnp.logical_not(first_head)
            query = jnp.where(only, query_all, jnp.zeros_like(query_all))
            grad = jnp.where(only, grad_all, jnp.zeros_like(grad_all))
            log = logs[:, head * HEAD_DIM : head * HEAD_DIM + 1]
            probs, grads = [], []
            inner = jnp.zeros((rows, 1), FULL)
            for block in range(at + 1):
                prob = jnp.exp(dot_through(query, keys[block]) * scale - log)
                if block == at:
                    prob = jnp.where(allowed, prob, 0.0)
                grad_prob = dot_through(grad, values[block])
                inner = inner + jnp.sum(prob * grad_prob, axis=1, keepdims=True)
                probs.append(prob)
                grads.append(grad_prob)
            out = None
            for block in range(at + 1):
                grad_score = (probs[block] * (grads[block] - inner)).astype(LOW)
                out = added(out, dot(grad_score, keys[block]))
                key_sums[block][head] = added(key_sums[block][head], dot_rows(grad_score, query_all))
                value_sums[block][head] = added(
                    value_sums[block][head], dot_rows(probs[block].astype(LOW), grad_all)
                )
            found.append(out)
        grads_out[spans[at], :PAIR] = unrotated(jnp.where(first_head, found[0], found[1]) * scale, at)
    for at in range(2):
        both = jnp.where(first_head, key_sums[at][0], key_sums[at][1]) * scale
        grads_out[spans[at], PAIR : 2 * PAIR] = unrotated(both, at)
        both = jnp.where(first_head, value_sums[at][0], value_sums[at][1])
        grads_out[spans[at], 2 * PAIR :] = both.astype(LOW)


def attend(info, qkv, cosine, sine):
    total, width = qkv.shape[0], qkv.shape[1] // 3
    slot_rows, pairs = total // 2, width // PAIR
    part = pl.BlockSpec((slot_rows, PAIR), lambda slot, pair, info: (slot, pair))
    three = pl.BlockSpec((slot_rows, 3 * PAIR), lambda slot, pair, info: (slot, pair))
    table = pl.BlockSpec((slot_rows, PAIR), lambda slot, pair, info: (0, 0))
    return pl.pallas_call(
        attend_kernel,
        grid_spec=pltpu.PrefetchScalarGridSpec(
            num_scalar_prefetch=1,
            grid=(2, pairs),
            in_specs=[three, table, table],
            out_specs=[part, part, three],
        ),
        out_shape=[
            in_hbm((total, width), LOW),
            in_hbm((total, width), FULL),
            in_hbm((total, 3 * width), LOW),
        ],
        compiler_params=pltpu.CompilerParams(vmem_limit_bytes=16 * 1024 * 1024),
        cost_estimate=pl.CostEstimate(
            flops=16 * total * slot_rows * width,
            bytes_accessed=total * width * 24,
            transcendentals=total * slot_rows * width // HEAD_DIM,
        ),
    )(info, qkv, cosine, sine)


def attend_back(info, qkv, grads, lse, cosine, sine):
    total, width = grads.shape
    slot_rows, pairs = total // 2, width // PAIR
    part = pl.BlockSpec((slot_rows, PAIR), lambda slot, pair, info: (slot, pair))
    three = pl.BlockSpec((slot_rows, 3 * PAIR), lambda slot, pair, info: (slot, pair))
    table = pl.BlockSpec((slot_rows, PAIR), lambda slot, pair, info: (0, 0))
    return pl.pallas_call(
        attend_back_kernel,
        grid_spec=pltpu.PrefetchScalarGridSpec(
            num_scalar_prefetch=1,
            grid=(2, pairs),
            in_specs=[three, part, part, table, table],
            out_specs=three,
        ),
        out_shape=in_hbm((total, 3 * width), LOW),
        compiler_params=pltpu.CompilerParams(vmem_limit_bytes=16 * 1024 * 1024),
        cost_estimate=pl.CostEstimate(
            flops=40 * total * slot_rows * width,
            bytes_accessed=total * width * 18,
            transcendentals=total * slot_rows * width // HEAD_DIM,
        ),
    )(info, *hbm(qkv, grads, lse), cosine, sine)


def dot(left, right):
    return jnp.dot(left, right, preferred_element_type=FULL)


def dot_rows(left, right):
    return lax.dot_general(left, right, (((0,), (0,)), ((), ())), preferred_element_type=FULL)


def dot_through(left, right):
    return lax.dot_general(left, right, (((1,), (1,)), ((), ())), preferred_element_type=FULL)


UNIT_TILE = 256


def activate_kernel(normed, weight, both_ref, active_ref):
    both = dot(normed[...], weight[...])
    both_ref[...] = both
    gate, upper = both[:, :UNIT_TILE], both[:, UNIT_TILE:]
    active_ref[...] = (gate * jax.nn.sigmoid(gate) * upper).astype(LOW)


def activate(normed, weight):
    rows, width = normed.shape
    units = weight.shape[1] // 2
    return pl.pallas_call(
        activate_kernel,
        grid=(units // UNIT_TILE,),
        in_specs=[
            pl.BlockSpec((rows, width), lambda at: (0, 0)),
            pl.BlockSpec((width, 2 * UNIT_TILE), lambda at: (0, at)),
        ],
        out_specs=[
            pl.BlockSpec((rows, 2 * UNIT_TILE), lambda at: (0, at)),
            pl.BlockSpec((rows, UNIT_TILE), lambda at: (0, at)),
        ],
        out_shape=[in_hbm((rows, 2 * units), FULL), in_hbm((rows, units), LOW)],
        compiler_params=pltpu.CompilerParams(vmem_limit_bytes=40 * 1024 * 1024),
        cost_estimate=pl.CostEstimate(
            flops=4 * rows * units * width,
            bytes_accessed=rows * units * 10 + units * width * 4,
            transcendentals=rows * units,
        ),
    )(*hbm(normed, weight))


def activate_back_kernel(grad_low, weight, both_ref, out):
    grads = dot_through(grad_low[...], weight[...])
    gate, upper = both_ref[:, :UNIT_TILE], both_ref[:, UNIT_TILE:]
    sigmoid = jax.nn.sigmoid(gate)
    out[:, :UNIT_TILE] = (grads * upper * sigmoid * (1.0 + gate * (1.0 - sigmoid))).astype(LOW)
    out[:, UNIT_TILE:] = (grads * gate * sigmoid).astype(LOW)


def activate_back(grad_low, weight, both):
    rows, units = both.shape[0], both.shape[1] // 2
    width = grad_low.shape[1]
    part = pl.BlockSpec((rows, 2 * UNIT_TILE), lambda at: (0, at))
    return pl.pallas_call(
        activate_back_kernel,
        grid=(units // UNIT_TILE,),
        in_specs=[
            pl.BlockSpec((rows, width), lambda at: (0, 0)),
            pl.BlockSpec((UNIT_TILE, width), lambda at: (at, 0)),
            part,
        ],
        out_specs=part,
        out_shape=in_hbm((rows, 2 * units), LOW),
        compiler_params=pltpu.CompilerParams(vmem_limit_bytes=40 * 1024 * 1024),
        cost_estimate=pl.CostEstimate(
            flops=2 * rows * units * width,
            bytes_accessed=rows * units * 12 + units * width * 2,
            transcendentals=rows * units,
        ),
    )(*hbm(grad_low, weight, both))


def project_kernel(through, left, weight, low, own):
    groups, total, depth = left.shape
    if through:
        found = dot_through(left[0], weight[:, :depth])
        for group in range(1, groups):
            found = found + dot_through(
                left[group], weight[:, group * depth : (group + 1) * depth]
            )
    else:
        found = dot(left[0], weight[...])
    low[...] = found.astype(LOW)
    own[...] = found[: own.shape[0], :]


def project(left, weight, through):
    groups, total, depth = left.shape
    width = weight.shape[0] if through else weight.shape[1]
    tile = 256
    block = (tile, groups * depth) if through else (depth, tile)
    return pl.pallas_call(
        functools.partial(project_kernel, through),
        grid=(width // tile,),
        in_specs=[
            pl.BlockSpec((groups, total, depth), lambda at: (0, 0, 0)),
            pl.BlockSpec(block, (lambda at: (at, 0)) if through else (lambda at: (0, at))),
        ],
        out_specs=[
            pl.BlockSpec((total, tile), lambda at: (0, at)),
            pl.BlockSpec((total // 4, tile), lambda at: (0, at)),
        ],
        out_shape=[in_hbm((total, width), LOW), in_hbm((total // 4, width), FULL)],
        compiler_params=pltpu.CompilerParams(vmem_limit_bytes=40 * 1024 * 1024),
        cost_estimate=pl.CostEstimate(
            flops=2 * groups * total * depth * width,
            bytes_accessed=2 * groups * depth * (total + width) + 3 * total * width,
            transcendentals=0,
        ),
    )(*hbm(left, weight))


AXIS_BLOCK = {"y": 1, "x": 2}
PIECES = 4
FIRST, SECOND = ("x", "y"), ("y", "x")


def peer(*axes):
    return {axis: 1 - lax.axis_index(axis) for axis in axes}


def paired(axis, step):
    index = lax.axis_index(axis)
    return {axis: index + step * (1 - 2 * ((index // step) % 2))}


def beside(step):
    count = lax.axis_size("z")
    return {"z": (lax.axis_index("z") + step + count) % count}


def signal(barrier, device):
    pl.semaphore_signal(barrier, inc=1, device_id=device, device_id_type=pl.DeviceIdType.MESH)


def greet(devices, line=False):
    barrier = pltpu.get_barrier_semaphore()
    count = len(devices)
    for device in devices:
        signal(barrier, device)
    if line:
        index, last = lax.axis_index("z"), lax.axis_size("z") - 1
        for step, there in ((1, index < last), (-1, index > 0)):

            @pl.when(there)
            def _():
                signal(barrier, beside(step))

            count = count + there.astype(jnp.int32)
    pl.semaphore_wait(barrier, count)


class PlaneSum:
    def __init__(self, low, own, first_in, second_out, second_in, send, recv, spread=None):
        self.low, self.own, self.spread = low, own, spread
        self.first_in, self.second_out, self.second_in = first_in, second_out, second_in
        self.send, self.recv = send, recv
        self.rows = own.shape[0]
        self.step = self.rows // (2 * PIECES)
        self.pieces = [(half, at) for at in range(PIECES) for half in range(2)]

    def span(self, block, half, at):
        return pl.ds(block * self.rows + (half * PIECES + at) * self.step, self.step)

    def copy(self, kind, half, at, source, target, axis):
        return pltpu.make_async_remote_copy(
            src_ref=source,
            dst_ref=target,
            send_sem=self.send.at[kind, half, at],
            recv_sem=self.recv.at[kind, half, at],
            device_id=peer(axis),
            device_id_type=pl.DeviceIdType.MESH,
        )

    def first(self, kind, half, at):
        block = (AXIS_BLOCK[FIRST[half]], 3)[kind]
        return self.copy(
            kind,
            half,
            at,
            self.low.at[self.span(block, half, at)],
            self.first_in.at[half, at, kind],
            FIRST[half],
        )

    def second(self, half, at):
        return self.copy(
            2, half, at, self.second_out.at[half, at], self.second_in.at[half, at], SECOND[half]
        )

    def spreading(self, axis, half, at):
        return self.copy(
            2 + AXIS_BLOCK[axis],
            half,
            at,
            self.spread.at[self.span(0, half, at)],
            self.spread.at[self.span(AXIS_BLOCK[axis], half, at)],
            axis,
        )

    def forwarding(self, half, at):
        block = AXIS_BLOCK[SECOND[half]]
        return self.copy(
            5,
            half,
            at,
            self.spread.at[self.span(block, half, at)],
            self.spread.at[self.span(3, half, at)],
            FIRST[half],
        )

    def start(self):
        for half, at in self.pieces:
            self.first(0, half, at).start()
            self.first(1, half, at).start()

    def middle(self, half, at):
        self.first(0, half, at).wait_recv()
        self.first(1, half, at).wait_recv()
        block = AXIS_BLOCK[SECOND[half]]
        total = self.low[self.span(block, half, at), :].astype(FULL)
        total = total + self.first_in[half, at, 1].astype(FULL)
        self.second_out[half, at] = total.astype(LOW)
        self.second(half, at).start()

    def total(self, half, at):
        self.second(half, at).wait_recv()
        total = self.own[self.span(0, half, at), :] + self.first_in[half, at, 0].astype(FULL)
        return total + self.second_in[half, at].astype(FULL)

    def give(self, half, at, rows):
        self.spread[self.span(0, half, at), :] = rows
        self.spreading("x", half, at).start()
        self.spreading("y", half, at).start()

    def forward(self, half, at):
        self.spreading(SECOND[half], half, at).wait_recv()
        self.forwarding(half, at).start()

    def finish(self):
        for half, at in self.pieces:
            self.first(0, half, at).wait_send()
            self.first(1, half, at).wait_send()
            self.second(half, at).wait_send()
            if self.spread is not None:
                self.close_spread(half, at)

    def close_spread(self, half, at):
        self.spreading("x", half, at).wait_send()
        self.spreading("y", half, at).wait_send()
        self.spreading(FIRST[half], half, at).wait_recv()
        self.forwarding(half, at).wait()

    def run(self, each):
        count = len(self.pieces)
        self.start()
        for turn in range(count + 3):
            if turn < count:
                self.middle(*self.pieces[turn])
            if 1 <= turn <= count:
                half, at = self.pieces[turn - 1]
                self.give(half, at, each(self.span(0, half, at), self.total(half, at)))
            if turn >= 3:
                self.forward(*self.pieces[turn - 3])
        self.finish()


def forward_kernel(low, own, tokens, gain, attended, spread, first_in, out, second_in, send, recv):
    greet([peer("x"), peer("y")])
    plane = PlaneSum(low, own, first_in, out, second_in, send, recv, spread)

    def each(span, total):
        values = tokens[span, :].astype(FULL) + total
        attended[span, :] = values
        return mix((values * factor_of(values) * gain[...]).astype(LOW), lax.axis_size("z"))

    plane.run(each)


def norm_back(values, gain, grads):
    factor = factor_of(values)
    weighted = grads * gain
    inner = jnp.mean(weighted * values, axis=-1, keepdims=True)
    grad_gain = jnp.sum(grads * values * factor, axis=0, keepdims=True)
    return factor * weighted - values * (factor * factor * factor) * inner, grad_gain


def backward_kernel(
    low, own, attended, gain, grad_out, grad_attended, grad_gain, spread, first_in, out, second_in,
    send, recv
):
    greet([peer("x"), peer("y")])
    plane = PlaneSum(low, own, first_in, out, second_in, send, recv, spread)
    grad_gain[...] = jnp.zeros_like(grad_gain)

    def each(span, total):
        grads, for_gain = norm_back(
            attended[span, :], gain[...], mix(total, lax.axis_size("z"), True)
        )
        grads = grads + grad_out[span, :]
        grad_attended[span, :] = grads
        grad_gain[...] += for_gain
        return grads.astype(LOW)

    plane.run(each)


def blocks_align(width, depth):
    return (width // (4 * depth)) % 128 == 0


def mix(values, depth, back=False):
    if not blocks_align(values.shape[1], depth):
        return values
    block = values.shape[1] // (4 * depth)
    order = [(z * 2 + x) * 2 + c for c in range(2) for z in range(depth) for x in range(2)]
    if back:
        order = sorted(range(4 * depth), key=order.__getitem__)
    return jnp.concatenate([values[:, at * block : (at + 1) * block] for at in order], axis=1)


class LineSum:
    def __init__(self, core_first, parts, sums, line_in, last_in, sems):
        self.core_first, self.parts = core_first, parts
        self.sums, self.line_in, self.last_in = sums, line_in, last_in
        self.core_send, self.core_recv, self.send, self.right_recv, self.left_recv = sems
        self.depth = sums.shape[0]

    def place(self, at, core):
        return (core, at) if self.core_first else (at, core)

    def core(self, at):
        return pltpu.make_async_remote_copy(
            src_ref=self.parts.at[self.place(at, 1 - lax.axis_index("c"))],
            dst_ref=self.sums.at[at],
            send_sem=self.core_send.at[at],
            recv_sem=self.core_recv.at[at],
            device_id=peer("c"),
            device_id_type=pl.DeviceIdType.MESH,
        )

    def line(self, at, step, last=False):
        sems = self.right_recv if step == 1 else self.left_recv
        return pltpu.make_async_remote_copy(
            src_ref=self.sums.at[at],
            dst_ref=self.last_in if last else self.line_in.at[at],
            send_sem=self.send.at[at],
            recv_sem=sems.at[at],
            device_id=beside(step),
            device_id_type=pl.DeviceIdType.MESH,
        )

    def start(self):
        ends_first = sorted(range(self.depth), key=lambda at: min(at, self.depth - 1 - at))
        for at in ends_first:
            self.core(at).start()

    def both_cores(self, at):
        return (
            self.parts[self.place(at, lax.axis_index("c"))].astype(FULL) + self.sums[at].astype(FULL)
        )

    def pass_on(self, at, step, first):
        self.core(at).wait_recv()
        total = self.both_cores(at)
        if not first:
            self.line(at, step).wait_recv()
            total = total + self.line_in[at].astype(FULL)
        self.sums[at] = total.astype(LOW)
        if step == 1:
            self.line(at, 1).start()
            return
        ends = at == lax.axis_index("z") - 1

        @pl.when(ends)
        def _():
            self.line(at, -1, True).start()

        @pl.when(jnp.logical_not(ends))
        def _():
            self.line(at, -1).start()

    def from_ends(self):
        index, last = lax.axis_index("z"), self.depth - 1
        for number in range(last):

            @pl.when(index == 0)
            def _():
                self.pass_on(last - number, 1, True)

            @pl.when(index == last)
            def _():
                self.pass_on(number, -1, True)

    def turn(self, time):
        index, last = lax.axis_index("z"), self.depth - 1

        @pl.when((index > 0) & (index <= time))
        def _():
            self.pass_on(index + last - time, 1, False)

        @pl.when((index < last) & (last - index <= time))
        def _():
            self.pass_on(time - (last - index), -1, False)

    def finish(self, total):
        index, last = lax.axis_index("z"), self.depth - 1
        self.core(index).wait_recv()
        total[...] = self.both_cores(index)

        @pl.when(index > 0)
        def _():
            self.line(index, 1).wait_recv()
            total[...] += self.line_in[index].astype(FULL)

        @pl.when(index < last)
        def _():
            self.line(index, -1, True).wait_recv()
            total[...] += self.last_in[...].astype(FULL)

    def close(self):
        index = lax.axis_index("z")
        for at in range(self.depth):
            self.core(at).wait_send()

            @pl.when(index < at)
            def _():
                self.line(at, 1).wait_send()

            @pl.when(index > at)
            def _():
                self.line(at, -1).wait_send()


def line_scratch(depth, shape):
    rows, columns = shape[2:]
    sems = [pltpu.SemaphoreType.DMA((depth,))] * 5
    return [pltpu.VMEM((depth, rows, columns), LOW)] * 2 + [pltpu.VMEM((rows, columns), LOW)] + sems


def last_kernel(deep, with_out, *refs):
    refs = list(refs)

    def take(count):
        taken, refs[:count] = refs[:count], []
        return taken

    low, own, tokens, gain, grad_attended, grad_gain_mlp, gu_rows, qkv_parts = take(8)
    out_parts = take(1)[0] if with_out else None
    grad_input, gains, grad_gate, grad_up, grad_query, grad_key, grad_value = take(7)
    grad_out = take(1)[0] if with_out else None
    plane_refs = take(5)
    qkv_refs, (qkv_total,) = take(8), take(1)
    if with_out:
        out_refs, (out_total,) = take(8), take(1)
    sent, back, gu_back, back_send, back_recv, gain_in, gain_out, gain_send, gain_recv = take(9)

    depth = qkv_parts.shape[1]
    steps = [("c", 1), ("x", 1), ("y", 1)]
    step = 1
    while step < depth:
        steps.append(("z", step))
        step *= 2
    far = [paired(axis, step) for axis, step in steps if step > 1]
    greet([peer("c"), peer("x"), peer("y"), peer("x", "y")] + far, line=True)

    plane = PlaneSum(low, own, *plane_refs)
    lines = [LineSum(True, qkv_parts, *qkv_refs[:3], qkv_refs[3:])]
    if with_out:
        lines.append(LineSum(False, out_parts, *out_refs[:3], out_refs[3:]))
    mine = lax.axis_index("x") * 2 + lax.axis_index("y")
    members = [("y",), ("x",), ("x", "y")]

    def exchange(kind, at):
        there = peer(*members[at])
        theirs = there.get("x", lax.axis_index("x")) * 2 + there.get("y", lax.axis_index("y"))
        source, target = ((sent, back), (gu_rows, gu_back))[kind]
        return pltpu.make_async_remote_copy(
            src_ref=source.at[theirs],
            dst_ref=target.at[mine],
            send_sem=back_send.at[kind, at],
            recv_sem=back_recv.at[kind, at],
            device_id=there,
            device_id_type=pl.DeviceIdType.MESH,
        )

    def spread_parts(targets, source, tile, in_blocks):
        for part in range(4):
            for at in range(source.shape[2] // tile):
                target = targets[at % len(targets)]
                columns = source[part, :, at * tile : (at + 1) * tile].astype(FULL)
                runs = part_columns(
                    target.shape[1], depth, in_blocks, part, at // len(targets) * tile, tile
                )
                for own, place, length in runs:
                    target[:, place : place + length] = columns[:, own : own + length]

    for line in lines:
        line.start()
    plane.start()
    for line in lines:
        line.from_ends()
    gu_back[mine] = gu_rows[mine]

    grad_gain = jnp.zeros((1, own.shape[1]), FULL)
    todo = [("middle", 0)]
    for at in range(1, len(plane.pieces)):
        todo += [("middle", at), ("total", at - 1)]
    todo.append(("total", len(plane.pieces) - 1))
    share = -(-len(todo) // max(1, depth - 1))
    for number in range(depth - 1):
        if number:
            lines[0].turn(number)
        if number == (depth - 1) // 2:
            for at in range(3):
                exchange(1, at).start()
        for kind, at in todo[number * share : (number + 1) * share]:
            half, piece = plane.pieces[at]
            if kind == "middle":
                plane.middle(half, piece)
                continue
            span = plane.span(0, half, piece)
            grads, for_gain = norm_back(
                tokens[span, :].astype(FULL), gain[...], mix(plane.total(half, piece), depth, True)
            )
            grad_input[span, :] = grads + grad_attended[span, :]
            grad_gain = grad_gain + for_gain

    gain_out[0, 0:1, :] = grad_gain
    gain_out[0, 1:2, :] = grad_gain_mlp[...]

    def swap(at):
        axis, step = steps[at]
        return pltpu.make_async_remote_copy(
            src_ref=gain_out.at[at],
            dst_ref=gain_in.at[at],
            send_sem=gain_send.at[at],
            recv_sem=gain_recv.at[at],
            device_id=paired(axis, step),
            device_id_type=pl.DeviceIdType.MESH,
        )

    def swap_on(at):
        swap(at).wait_recv()
        total = gain_out[at] + gain_in[at]
        if at + 1 < len(steps):
            gain_out[at + 1] = total
            swap(at + 1).start()
        else:
            gains[...] = total

    swap(0).start()

    lines[0].finish(qkv_total)
    rows = qkv_parts.shape[2] // 4
    for at in range(4):
        sent[at] = qkv_total[at * rows : (at + 1) * rows, :].astype(LOW)
    for at in range(3):
        exchange(0, at).start()
    back[mine] = sent[mine]
    if with_out:
        for number in range(1, depth - 1):
            lines[1].turn(number)
    swap_on(0)
    for at in range(3):
        exchange(1, at).wait_recv()
    spread_parts((grad_gate, grad_up), gu_back, UNIT_TILE, True)
    swap_on(1)
    for at in range(2, len(steps)):
        swap_on(at)
    for at in range(3):
        exchange(0, at).wait_recv()
    spread_parts((grad_query, grad_key, grad_value), back, PAIR, deep)
    if with_out:
        lines[1].finish(out_total)
        grad_out[...] = out_total[...]

    for at in range(3):
        exchange(0, at).wait_send()
        exchange(1, at).wait_send()
    for at in range(len(steps)):
        swap(at).wait_send()
    plane.finish()
    for line in lines:
        line.close()


def last_call(deep, depth, rows, width, plane_operands, gu_rows, qkv_parts, out_parts):
    whole = pl.BlockSpec(memory_space=pltpu.VMEM)
    with_out = out_parts is not None
    operands = list(plane_operands) + [gu_rows, qkv_parts] + ([out_parts] if with_out else [])
    part_rows, part_width = qkv_parts.shape[2] // 4, qkv_parts.shape[3]
    outs = [like((rows, width), FULL), like((2, width), FULL)]
    outs += [like((part_rows, 2 * gu_rows.shape[2]), FULL)] * 2
    outs += [like((part_rows, 4 * part_width // 3), FULL)] * 3
    scratch = plane_scratch(rows, width) + line_scratch(depth, qkv_parts.shape)
    scratch.append(pltpu.VMEM(qkv_parts.shape[2:], FULL))
    if with_out:
        outs.append(like(out_parts.shape[2:], FULL))
        scratch += line_scratch(depth, out_parts.shape)
        scratch.append(pltpu.VMEM(out_parts.shape[2:], FULL))
    swaps = 3 + (depth - 1).bit_length()
    scratch += [
        pltpu.VMEM((4, part_rows, part_width), LOW),
        pltpu.VMEM((4, part_rows, part_width), LOW),
        pltpu.VMEM(gu_rows.shape, LOW),
        pltpu.SemaphoreType.DMA((2, 3)),
        pltpu.SemaphoreType.DMA((2, 3)),
        pltpu.VMEM((swaps, 2, width), FULL),
        pltpu.VMEM((swaps, 2, width), FULL),
        pltpu.SemaphoreType.DMA((swaps,)),
        pltpu.SemaphoreType.DMA((swaps,)),
    ]
    return pl.pallas_call(
        functools.partial(last_kernel, deep, with_out),
        out_shape=outs,
        in_specs=[whole] * len(operands),
        out_specs=[whole] * len(outs),
        scratch_shapes=scratch,
        compiler_params=pltpu.CompilerParams(
            collective_id=3, has_side_effects=True, vmem_limit_bytes=50 * 1024 * 1024
        ),
        cost_estimate=pl.CostEstimate(
            flops=rows * width * 100, bytes_accessed=rows * width * 400, transcendentals=0
        ),
    )(*operands)


class LineGather:
    def __init__(self, core_first, full, sems):
        self.core_first, self.full = core_first, full
        self.right_send, self.right_recv, self.left_send, self.left_recv = sems[:4]
        self.core_send, self.core_recv = sems[4:]
        self.depth = full.shape[1 if core_first else 0]

    def copy(self, at, send, recv, device):
        core = lax.axis_index("c")
        place = self.full.at[(core, at) if self.core_first else (at, core)]
        return pltpu.make_async_remote_copy(
            src_ref=place,
            dst_ref=place,
            send_sem=send.at[at],
            recv_sem=recv.at[at],
            device_id=device,
            device_id_type=pl.DeviceIdType.MESH,
        )

    def right(self, at):
        return self.copy(at, self.right_send, self.right_recv, beside(1))

    def left(self, at):
        return self.copy(at, self.left_send, self.left_recv, beside(-1))

    def core(self, at):
        return self.copy(at, self.core_send, self.core_recv, peer("c"))

    def pass_on(self, number):
        index, last = lax.axis_index("z"), self.depth - 1
        for step, move in ((1, self.right), (-1, self.left)):
            at = index - number * step
            inside = (at >= 0) & (at <= last)

            @pl.when(inside)
            def _():
                if number:
                    move(at).wait_recv()

                @pl.when((index < last) if step == 1 else (index > 0))
                def _():
                    move(at).start()

                if number or step == 1:
                    self.core(at).start()

    def close(self):
        index, last = lax.axis_index("z"), self.depth - 1
        for at in range(self.depth):
            self.core(at).wait()

            @pl.when((index < last) & (at <= index))
            def _():
                self.right(at).wait_send()

            @pl.when((index > 0) & (at >= index))
            def _():
                self.left(at).wait_send()


def first_kernel(with_out, *refs):
    refs = list(refs)

    def take(count):
        taken, refs[:count] = refs[:count], []
        return taken

    weights, (tokens, gain_parts) = take(5), take(2)
    w_out = take(1)[0] if with_out else None
    full_qkv, gu_rows, spread, gains = take(4)
    full_out = take(1)[0] if with_out else None
    spread_send, spread_recv, gain_all, gain_send, gain_recv = take(5)
    swap_send, swap_recv, local, qkv_parts, gu_parts = take(5)
    lines = [LineGather(True, full_qkv, take(6))]
    if with_out:
        lines.insert(0, LineGather(False, full_out, take(6)))

    depth = full_qkv.shape[1]
    at_z, at_x, at_c, at_y = (lax.axis_index(axis) for axis in AXES)
    mine = at_x * 2 + at_y
    steps = []
    step = 1
    while step < depth:
        steps.append(("z", step))
        step *= 2
    steps += [("c", 1), ("y", 1), ("x", 1)]
    index = ((at_x * 2 + at_y) * 2 + at_c) * depth + at_z
    far = [paired(axis, step) for axis, step in steps if step > 1]
    greet([peer("c"), peer("x"), peer("y"), peer("x", "y")] + far, line=True)

    def gather_parts(target, sources, tile, in_blocks):
        for part in range(4):
            for at in range(target.shape[2] // tile):
                source = sources[at % len(sources)]
                runs = part_columns(
                    source.shape[1], depth, in_blocks, part, at // len(sources) * tile, tile
                )
                pieces = [source[:, place : place + length] for _, place, length in runs]
                whole = pieces[0] if len(pieces) == 1 else jnp.concatenate(pieces, axis=1)
                target[part, :, at * tile : (at + 1) * tile] = whole

    gather_parts(qkv_parts, weights[:3], PAIR, with_out)
    members = [("y",), ("x",), ("x", "y")]
    part_rows = qkv_parts.shape[1]

    def exchange(kind, at):
        there = peer(*members[at])
        theirs = there.get("x", at_x) * 2 + there.get("y", at_y)
        source, target = (
            (qkv_parts, full_qkv.at[at_c, at_z, pl.ds(mine * part_rows, part_rows)]),
            (gu_parts, gu_rows.at[mine]),
        )[kind]
        return pltpu.make_async_remote_copy(
            src_ref=source.at[theirs],
            dst_ref=target,
            send_sem=swap_send.at[kind, at],
            recv_sem=swap_recv.at[kind, at],
            device_id=there,
            device_id_type=pl.DeviceIdType.MESH,
        )

    own_qkv = pltpu.make_async_copy(
        qkv_parts.at[mine],
        full_qkv.at[at_c, at_z, pl.ds(mine * part_rows, part_rows)],
        local.at[0],
    )
    own_gu = pltpu.make_async_copy(gu_parts.at[mine], gu_rows.at[mine], local.at[1])
    for at in (2, 0, 1):
        exchange(0, at).start()
    own_qkv.start()
    if with_out:
        own_out = pltpu.make_async_copy(w_out, full_out.at[at_z, at_c], local.at[2])
        own_out.start()

    def swap(at):
        axis, step = steps[at]
        count = 2**at
        place = gain_all.at[pl.ds((index // count) * count, count)]
        return pltpu.make_async_remote_copy(
            src_ref=place,
            dst_ref=place,
            send_sem=gain_send.at[at],
            recv_sem=gain_recv.at[at],
            device_id=paired(axis, step),
            device_id_type=pl.DeviceIdType.MESH,
        )

    gain_all[index] = gain_parts[0]
    for at in range(len(steps)):
        swap(at).start()
        if at == 1:
            gather_parts(gu_parts, weights[3:], UNIT_TILE, True)
            own_gu.start()
        swap(at).wait_recv()
        if steps[at][0] != "z" and steps[at - 1][0] == "z" and with_out:
            own_out.wait()
            lines[0].pass_on(0)
    for other in range(3):
        exchange(0, other).wait_recv()
    own_qkv.wait()
    lines[-1].pass_on(0)
    each = gain_parts.shape[2]
    for at in range(8 * depth):
        x, y, c, z = at // (4 * depth), at // (2 * depth) % 2, at // depth % 2, at % depth
        place = (((z * 2 + x) * 2 + c) * 2 + y) * each
        gains[:, place : place + each] = gain_all[at]

    plane = PlaneSum(None, tokens, None, None, None, spread_send, spread_recv, spread)
    gain = gains[0:1, :]
    for half, at in plane.pieces:
        values = tokens[plane.span(0, half, at), :].astype(FULL)
        plane.give(half, at, mix((values * factor_of(values) * gain).astype(LOW), depth))
    for at in range(3):
        exchange(1, at).start()

    todo = list(plane.pieces)
    share = -(-len(todo) // max(1, depth - 1))
    for number in range(1, depth):
        for line in lines:
            line.pass_on(number)
        for half, at in todo[(number - 1) * share : number * share]:
            plane.forward(half, at)
    for half, at in plane.pieces:
        plane.close_spread(half, at)
    own_gu.wait()
    for at in range(3):
        exchange(0, at).wait_send()
        exchange(1, at).wait()
    for at in range(len(steps)):
        swap(at).wait_send()
    for line in lines:
        line.close()


def first_call(depth, weights, tokens, gain_parts, w_out):
    rows, width = tokens.shape
    whole = pl.BlockSpec(memory_space=pltpu.VMEM)
    there = pl.BlockSpec(memory_space=pl.ANY)
    operands = list(weights) + [tokens, gain_parts]
    in_specs = [whole] * len(operands)
    part_rows, part_width, part_units = weights[0].shape[0], 3 * width // 4, weights[3].shape[1] // 2
    outs = [
        in_hbm((2, depth, 4 * part_rows, part_width), LOW),
        in_hbm((4, part_rows, part_units), LOW),
        in_hbm((4 * rows, width), LOW),
        like((2, width), FULL),
    ]
    out_specs = [there, there, whole, whole]
    swaps = 3 + (depth - 1).bit_length()
    scratch = [
        pltpu.SemaphoreType.DMA((6, 2, PIECES)),
        pltpu.SemaphoreType.DMA((6, 2, PIECES)),
        pltpu.VMEM((8 * depth, 2, width // (8 * depth)), FULL),
        pltpu.SemaphoreType.DMA((swaps,)),
        pltpu.SemaphoreType.DMA((swaps,)),
        pltpu.SemaphoreType.DMA((2, 3)),
        pltpu.SemaphoreType.DMA((2, 3)),
        pltpu.SemaphoreType.DMA((3,)),
        pltpu.VMEM((4, part_rows, part_width), LOW),
        pltpu.VMEM((4, part_rows, part_units), LOW),
    ]
    scratch += [pltpu.SemaphoreType.DMA((depth,))] * 6
    if w_out is not None:
        operands.append(w_out)
        in_specs.append(there)
        outs.append(in_hbm((depth, 2) + w_out.shape, LOW))
        out_specs.append(there)
        scratch += [pltpu.SemaphoreType.DMA((depth,))] * 6
    return pl.pallas_call(
        functools.partial(first_kernel, w_out is not None),
        out_shape=outs,
        in_specs=in_specs,
        out_specs=out_specs,
        scratch_shapes=scratch,
        compiler_params=pltpu.CompilerParams(
            collective_id=4, has_side_effects=True, vmem_limit_bytes=24 * 1024 * 1024
        ),
        cost_estimate=pl.CostEstimate(
            flops=rows * width * 100, bytes_accessed=rows * width * 200, transcendentals=0
        ),
    )(*operands)


def plane_scratch(rows, width):
    step = rows // (2 * PIECES)
    return [
        pltpu.VMEM((2, PIECES, 2, step, width), LOW),
        pltpu.VMEM((2, PIECES, step, width), LOW),
        pltpu.VMEM((2, PIECES, step, width), LOW),
        pltpu.SemaphoreType.DMA((6, 2, PIECES)),
        pltpu.SemaphoreType.DMA((6, 2, PIECES)),
    ]


def plane_call(kernel, number, rows, width, outs, *operands):
    whole = pl.BlockSpec(memory_space=pltpu.VMEM)
    return pl.pallas_call(
        kernel,
        out_shape=outs,
        in_specs=[whole] * len(operands),
        out_specs=[whole] * len(outs),
        scratch_shapes=plane_scratch(rows, width),
        compiler_params=pltpu.CompilerParams(
            collective_id=number, has_side_effects=True, vmem_limit_bytes=32 * 1024 * 1024
        ),
        cost_estimate=pl.CostEstimate(
            flops=rows * width * 100, bytes_accessed=rows * width * 200, transcendentals=0
        ),
    )(*operands)


def body(
    tokens,
    cotangent,
    seq_lengths,
    assignment,
    w_query,
    w_key,
    w_value,
    w_out,
    w_gate,
    w_up,
    w_down,
    gain_attn,
    gain_mlp,
):
    rows, width = tokens.shape
    depth = lax.axis_size("z")
    at_z, at_x, at_c, at_y = (lax.axis_index(axis) for axis in AXES)
    mine = at_x * 2 + at_y
    whole_heads = w_out.shape[0] % HEAD_DIM == 0
    head_deep = depth if whole_heads else 0
    head_width = width // 4

    def in_order(weight, back=False):
        if blocks_align(width, depth):
            return weight
        order = (2, 0, 1, 3, 4) if back else (1, 2, 0, 3, 4)
        shape = (depth, 2, 2) if back else (2, depth, 2)
        apart = weight.reshape(shape + (-1, weight.shape[1]))
        return apart.transpose(order).reshape(weight.shape)

    def core_columns(values, core):
        if blocks_align(width, depth):
            return lax.dynamic_slice_in_dim(values, core * (width // 2), width // 2, axis=1)
        apart = values.reshape(values.shape[0], depth, 2, 2, -1)
        part = lax.dynamic_index_in_dim(apart, core, 3, keepdims=False)
        return part.reshape(values.shape[0], -1)

    slot_at = [(at_z * 2 + x) * 2 + at_c for x in (at_x, 1 - at_x)]
    slot_length = [seq_lengths[assignment[slot]] for slot in slot_at]
    row = jnp.arange(rows)
    valid_rows = (at_y * rows + row < slot_length[0]).astype(FULL)[:, None]

    full_qkv, gu_rows, normed_all, gains, *rest = first_call(
        depth,
        (w_query, w_key, w_value, w_gate, w_up),
        tokens,
        jnp.stack([gain_attn, gain_mlp])[None].astype(FULL),
        w_out if whole_heads else None,
    )
    full_qkv = in_order(full_qkv.reshape(width, -1))
    gain_one, gain_two = gains[0], gains[1]
    full_gu = lax.all_gather(
        gu_rows.reshape(-1, gu_rows.shape[2]), ("c", "z"), axis=0, tiled=True
    )
    full_gu = in_order(full_gu)
    if whole_heads:
        full_out = rest[0].reshape(-1, width)
    else:
        every = lax.all_gather(w_out, AXES, axis=0, tiled=True)
        full_out = lax.dynamic_slice_in_dim(every, mine * head_width, head_width, axis=0)
    w_down, normed_all = lax.optimization_barrier((w_down, normed_all))

    grad_out = cotangent.astype(FULL) * valid_rows
    grad_low = grad_out.astype(LOW)
    normed_all, grad_low = lax.optimization_barrier((normed_all, grad_low))
    near = plane_gather_near(grad_low)
    qkv = dot(normed_all, full_qkv)
    qkv, near = lax.optimization_barrier((qkv, near))
    far = plane_gather_far(grad_low, near)
    cosine, sine = rope_tables(jnp.arange(2 * rows))
    info = jnp.stack([at_y.astype(jnp.int32)] + slot_length)
    heads_out, lse, qkv = attend(info, qkv, cosine, sine)
    w_down, heads_out, far = lax.optimization_barrier((w_down, heads_out, far))
    grad_low_all = plane_gathered(grad_low, near, far)
    full_down = lax.all_gather(w_down, ("z", "c"), axis=0, tiled=True)
    branch_low, branch_own = project(heads_out[None], full_out, False)
    attended, normed2_all = plane_call(
        forward_kernel,
        1,
        rows,
        width,
        [like((rows, width), FULL), in_hbm((4 * rows, width), LOW)],
        branch_low,
        branch_own,
        tokens,
        gain_two[None],
    )
    both, active = activate(normed2_all, full_gu)

    down_part = dot_rows(active, grad_low_all).astype(LOW)
    grad_w_down = lax.psum_scatter(down_part, ("z", "c"), scatter_dimension=0, tiled=True)
    grad_w_down = grad_w_down.astype(FULL)
    down_part, grad_low_all = lax.optimization_barrier((down_part, grad_low_all))
    grad_gu = activate_back(grad_low_all, full_down, both)
    theirs = dot_rows(core_columns(normed2_all, 1 - at_c), grad_gu).astype(LOW)
    from_core = swap_c(theirs)
    theirs, grad_gu = lax.optimization_barrier((theirs, grad_gu))
    back_low, back_own = project(grad_gu[None], full_gu, True)
    back_low, from_core, grad_gu = lax.optimization_barrier((back_low, from_core, grad_gu))
    ours = dot_rows(core_columns(normed2_all, at_c), grad_gu) + from_core.astype(FULL)
    grad_gu_rows = lax.psum_scatter(ours.astype(LOW), "z", scatter_dimension=0, tiled=True)
    ours, back_low = lax.optimization_barrier((ours, back_low))
    grad_attended, grad_gain_mlp, grad_branch = plane_call(
        backward_kernel,
        2,
        rows,
        width,
        [like((rows, width), FULL), like((1, width), FULL), in_hbm((4 * rows, width), LOW)],
        back_low,
        back_own,
        attended,
        gain_two[None],
        grad_out,
    )
    grad_branch, active = lax.optimization_barrier((grad_branch, active))

    grad_w_out = dot_rows(heads_out, grad_branch)
    out_parts = None
    if whole_heads:
        out_parts = grad_w_out.astype(LOW).reshape(depth, 2, -1, width)
    else:
        spread = lax.dynamic_update_slice_in_dim(
            jnp.zeros((width, width), FULL), grad_w_out, mine * head_width, axis=0
        )
        grad_w_out = lax.psum_scatter(spread, AXES, scatter_dimension=0, tiled=True)
    grad_mixed = dot_through(grad_branch, full_out).astype(LOW)
    last_low, last_own = project(active[None], full_down, False)
    last_low, grad_mixed = lax.optimization_barrier((last_low, grad_mixed))
    near = plane_reduce_near(last_low)
    grad_qkv = attend_back(info, qkv, grad_mixed, lse, cosine, sine)
    grad_qkv, near, grad_w_down = lax.optimization_barrier((grad_qkv, near, grad_w_down))
    far = plane_reduce_far(last_low, near)
    grad_qkv_part = in_order(dot_rows(normed_all, grad_qkv).astype(LOW), True)
    back_low, back_own = project(grad_qkv[None], full_qkv, True)
    back_low, far = lax.optimization_barrier((back_low, far))
    result = attended + plane_reduced(last_own, near, far)
    output = (result * valid_rows).astype(LOW)
    grad_input, grad_gains, *last_weights = last_call(
        head_deep,
        depth,
        rows,
        width,
        [
            back_low,
            back_own,
            tokens,
            gain_one[None],
            grad_attended,
            grad_gain_mlp,
        ],
        grad_gu_rows.reshape(4, -1, grad_gu_rows.shape[1]),
        grad_qkv_part.reshape(2, depth, -1, grad_qkv_part.shape[1]),
        out_parts,
    )
    grad_w_gate, grad_w_up, grad_w_query, grad_w_key, grad_w_value = last_weights[:5]
    if whole_heads:
        grad_w_out = last_weights[5]
    index = ((at_z * 2 + at_x) * 2 + at_c) * 2 + at_y
    part = width // (8 * depth)
    grad_gains = lax.dynamic_slice_in_dim(grad_gains, index * part, part, axis=1)
    return (
        output,
        grad_input,
        grad_w_query,
        grad_w_key,
        grad_w_value,
        grad_w_out,
        grad_w_gate,
        grad_w_up,
        grad_w_down,
        grad_gains[0],
        grad_gains[1],
    )


def solution(mesh):
    shape = (mesh.shape["dp"] // 4, 2, 2, mesh.shape["seq"])
    grid = Mesh(mesh.devices.reshape(shape), AXES)
    split = P(AXES, None)
    part = P(AXES)
    return jax.shard_map(
        body,
        mesh=grid,
        in_specs=(split, split, P(), P()) + (split,) * 7 + (part, part),
        out_specs=(split,) * 9 + (part, part),
        check_vma=False,
    )
```

```python
import functools

import jax
import jax.experimental.pallas as pl
import jax.experimental.pallas.tpu as pltpu
import jax.numpy as jnp
from jax import lax
from jax.sharding import Mesh, PartitionSpec as P

HEAD_DIM = 64
PAIR = 2 * HEAD_DIM
norm_eps = 1e-05
rope_base = 130000.0
AXES = ("z", "x", "c", "y")
LOW = jnp.bfloat16
FULL = jnp.float32
like = jax.ShapeDtypeStruct
in_hbm = pltpu.HBM


def hbm(*values):
    return [pltpu.with_memory_space_constraint(value, pltpu.HBM) for value in values]


def swap_x(value):
    return lax.ppermute(value, "x", [(0, 1), (1, 0)])


def swap_y(value):
    return lax.ppermute(value, "y", [(0, 1), (1, 0)])


def swap_c(value):
    return lax.ppermute(value, "c", [(0, 1), (1, 0)])


def plane_gather_near(value):
    half = value.shape[0] // 2
    return swap_y(value[:half]), swap_x(value[half:])


def plane_gather_far(value, near):
    half = value.shape[0] // 2
    return (
        swap_x(jnp.concatenate([value[:half], near[0]], axis=0)),
        swap_y(jnp.concatenate([value[half:], near[1]], axis=0)),
    )


def plane_gathered(value, near, far):
    half = value.shape[0] // 2
    top, low = far
    return jnp.concatenate(
        [value, near[0], low[:half], top[:half], near[1], top[half:], low[half:]], axis=0
    )


def plane_blocks(value):
    count = value.shape[0] // 4
    return [value[at * count : (at + 1) * count] for at in range(4)]


def plane_reduce_near(value):
    _, by_y, by_x, by_d = plane_blocks(value)
    half = by_y.shape[0] // 2
    return (
        swap_x(jnp.concatenate([by_x[:half], by_d[:half]], axis=0)),
        swap_y(jnp.concatenate([by_y[half:], by_d[half:]], axis=0)),
    )


def plane_reduce_far(value, near):
    _, by_y, by_x, _ = plane_blocks(value)
    half = by_y.shape[0] // 2
    return (
        swap_y((by_y[:half].astype(FULL) + near[0][half:].astype(FULL)).astype(LOW)),
        swap_x((by_x[half:].astype(FULL) + near[1][half:].astype(FULL)).astype(LOW)),
    )


def plane_reduced(own, near, far):
    half = own.shape[0] // 2
    return own + jnp.concatenate(
        [
            near[0][:half].astype(FULL) + far[0].astype(FULL),
            near[1][:half].astype(FULL) + far[1].astype(FULL),
        ],
        axis=0,
    )


def part_place(depth, part, block):
    return ((block // 2 * 2 + part // 2) * 2 + block % 2) * 2 + part % 2


def part_columns(width, depth, in_blocks, part, start, count):
    if not in_blocks:
        return [(0, part * (width // 4) + start, count)]
    each = width // (8 * depth)
    length = min(each, count)
    return [
        (
            at,
            part_place(depth, part, (start + at) // each) * each + (start + at) % each,
            length,
        )
        for at in range(0, count, length)
    ]


def factor_of(values):
    return lax.rsqrt(jnp.mean(values * values, axis=-1, keepdims=True) + norm_eps)


def rope_tables(positions):
    halves = HEAD_DIM // 2
    frequency = rope_base ** (-(jnp.arange(halves).astype(FULL) * 2.0 / HEAD_DIM))
    angles = positions.astype(FULL)[:, None] * frequency[None, :]
    cosine = jnp.cos(angles)
    sine = jnp.sin(angles)
    return (
        jnp.concatenate([cosine] * 4, axis=1),
        jnp.concatenate([-sine, sine, -sine, sine], axis=1),
    )


def turned(values, low_half):
    lanes = values.shape[1]
    halves = HEAD_DIM // 2
    return jnp.where(
        low_half, pltpu.roll(values, lanes - halves, 1), pltpu.roll(values, halves, 1)
    )


def lane_masks(rows):
    lane = lax.broadcasted_iota(jnp.int32, (rows, PAIR), 1)
    return lane % HEAD_DIM < HEAD_DIM // 2, lane < HEAD_DIM


def diagonal_mask(first, length, rows):
    query = lax.broadcasted_iota(jnp.int32, (rows, rows), 0)
    key = lax.broadcasted_iota(jnp.int32, (rows, rows), 1)
    return (key <= query) & (key + first < length)


def attend_kernel(info, qkv_ref, c_ref, s_ref, mixed, lse, qkv_out):
    rows = qkv_ref.shape[0] // 2
    length = info[1 + pl.program_id(0)]
    scale = HEAD_DIM ** (-0.5)
    low_half, first_head = lane_masks(rows)
    place = [pl.multiple_of(jnp.where(info[0] == at, 0, rows), rows) for at in range(2)]
    queries, keys, values = [], [], []
    for at in range(2):
        span = pl.ds(place[at], rows)
        table = pl.ds(at * rows, rows)
        for number, kept in enumerate((queries, keys, values)):
            lanes = slice(number * PAIR, (number + 1) * PAIR)
            item = qkv_ref[span, lanes]
            if number < 2:
                item = item * c_ref[table, :] + turned(item, low_half) * s_ref[table, :]
            item = item.astype(LOW)
            qkv_out[span, lanes] = item
            kept.append(item)
    for at in range(2):
        allowed = diagonal_mask(at * rows, length, rows)
        found, logs = [], []
        for head in range(2):
            only = first_head if head == 0 else jnp.logical_not(first_head)
            query = jnp.where(only, queries[at], jnp.zeros_like(queries[at]))
            scores = []
            for block in range(at + 1):
                score = dot_through(query, keys[block]) * scale
                scores.append(jnp.where(allowed, score, -1e30) if block == at else score)
            top = jnp.max(scores[0], axis=1, keepdims=True)
            for score in scores[1:]:
                top = jnp.maximum(top, jnp.max(score, axis=1, keepdims=True))
            weights = [jnp.exp(score - top) for score in scores]
            total = jnp.sum(weights[0], axis=1, keepdims=True)
            for weight in weights[1:]:
                total = total + jnp.sum(weight, axis=1, keepdims=True)
            share = 1.0 / total
            out = dot((weights[0] * share).astype(LOW), values[0])
            for block in range(1, at + 1):
                out = out + dot((weights[block] * share).astype(LOW), values[block])
            found.append(out)
            logs.append(top + jnp.log(total))
        span = pl.ds(place[at], rows)
        mixed[span, :] = jnp.where(first_head, found[0], found[1]).astype(LOW)
        lse[span, :] = jnp.where(first_head, logs[0], logs[1])


def attend_back_kernel(info, qkv_ref, g_ref, lse_ref, c_ref, s_ref, grads_out):
    rows = qkv_ref.shape[0] // 2
    length = info[1 + pl.program_id(0)]
    scale = HEAD_DIM ** (-0.5)
    low_half, first_head = lane_masks(rows)
    place = [pl.multiple_of(jnp.where(info[0] == at, 0, rows), rows) for at in range(2)]
    spans = [pl.ds(start, rows) for start in place]
    keys = [qkv_ref[span, PAIR : 2 * PAIR] for span in spans]
    values = [qkv_ref[span, 2 * PAIR :] for span in spans]
    key_sums = [[None, None], [None, None]]
    value_sums = [[None, None], [None, None]]

    def unrotated(item, at):
        table = pl.ds(at * rows, rows)
        scaled = item * s_ref[table, :]
        return (item * c_ref[table, :] + turned(scaled, low_half)).astype(LOW)

    def added(old, new):
        return new if old is None else old + new

    for at in range(2):
        allowed = diagonal_mask(at * rows, length, rows)
        query_all, grad_all, logs = qkv_ref[spans[at], :PAIR], g_ref[spans[at], :], lse_ref[spans[at], :]
        found = []
        for head in range(2):
            only = first_head if head == 0 else jnp.logical_not(first_head)
            query = jnp.where(only, query_all, jnp.zeros_like(query_all))
            grad = jnp.where(only, grad_all, jnp.zeros_like(grad_all))
            log = logs[:, head * HEAD_DIM : head * HEAD_DIM + 1]
            probs, grads = [], []
            inner = jnp.zeros((rows, 1), FULL)
            for block in range(at + 1):
                prob = jnp.exp(dot_through(query, keys[block]) * scale - log)
                if block == at:
                    prob = jnp.where(allowed, prob, 0.0)
                grad_prob = dot_through(grad, values[block])
                inner = inner + jnp.sum(prob * grad_prob, axis=1, keepdims=True)
                probs.append(prob)
                grads.append(grad_prob)
            out = None
            for block in range(at + 1):
                grad_score = (probs[block] * (grads[block] - inner)).astype(LOW)
                out = added(out, dot(grad_score, keys[block]))
                key_sums[block][head] = added(key_sums[block][head], dot_rows(grad_score, query_all))
                value_sums[block][head] = added(
                    value_sums[block][head], dot_rows(probs[block].astype(LOW), grad_all)
                )
            found.append(out)
        grads_out[spans[at], :PAIR] = unrotated(jnp.where(first_head, found[0], found[1]) * scale, at)
    for at in range(2):
        both = jnp.where(first_head, key_sums[at][0], key_sums[at][1]) * scale
        grads_out[spans[at], PAIR : 2 * PAIR] = unrotated(both, at)
        both = jnp.where(first_head, value_sums[at][0], value_sums[at][1])
        grads_out[spans[at], 2 * PAIR :] = both.astype(LOW)


def attend(info, qkv, cosine, sine):
    total, width = qkv.shape[0], qkv.shape[1] // 3
    slot_rows, pairs = total // 2, width // PAIR
    part = pl.BlockSpec((slot_rows, PAIR), lambda slot, pair, info: (slot, pair))
    three = pl.BlockSpec((slot_rows, 3 * PAIR), lambda slot, pair, info: (slot, pair))
    table = pl.BlockSpec((slot_rows, PAIR), lambda slot, pair, info: (0, 0))
    return pl.pallas_call(
        attend_kernel,
        grid_spec=pltpu.PrefetchScalarGridSpec(
            num_scalar_prefetch=1,
            grid=(2, pairs),
            in_specs=[three, table, table],
            out_specs=[part, part, three],
        ),
        out_shape=[
            in_hbm((total, width), LOW),
            in_hbm((total, width), FULL),
            in_hbm((total, 3 * width), LOW),
        ],
        compiler_params=pltpu.CompilerParams(vmem_limit_bytes=16 * 1024 * 1024),
        cost_estimate=pl.CostEstimate(
            flops=16 * total * slot_rows * width,
            bytes_accessed=total * width * 24,
            transcendentals=total * slot_rows * width // HEAD_DIM,
        ),
    )(info, qkv, cosine, sine)


def attend_back(info, qkv, grads, lse, cosine, sine):
    total, width = grads.shape
    slot_rows, pairs = total // 2, width // PAIR
    part = pl.BlockSpec((slot_rows, PAIR), lambda slot, pair, info: (slot, pair))
    three = pl.BlockSpec((slot_rows, 3 * PAIR), lambda slot, pair, info: (slot, pair))
    table = pl.BlockSpec((slot_rows, PAIR), lambda slot, pair, info: (0, 0))
    return pl.pallas_call(
        attend_back_kernel,
        grid_spec=pltpu.PrefetchScalarGridSpec(
            num_scalar_prefetch=1,
            grid=(2, pairs),
            in_specs=[three, part, part, table, table],
            out_specs=three,
        ),
        out_shape=in_hbm((total, 3 * width), LOW),
        compiler_params=pltpu.CompilerParams(vmem_limit_bytes=16 * 1024 * 1024),
        cost_estimate=pl.CostEstimate(
            flops=40 * total * slot_rows * width,
            bytes_accessed=total * width * 18,
            transcendentals=total * slot_rows * width // HEAD_DIM,
        ),
    )(info, *hbm(qkv, grads, lse), cosine, sine)


def dot(left, right):
    return jnp.dot(left, right, preferred_element_type=FULL)


def dot_rows(left, right):
    return lax.dot_general(left, right, (((0,), (0,)), ((), ())), preferred_element_type=FULL)


def dot_through(left, right):
    return lax.dot_general(left, right, (((1,), (1,)), ((), ())), preferred_element_type=FULL)


UNIT_TILE = 256


def activate_kernel(normed, weight, both_ref, active_ref):
    both = dot(normed[...], weight[...])
    both_ref[...] = both
    gate, upper = both[:, :UNIT_TILE], both[:, UNIT_TILE:]
    active_ref[...] = (gate * jax.nn.sigmoid(gate) * upper).astype(LOW)


def activate(normed, weight):
    rows, width = normed.shape
    units = weight.shape[1] // 2
    return pl.pallas_call(
        activate_kernel,
        grid=(units // UNIT_TILE,),
        in_specs=[
            pl.BlockSpec((rows, width), lambda at: (0, 0)),
            pl.BlockSpec((width, 2 * UNIT_TILE), lambda at: (0, at)),
        ],
        out_specs=[
            pl.BlockSpec((rows, 2 * UNIT_TILE), lambda at: (0, at)),
            pl.BlockSpec((rows, UNIT_TILE), lambda at: (0, at)),
        ],
        out_shape=[in_hbm((rows, 2 * units), FULL), in_hbm((rows, units), LOW)],
        compiler_params=pltpu.CompilerParams(vmem_limit_bytes=40 * 1024 * 1024),
        cost_estimate=pl.CostEstimate(
            flops=4 * rows * units * width,
            bytes_accessed=rows * units * 10 + units * width * 4,
            transcendentals=rows * units,
        ),
    )(*hbm(normed, weight))


def activate_back_kernel(grad_low, weight, both_ref, out):
    grads = dot_through(grad_low[...], weight[...])
    gate, upper = both_ref[:, :UNIT_TILE], both_ref[:, UNIT_TILE:]
    sigmoid = jax.nn.sigmoid(gate)
    out[:, :UNIT_TILE] = (grads * upper * sigmoid * (1.0 + gate * (1.0 - sigmoid))).astype(LOW)
    out[:, UNIT_TILE:] = (grads * gate * sigmoid).astype(LOW)


def activate_back(grad_low, weight, both):
    rows, units = both.shape[0], both.shape[1] // 2
    width = grad_low.shape[1]
    part = pl.BlockSpec((rows, 2 * UNIT_TILE), lambda at: (0, at))
    return pl.pallas_call(
        activate_back_kernel,
        grid=(units // UNIT_TILE,),
        in_specs=[
            pl.BlockSpec((rows, width), lambda at: (0, 0)),
            pl.BlockSpec((UNIT_TILE, width), lambda at: (at, 0)),
            part,
        ],
        out_specs=part,
        out_shape=in_hbm((rows, 2 * units), LOW),
        compiler_params=pltpu.CompilerParams(vmem_limit_bytes=40 * 1024 * 1024),
        cost_estimate=pl.CostEstimate(
            flops=2 * rows * units * width,
            bytes_accessed=rows * units * 12 + units * width * 2,
            transcendentals=rows * units,
        ),
    )(*hbm(grad_low, weight, both))


def project_kernel(through, left, weight, low, own):
    groups, total, depth = left.shape
    if through:
        found = dot_through(left[0], weight[:, :depth])
        for group in range(1, groups):
            found = found + dot_through(
                left[group], weight[:, group * depth : (group + 1) * depth]
            )
    else:
        found = dot(left[0], weight[...])
    low[...] = found.astype(LOW)
    own[...] = found[: own.shape[0], :]


def project(left, weight, through):
    groups, total, depth = left.shape
    width = weight.shape[0] if through else weight.shape[1]
    tile = 256
    block = (tile, groups * depth) if through else (depth, tile)
    return pl.pallas_call(
        functools.partial(project_kernel, through),
        grid=(width // tile,),
        in_specs=[
            pl.BlockSpec((groups, total, depth), lambda at: (0, 0, 0)),
            pl.BlockSpec(block, (lambda at: (at, 0)) if through else (lambda at: (0, at))),
        ],
        out_specs=[
            pl.BlockSpec((total, tile), lambda at: (0, at)),
            pl.BlockSpec((total // 4, tile), lambda at: (0, at)),
        ],
        out_shape=[in_hbm((total, width), LOW), in_hbm((total // 4, width), FULL)],
        compiler_params=pltpu.CompilerParams(vmem_limit_bytes=40 * 1024 * 1024),
        cost_estimate=pl.CostEstimate(
            flops=2 * groups * total * depth * width,
            bytes_accessed=2 * groups * depth * (total + width) + 3 * total * width,
            transcendentals=0,
        ),
    )(*hbm(left, weight))


AXIS_BLOCK = {"y": 1, "x": 2}
PIECES = 4
FIRST, SECOND = ("x", "y"), ("y", "x")


def peer(*axes):
    return {axis: 1 - lax.axis_index(axis) for axis in axes}


def paired(axis, step):
    index = lax.axis_index(axis)
    return {axis: index + step * (1 - 2 * ((index // step) % 2))}


def beside(step):
    count = lax.axis_size("z")
    return {"z": (lax.axis_index("z") + step + count) % count}


def signal(barrier, device):
    pl.semaphore_signal(barrier, inc=1, device_id=device, device_id_type=pl.DeviceIdType.MESH)


def greet(devices, line=False):
    barrier = pltpu.get_barrier_semaphore()
    count = len(devices)
    for device in devices:
        signal(barrier, device)
    if line:
        index, last = lax.axis_index("z"), lax.axis_size("z") - 1
        for step, there in ((1, index < last), (-1, index > 0)):

            @pl.when(there)
            def _():
                signal(barrier, beside(step))

            count = count + there.astype(jnp.int32)
    pl.semaphore_wait(barrier, count)


class PlaneSum:
    def __init__(
        self, low, own, first_in, second_out, second_in, send, recv, between, local, spread=None
    ):
        self.low, self.own, self.spread = low, own, spread
        self.first_in, self.second_out, self.second_in = first_in, second_out, second_in
        self.send, self.recv = send, recv
        self.between, self.local = between, local
        self.rows = own.shape[0]
        self.step = self.rows // (2 * PIECES)
        self.pieces = [(half, at) for at in range(PIECES) for half in range(2)]

    def span(self, block, half, at):
        return pl.ds(block * self.rows + (half * PIECES + at) * self.step, self.step)

    def copy(self, kind, half, at, source, target, axis):
        return pltpu.make_async_remote_copy(
            src_ref=source,
            dst_ref=target,
            send_sem=self.send.at[kind, half, at],
            recv_sem=self.recv.at[kind, half, at],
            device_id=peer(axis),
            device_id_type=pl.DeviceIdType.MESH,
        )

    def first(self, kind, half, at):
        block = (AXIS_BLOCK[FIRST[half]], 3)[kind]
        return self.copy(
            kind,
            half,
            at,
            self.low.at[self.span(block, half, at)],
            self.first_in.at[half, at, kind],
            FIRST[half],
        )

    def second(self, half, at):
        return self.copy(
            2, half, at, self.second_out.at[half, at], self.second_in.at[half, at], SECOND[half]
        )

    def spreading(self, axis, half, at):
        return self.copy(
            2 + AXIS_BLOCK[axis],
            half,
            at,
            self.spread.at[self.span(0, half, at)],
            self.spread.at[self.span(AXIS_BLOCK[axis], half, at)],
            axis,
        )

    def forwarding(self, half, at):
        block = AXIS_BLOCK[SECOND[half]]
        return self.copy(
            5,
            half,
            at,
            self.spread.at[self.span(block, half, at)],
            self.spread.at[self.span(3, half, at)],
            FIRST[half],
        )

    def load(self, half):
        count = self.rows // 2
        place = pl.ds(AXIS_BLOCK[SECOND[half]] * self.rows + half * count, count)
        return pltpu.make_async_copy(self.low.at[place], self.between.at[half], self.local.at[half])

    def start(self):
        for half, at in self.pieces:
            self.first(0, half, at).start()
            self.first(1, half, at).start()
        for half in range(2):
            self.load(half).start()

    def middle(self, half, at):
        if at == 0:
            self.load(half).wait()
        self.first(0, half, at).wait_recv()
        self.first(1, half, at).wait_recv()
        total = self.between[half, at * self.step : (at + 1) * self.step, :].astype(FULL)
        total = total + self.first_in[half, at, 1].astype(FULL)
        self.second_out[half, at] = total.astype(LOW)
        self.second(half, at).start()

    def total(self, half, at):
        self.second(half, at).wait_recv()
        total = self.own[self.span(0, half, at), :] + self.first_in[half, at, 0].astype(FULL)
        return total + self.second_in[half, at].astype(FULL)

    def give(self, half, at, rows):
        self.spread[self.span(0, half, at), :] = rows
        self.spreading("x", half, at).start()
        self.spreading("y", half, at).start()

    def forward(self, half, at):
        self.spreading(SECOND[half], half, at).wait_recv()
        self.forwarding(half, at).start()

    def finish(self):
        for half, at in self.pieces:
            self.first(0, half, at).wait_send()
            self.first(1, half, at).wait_send()
            self.second(half, at).wait_send()
            if self.spread is not None:
                self.close_spread(half, at)

    def close_spread(self, half, at):
        self.spreading("x", half, at).wait_send()
        self.spreading("y", half, at).wait_send()
        self.spreading(FIRST[half], half, at).wait_recv()
        self.forwarding(half, at).wait()

    def run(self, each):
        count = len(self.pieces)
        self.start()
        for turn in range(count + 3):
            if turn < count:
                self.middle(*self.pieces[turn])
            if 1 <= turn <= count:
                half, at = self.pieces[turn - 1]
                self.give(half, at, each(self.span(0, half, at), self.total(half, at)))
            if turn >= 3:
                self.forward(*self.pieces[turn - 3])
        self.finish()


def forward_kernel(low, own, tokens, gain, attended, spread, *scratch):
    greet([peer("x"), peer("y")])
    plane = PlaneSum(low, own, *scratch, spread)

    def each(span, total):
        values = tokens[span, :].astype(FULL) + total
        attended[span, :] = values
        return mix((values * factor_of(values) * gain[...]).astype(LOW), lax.axis_size("z"))

    plane.run(each)


def norm_back(values, gain, grads):
    factor = factor_of(values)
    weighted = grads * gain
    inner = jnp.mean(weighted * values, axis=-1, keepdims=True)
    grad_gain = jnp.sum(grads * values * factor, axis=0, keepdims=True)
    return factor * weighted - values * (factor * factor * factor) * inner, grad_gain


def backward_kernel(low, own, attended, gain, grad_out, grad_attended, grad_gain, spread, *scratch):
    greet([peer("x"), peer("y")])
    plane = PlaneSum(low, own, *scratch, spread)
    grad_gain[...] = jnp.zeros_like(grad_gain)

    def each(span, total):
        grads, for_gain = norm_back(
            attended[span, :], gain[...], mix(total, lax.axis_size("z"), True)
        )
        grads = grads + grad_out[span, :]
        grad_attended[span, :] = grads
        grad_gain[...] += for_gain
        return grads.astype(LOW)

    plane.run(each)


def blocks_align(width, depth):
    return (width // (4 * depth)) % 128 == 0


def mix(values, depth, back=False):
    if not blocks_align(values.shape[1], depth):
        return values
    block = values.shape[1] // (4 * depth)
    order = [(z * 2 + x) * 2 + c for c in range(2) for z in range(depth) for x in range(2)]
    if back:
        order = sorted(range(4 * depth), key=order.__getitem__)
    return jnp.concatenate([values[:, at * block : (at + 1) * block] for at in order], axis=1)


class LineSum:
    def __init__(self, core_first, parts, sums, line_in, last_in, ours, sems):
        self.core_first, self.parts, self.ours = core_first, parts, ours
        self.sums, self.line_in, self.last_in = sums, line_in, last_in
        self.core_send, self.core_recv, self.send, self.right_recv, self.left_recv = sems[:5]
        self.local = sems[5]
        self.depth = sums.shape[0]

    def place(self, at, core):
        return (core, at) if self.core_first else (at, core)

    def core(self, at):
        return pltpu.make_async_remote_copy(
            src_ref=self.parts.at[self.place(at, 1 - lax.axis_index("c"))],
            dst_ref=self.sums.at[at],
            send_sem=self.core_send.at[at],
            recv_sem=self.core_recv.at[at],
            device_id=peer("c"),
            device_id_type=pl.DeviceIdType.MESH,
        )

    def line(self, at, step, last=False):
        sems = self.right_recv if step == 1 else self.left_recv
        return pltpu.make_async_remote_copy(
            src_ref=self.sums.at[at],
            dst_ref=self.last_in if last else self.line_in.at[at],
            send_sem=self.send.at[at],
            recv_sem=sems.at[at],
            device_id=beside(step),
            device_id_type=pl.DeviceIdType.MESH,
        )

    def start(self):
        ends_first = sorted(range(self.depth), key=lambda at: min(at, self.depth - 1 - at))
        for at in ends_first:
            self.core(at).start()
            self.load(at).start()

    def load(self, at):
        place = self.parts.at[self.place(at, lax.axis_index("c"))]
        return pltpu.make_async_copy(place, self.ours.at[at], self.local.at[at])

    def both_cores(self, at):
        self.load(at).wait()
        self.core(at).wait_recv()
        return self.ours[at].astype(FULL) + self.sums[at].astype(FULL)

    def pass_on(self, at, step, first):
        total = self.both_cores(at)
        if not first:
            self.line(at, step).wait_recv()
            total = total + self.line_in[at].astype(FULL)
        self.sums[at] = total.astype(LOW)
        if step == 1:
            self.line(at, 1).start()
            return
        ends = at == lax.axis_index("z") - 1

        @pl.when(ends)
        def _():
            self.line(at, -1, True).start()

        @pl.when(jnp.logical_not(ends))
        def _():
            self.line(at, -1).start()

    def from_ends(self):
        index, last = lax.axis_index("z"), self.depth - 1
        for number in range(last):

            @pl.when(index == 0)
            def _():
                self.pass_on(last - number, 1, True)

            @pl.when(index == last)
            def _():
                self.pass_on(number, -1, True)

    def turn(self, time):
        index, last = lax.axis_index("z"), self.depth - 1

        @pl.when((index > 0) & (index <= time))
        def _():
            self.pass_on(index + last - time, 1, False)

        @pl.when((index < last) & (last - index <= time))
        def _():
            self.pass_on(time - (last - index), -1, False)

    def finish(self, total):
        index, last = lax.axis_index("z"), self.depth - 1
        total[...] = self.both_cores(index)

        @pl.when(index > 0)
        def _():
            self.line(index, 1).wait_recv()
            total[...] += self.line_in[index].astype(FULL)

        @pl.when(index < last)
        def _():
            self.line(index, -1, True).wait_recv()
            total[...] += self.last_in[...].astype(FULL)

    def close(self):
        index = lax.axis_index("z")
        for at in range(self.depth):
            self.core(at).wait_send()

            @pl.when(index < at)
            def _():
                self.line(at, 1).wait_send()

            @pl.when(index > at)
            def _():
                self.line(at, -1).wait_send()


def line_scratch(depth, shape):
    rows, columns = shape[2:]
    sems = [pltpu.SemaphoreType.DMA((depth,))] * 6
    buffers = [pltpu.VMEM((depth, rows, columns), LOW)] * 2
    buffers += [pltpu.VMEM((rows, columns), LOW), pltpu.VMEM((depth, rows, columns), LOW)]
    return buffers + sems


def last_kernel(deep, with_out, *refs):
    refs = list(refs)

    def take(count):
        taken, refs[:count] = refs[:count], []
        return taken

    low, own, tokens, gain, grad_gain_mlp, gu_rows, qkv_parts = take(7)
    out_parts = take(1)[0] if with_out else None
    grad_input, gains, grad_gate, grad_up, grad_query, grad_key, grad_value = take(7)
    grad_out = take(1)[0] if with_out else None
    plane_refs = take(7)
    qkv_refs, (qkv_total,) = take(10), take(1)
    if with_out:
        out_refs, (out_total,) = take(10), take(1)
    sent, back, gu_back, back_send, back_recv, own_local = take(6)
    gain_in, gain_out, gain_send, gain_recv = take(4)

    depth = qkv_parts.shape[1]
    steps = [("c", 1), ("x", 1), ("y", 1)]
    step = 1
    while step < depth:
        steps.append(("z", step))
        step *= 2
    far = [paired(axis, step) for axis, step in steps if step > 1]
    greet([peer("c"), peer("x"), peer("y"), peer("x", "y")] + far, line=True)

    plane = PlaneSum(low, own, *plane_refs)
    lines = [LineSum(True, qkv_parts, *qkv_refs[:4], qkv_refs[4:])]
    if with_out:
        lines.append(LineSum(False, out_parts, *out_refs[:4], out_refs[4:]))
    mine = lax.axis_index("x") * 2 + lax.axis_index("y")
    members = [("y",), ("x",), ("x", "y")]

    def exchange(kind, at):
        there = peer(*members[at])
        theirs = there.get("x", lax.axis_index("x")) * 2 + there.get("y", lax.axis_index("y"))
        source, target = ((sent, back), (gu_rows, gu_back))[kind]
        return pltpu.make_async_remote_copy(
            src_ref=source.at[theirs],
            dst_ref=target.at[mine],
            send_sem=back_send.at[kind, at],
            recv_sem=back_recv.at[kind, at],
            device_id=there,
            device_id_type=pl.DeviceIdType.MESH,
        )

    def spread_parts(targets, source, tile, in_blocks):
        for part in range(4):
            for at in range(source.shape[2] // tile):
                target = targets[at % len(targets)]
                columns = source[part, :, at * tile : (at + 1) * tile].astype(target.dtype)
                runs = part_columns(
                    target.shape[1], depth, in_blocks, part, at // len(targets) * tile, tile
                )
                for own, place, length in runs:
                    target[:, place : place + length] = columns[:, own : own + length]

    for line in lines:
        line.start()
    plane.start()
    for line in lines:
        line.from_ends()
    own_units = pltpu.make_async_copy(gu_rows.at[mine], gu_back.at[mine], own_local.at[0])
    own_units.start()

    grad_gain = jnp.zeros((1, own.shape[1]), FULL)
    todo = [("middle", 0)]
    for at in range(1, len(plane.pieces)):
        todo += [("middle", at), ("total", at - 1)]
    todo.append(("total", len(plane.pieces) - 1))
    share = -(-len(todo) // max(1, depth - 1))
    for number in range(depth - 1):
        if number:
            lines[0].turn(number)
        if number == (depth - 1) // 2:
            for at in range(3):
                exchange(1, at).start()
        for kind, at in todo[number * share : (number + 1) * share]:
            half, piece = plane.pieces[at]
            if kind == "middle":
                plane.middle(half, piece)
                continue
            span = plane.span(0, half, piece)
            grads, for_gain = norm_back(
                tokens[span, :].astype(FULL), gain[...], mix(plane.total(half, piece), depth, True)
            )
            grad_input[span, :] = grads
            grad_gain = grad_gain + for_gain

    gain_out[0, 0:1, :] = grad_gain
    gain_out[0, 1:2, :] = grad_gain_mlp[...]

    def swap(at):
        axis, step = steps[at]
        return pltpu.make_async_remote_copy(
            src_ref=gain_out.at[at],
            dst_ref=gain_in.at[at],
            send_sem=gain_send.at[at],
            recv_sem=gain_recv.at[at],
            device_id=paired(axis, step),
            device_id_type=pl.DeviceIdType.MESH,
        )

    def swap_on(at):
        swap(at).wait_recv()
        total = gain_out[at] + gain_in[at]
        if at + 1 < len(steps):
            gain_out[at + 1] = total
            swap(at + 1).start()
        else:
            gains[...] = total

    swap(0).start()
    for at in range(3):
        swap_on(at)

    lines[0].finish(qkv_total)
    rows = qkv_parts.shape[2] // 4
    for at in range(4):
        sent[at] = qkv_total[at * rows : (at + 1) * rows, :].astype(LOW)
    for at in range(3):
        exchange(0, at).start()
    back[mine] = sent[mine]
    if with_out:
        for number in range(1, depth - 1):
            lines[1].turn(number)
    swap_on(3)
    for at in range(3):
        exchange(1, at).wait_recv()
    own_units.wait()
    spread_parts((grad_gate, grad_up), gu_back, UNIT_TILE, True)
    for at in range(4, len(steps)):
        swap_on(at)
    for at in range(3):
        exchange(0, at).wait_recv()
    spread_parts((grad_query, grad_key, grad_value), back, PAIR, deep)
    if with_out:
        lines[1].finish(out_total)
        grad_out[...] = out_total[...]

    for at in range(3):
        exchange(0, at).wait_send()
        exchange(1, at).wait_send()
    for at in range(len(steps)):
        swap(at).wait_send()
    plane.finish()
    for line in lines:
        line.close()


def last_call(deep, depth, rows, width, plane_operands, gu_rows, qkv_parts, out_parts):
    whole = pl.BlockSpec(memory_space=pltpu.VMEM)
    with_out = out_parts is not None
    there = pl.BlockSpec(memory_space=pl.ANY)
    parts = [gu_rows, qkv_parts] + ([out_parts] if with_out else [])
    operands = hbm(plane_operands[0]) + list(plane_operands[1:]) + hbm(*parts)
    in_specs = [there] + [whole] * (len(plane_operands) - 1) + [there] * len(parts)
    part_rows, part_width = qkv_parts.shape[2] // 4, qkv_parts.shape[3]
    outs = [like((rows, width), FULL), like((2, width), FULL)]
    outs += [like((part_rows, 2 * gu_rows.shape[2]), LOW)] * 2
    outs += [like((part_rows, 4 * part_width // 3), FULL)] * 3
    scratch = plane_scratch(rows, width) + line_scratch(depth, qkv_parts.shape)
    scratch.append(pltpu.VMEM(qkv_parts.shape[2:], FULL))
    if with_out:
        outs.append(like(out_parts.shape[2:], FULL))
        scratch += line_scratch(depth, out_parts.shape)
        scratch.append(pltpu.VMEM(out_parts.shape[2:], FULL))
    swaps = 3 + (depth - 1).bit_length()
    scratch += [
        pltpu.VMEM((4, part_rows, part_width), LOW),
        pltpu.VMEM((4, part_rows, part_width), LOW),
        pltpu.VMEM(gu_rows.shape, LOW),
        pltpu.SemaphoreType.DMA((2, 3)),
        pltpu.SemaphoreType.DMA((2, 3)),
        pltpu.SemaphoreType.DMA((1,)),
        pltpu.VMEM((swaps, 2, width), FULL),
        pltpu.VMEM((swaps, 2, width), FULL),
        pltpu.SemaphoreType.DMA((swaps,)),
        pltpu.SemaphoreType.DMA((swaps,)),
    ]
    return pl.pallas_call(
        functools.partial(last_kernel, deep, with_out),
        out_shape=outs,
        in_specs=in_specs,
        out_specs=[whole] * len(outs),
        scratch_shapes=scratch,
        compiler_params=pltpu.CompilerParams(
            collective_id=3, has_side_effects=True, vmem_limit_bytes=50 * 1024 * 1024
        ),
        cost_estimate=pl.CostEstimate(
            flops=rows * width * 100, bytes_accessed=rows * width * 400, transcendentals=0
        ),
    )(*operands)


class LineGather:
    def __init__(self, core_first, full, sems):
        self.core_first, self.full = core_first, full
        self.right_send, self.right_recv, self.left_send, self.left_recv = sems[:4]
        self.core_send, self.core_recv = sems[4:]
        self.depth = full.shape[1 if core_first else 0]

    def copy(self, at, send, recv, device):
        core = lax.axis_index("c")
        place = self.full.at[(core, at) if self.core_first else (at, core)]
        return pltpu.make_async_remote_copy(
            src_ref=place,
            dst_ref=place,
            send_sem=send.at[at],
            recv_sem=recv.at[at],
            device_id=device,
            device_id_type=pl.DeviceIdType.MESH,
        )

    def right(self, at):
        return self.copy(at, self.right_send, self.right_recv, beside(1))

    def left(self, at):
        return self.copy(at, self.left_send, self.left_recv, beside(-1))

    def core(self, at):
        return self.copy(at, self.core_send, self.core_recv, peer("c"))

    def pass_on(self, number):
        index, last = lax.axis_index("z"), self.depth - 1
        for step, move in ((1, self.right), (-1, self.left)):
            at = index - number * step
            inside = (at >= 0) & (at <= last)

            @pl.when(inside)
            def _():
                if number:
                    move(at).wait_recv()

                @pl.when((index < last) if step == 1 else (index > 0))
                def _():
                    move(at).start()

                if number or step == 1:
                    self.core(at).start()

    def close(self):
        index, last = lax.axis_index("z"), self.depth - 1
        for at in range(self.depth):
            self.core(at).wait()

            @pl.when((index < last) & (at <= index))
            def _():
                self.right(at).wait_send()

            @pl.when((index > 0) & (at >= index))
            def _():
                self.left(at).wait_send()


def first_kernel(with_out, *refs):
    refs = list(refs)

    def take(count):
        taken, refs[:count] = refs[:count], []
        return taken

    weights, (tokens, gain_parts) = take(5), take(2)
    w_out = take(1)[0] if with_out else None
    full_qkv, gu_rows, spread, gains = take(4)
    full_out = take(1)[0] if with_out else None
    spread_send, spread_recv, gain_all, gain_send, gain_recv = take(5)
    swap_send, swap_recv, local, qkv_parts, gu_parts = take(5)
    held, held_sems = take(5), take(1)[0]
    lines = [LineGather(True, full_qkv, take(6))]
    if with_out:
        lines.insert(0, LineGather(False, full_out, take(6)))

    loads = [
        pltpu.make_async_copy(weight, kept, held_sems.at[at])
        for at, (weight, kept) in enumerate(zip(weights, held))
    ]
    for load in loads:
        load.start()
    depth = full_qkv.shape[1]
    at_z, at_x, at_c, at_y = (lax.axis_index(axis) for axis in AXES)
    mine = at_x * 2 + at_y
    steps = []
    step = 1
    while step < depth:
        steps.append(("z", step))
        step *= 2
    steps += [("c", 1), ("y", 1), ("x", 1)]
    index = ((at_x * 2 + at_y) * 2 + at_c) * depth + at_z
    far = [paired(axis, step) for axis, step in steps if step > 1]
    greet([peer("c"), peer("x"), peer("y"), peer("x", "y")] + far, line=True)

    def gather_parts(target, sources, tile, in_blocks):
        for part in range(4):
            for at in range(target.shape[2] // tile):
                source = sources[at % len(sources)]
                runs = part_columns(
                    source.shape[1], depth, in_blocks, part, at // len(sources) * tile, tile
                )
                pieces = [source[:, place : place + length] for _, place, length in runs]
                whole = pieces[0] if len(pieces) == 1 else jnp.concatenate(pieces, axis=1)
                target[part, :, at * tile : (at + 1) * tile] = whole

    for load in loads[:3]:
        load.wait()
    gather_parts(qkv_parts, held[:3], PAIR, with_out)
    members = [("y",), ("x",), ("x", "y")]
    part_rows = qkv_parts.shape[1]

    def exchange(kind, at):
        there = peer(*members[at])
        theirs = there.get("x", at_x) * 2 + there.get("y", at_y)
        source, target = (
            (qkv_parts, full_qkv.at[at_c, at_z, pl.ds(mine * part_rows, part_rows)]),
            (gu_parts, gu_rows.at[mine]),
        )[kind]
        return pltpu.make_async_remote_copy(
            src_ref=source.at[theirs],
            dst_ref=target,
            send_sem=swap_send.at[kind, at],
            recv_sem=swap_recv.at[kind, at],
            device_id=there,
            device_id_type=pl.DeviceIdType.MESH,
        )

    own_qkv = pltpu.make_async_copy(
        qkv_parts.at[mine],
        full_qkv.at[at_c, at_z, pl.ds(mine * part_rows, part_rows)],
        local.at[0],
    )
    own_gu = pltpu.make_async_copy(gu_parts.at[mine], gu_rows.at[mine], local.at[1])
    for at in (2, 0, 1):
        exchange(0, at).start()
    own_qkv.start()
    if with_out:
        own_out = pltpu.make_async_copy(w_out, full_out.at[at_z, at_c], local.at[2])
        own_out.start()

    def swap(at):
        axis, step = steps[at]
        count = 2**at
        place = gain_all.at[pl.ds((index // count) * count, count)]
        return pltpu.make_async_remote_copy(
            src_ref=place,
            dst_ref=place,
            send_sem=gain_send.at[at],
            recv_sem=gain_recv.at[at],
            device_id=paired(axis, step),
            device_id_type=pl.DeviceIdType.MESH,
        )

    gain_all[index] = gain_parts[0]
    for at in range(len(steps)):
        swap(at).start()
        if at == 1:
            for load in loads[3:]:
                load.wait()
            gather_parts(gu_parts, held[3:], UNIT_TILE, True)
            own_gu.start()
        swap(at).wait_recv()
        if steps[at][0] != "z" and steps[at - 1][0] == "z" and with_out:
            own_out.wait()
            lines[0].pass_on(0)
    for other in range(3):
        exchange(0, other).wait_recv()
    own_qkv.wait()
    lines[-1].pass_on(0)
    each = gain_parts.shape[2]
    for at in range(8 * depth):
        x, y, c, z = at // (4 * depth), at // (2 * depth) % 2, at // depth % 2, at % depth
        place = (((z * 2 + x) * 2 + c) * 2 + y) * each
        gains[:, place : place + each] = gain_all[at]

    plane = PlaneSum(None, tokens, None, None, None, spread_send, spread_recv, None, None, spread)
    gain = gains[0:1, :]
    for half, at in plane.pieces:
        values = tokens[plane.span(0, half, at), :].astype(FULL)
        plane.give(half, at, mix((values * factor_of(values) * gain).astype(LOW), depth))
    for at in range(3):
        exchange(1, at).start()

    todo = list(plane.pieces)
    share = -(-len(todo) // max(1, depth - 1))
    for number in range(1, depth):
        for line in lines:
            line.pass_on(number)
        for half, at in todo[(number - 1) * share : number * share]:
            plane.forward(half, at)
    for half, at in plane.pieces:
        plane.close_spread(half, at)
    own_gu.wait()
    for at in range(3):
        exchange(0, at).wait_send()
        exchange(1, at).wait()
    for at in range(len(steps)):
        swap(at).wait_send()
    for line in lines:
        line.close()


def first_call(depth, weights, tokens, gain_parts, w_out):
    rows, width = tokens.shape
    whole = pl.BlockSpec(memory_space=pltpu.VMEM)
    there = pl.BlockSpec(memory_space=pl.ANY)
    operands = hbm(*weights) + [tokens, gain_parts]
    in_specs = [there] * len(weights) + [whole, whole]
    part_rows, part_width, part_units = weights[0].shape[0], 3 * width // 4, weights[3].shape[1] // 2
    outs = [
        in_hbm((2, depth, 4 * part_rows, part_width), LOW),
        in_hbm((4, part_rows, part_units), LOW),
        in_hbm((4 * rows, width), LOW),
        like((2, width), FULL),
    ]
    out_specs = [there, there, whole, whole]
    swaps = 3 + (depth - 1).bit_length()
    scratch = [
        pltpu.SemaphoreType.DMA((6, 2, PIECES)),
        pltpu.SemaphoreType.DMA((6, 2, PIECES)),
        pltpu.VMEM((8 * depth, 2, width // (8 * depth)), FULL),
        pltpu.SemaphoreType.DMA((swaps,)),
        pltpu.SemaphoreType.DMA((swaps,)),
        pltpu.SemaphoreType.DMA((2, 3)),
        pltpu.SemaphoreType.DMA((2, 3)),
        pltpu.SemaphoreType.DMA((3,)),
        pltpu.VMEM((4, part_rows, part_width), LOW),
        pltpu.VMEM((4, part_rows, part_units), LOW),
    ]
    scratch += [pltpu.VMEM(weight.shape, LOW) for weight in weights]
    scratch.append(pltpu.SemaphoreType.DMA((len(weights),)))
    scratch += [pltpu.SemaphoreType.DMA((depth,))] * 6
    if w_out is not None:
        operands.append(w_out)
        in_specs.append(there)
        outs.append(in_hbm((depth, 2) + w_out.shape, LOW))
        out_specs.append(there)
        scratch += [pltpu.SemaphoreType.DMA((depth,))] * 6
    return pl.pallas_call(
        functools.partial(first_kernel, w_out is not None),
        out_shape=outs,
        in_specs=in_specs,
        out_specs=out_specs,
        scratch_shapes=scratch,
        compiler_params=pltpu.CompilerParams(
            collective_id=4, has_side_effects=True, vmem_limit_bytes=24 * 1024 * 1024
        ),
        cost_estimate=pl.CostEstimate(
            flops=rows * width * 100, bytes_accessed=rows * width * 200, transcendentals=0
        ),
    )(*operands)


def plane_scratch(rows, width):
    step = rows // (2 * PIECES)
    return [
        pltpu.VMEM((2, PIECES, 2, step, width), LOW),
        pltpu.VMEM((2, PIECES, step, width), LOW),
        pltpu.VMEM((2, PIECES, step, width), LOW),
        pltpu.SemaphoreType.DMA((6, 2, PIECES)),
        pltpu.SemaphoreType.DMA((6, 2, PIECES)),
        pltpu.VMEM((2, rows // 2, width), LOW),
        pltpu.SemaphoreType.DMA((2,)),
    ]


def plane_call(kernel, number, rows, width, outs, low, *operands):
    whole = pl.BlockSpec(memory_space=pltpu.VMEM)
    return pl.pallas_call(
        kernel,
        out_shape=outs,
        in_specs=[pl.BlockSpec(memory_space=pl.ANY)] + [whole] * len(operands),
        out_specs=[whole] * len(outs),
        scratch_shapes=plane_scratch(rows, width),
        compiler_params=pltpu.CompilerParams(
            collective_id=number, has_side_effects=True, vmem_limit_bytes=32 * 1024 * 1024
        ),
        cost_estimate=pl.CostEstimate(
            flops=rows * width * 100, bytes_accessed=rows * width * 200, transcendentals=0
        ),
    )(*hbm(low), *operands)


def body(
    tokens,
    cotangent,
    seq_lengths,
    assignment,
    w_query,
    w_key,
    w_value,
    w_out,
    w_gate,
    w_up,
    w_down,
    gain_attn,
    gain_mlp,
):
    rows, width = tokens.shape
    depth = lax.axis_size("z")
    at_z, at_x, at_c, at_y = (lax.axis_index(axis) for axis in AXES)
    mine = at_x * 2 + at_y
    whole_heads = w_out.shape[0] % HEAD_DIM == 0
    head_deep = depth if whole_heads else 0
    head_width = width // 4

    def in_order(weight, back=False):
        if blocks_align(width, depth):
            return weight
        order = (2, 0, 1, 3, 4) if back else (1, 2, 0, 3, 4)
        shape = (depth, 2, 2) if back else (2, depth, 2)
        apart = weight.reshape(shape + (-1, weight.shape[1]))
        return apart.transpose(order).reshape(weight.shape)

    def core_columns(values, core):
        if blocks_align(width, depth):
            return lax.dynamic_slice_in_dim(values, core * (width // 2), width // 2, axis=1)
        apart = values.reshape(values.shape[0], depth, 2, 2, -1)
        part = lax.dynamic_index_in_dim(apart, core, 3, keepdims=False)
        return part.reshape(values.shape[0], -1)

    slot_at = [(at_z * 2 + x) * 2 + at_c for x in (at_x, 1 - at_x)]
    slot_length = [seq_lengths[assignment[slot]] for slot in slot_at]
    row = jnp.arange(rows)
    valid_rows = (at_y * rows + row < slot_length[0]).astype(FULL)[:, None]

    full_qkv, gu_rows, normed_all, gains, *rest = first_call(
        depth,
        (w_query, w_key, w_value, w_gate, w_up),
        tokens,
        jnp.stack([gain_attn, gain_mlp])[None].astype(FULL),
        w_out if whole_heads else None,
    )
    full_qkv = in_order(full_qkv.reshape(width, -1))
    gain_one, gain_two = gains[0], gains[1]
    full_gu = lax.all_gather(
        gu_rows.reshape(-1, gu_rows.shape[2]), ("c", "z"), axis=0, tiled=True
    )
    full_gu = in_order(full_gu)
    if whole_heads:
        full_out = rest[0].reshape(-1, width)
    else:
        every = lax.all_gather(w_out, AXES, axis=0, tiled=True)
        full_out = lax.dynamic_slice_in_dim(every, mine * head_width, head_width, axis=0)
    w_down, normed_all = lax.optimization_barrier((w_down, normed_all))

    grad_out = cotangent.astype(FULL) * valid_rows
    grad_low = grad_out.astype(LOW)
    normed_all, grad_low = lax.optimization_barrier((normed_all, grad_low))
    near = plane_gather_near(grad_low)
    qkv = dot(normed_all, full_qkv)
    qkv, near = lax.optimization_barrier((qkv, near))
    far = plane_gather_far(grad_low, near)
    cosine, sine = rope_tables(jnp.arange(2 * rows))
    info = jnp.stack([at_y.astype(jnp.int32)] + slot_length)
    heads_out, lse, qkv = attend(info, qkv, cosine, sine)
    w_down, heads_out, far = lax.optimization_barrier((w_down, heads_out, far))
    grad_low_all = plane_gathered(grad_low, near, far)
    full_down = lax.all_gather(w_down, ("z", "c"), axis=0, tiled=True)
    branch_low, branch_own = project(heads_out[None], full_out, False)
    attended, normed2_all = plane_call(
        forward_kernel,
        1,
        rows,
        width,
        [like((rows, width), FULL), in_hbm((4 * rows, width), LOW)],
        branch_low,
        branch_own,
        tokens,
        gain_two[None],
    )
    both, active = activate(normed2_all, full_gu)

    down_part = dot_rows(active, grad_low_all).astype(LOW)
    grad_w_down = lax.psum_scatter(down_part, ("z", "c"), scatter_dimension=0, tiled=True)
    grad_w_down = grad_w_down.astype(FULL)
    down_part, grad_low_all = lax.optimization_barrier((down_part, grad_low_all))
    grad_gu = activate_back(grad_low_all, full_down, both)
    theirs = dot_rows(core_columns(normed2_all, 1 - at_c), grad_gu).astype(LOW)
    from_core = swap_c(theirs)
    theirs, grad_gu = lax.optimization_barrier((theirs, grad_gu))
    back_low, back_own = project(grad_gu[None], full_gu, True)
    back_low, from_core, grad_gu = lax.optimization_barrier((back_low, from_core, grad_gu))
    ours = dot_rows(core_columns(normed2_all, at_c), grad_gu) + from_core.astype(FULL)
    grad_gu_rows = lax.psum_scatter(ours.astype(LOW), "z", scatter_dimension=0, tiled=True)
    ours, back_low = lax.optimization_barrier((ours, back_low))
    grad_attended, grad_gain_mlp, grad_branch = plane_call(
        backward_kernel,
        2,
        rows,
        width,
        [like((rows, width), FULL), like((1, width), FULL), in_hbm((4 * rows, width), LOW)],
        back_low,
        back_own,
        attended,
        gain_two[None],
        grad_out,
    )
    grad_branch, active = lax.optimization_barrier((grad_branch, active))

    grad_w_out = dot_rows(heads_out, grad_branch)
    out_parts = None
    if whole_heads:
        out_parts = grad_w_out.astype(LOW).reshape(depth, 2, -1, width)
    else:
        spread = lax.dynamic_update_slice_in_dim(
            jnp.zeros((width, width), FULL), grad_w_out, mine * head_width, axis=0
        )
        grad_w_out = lax.psum_scatter(spread, AXES, scatter_dimension=0, tiled=True)
    grad_mixed = dot_through(grad_branch, full_out).astype(LOW)
    last_low, last_own = project(active[None], full_down, False)
    last_low, grad_mixed = lax.optimization_barrier((last_low, grad_mixed))
    near = plane_reduce_near(last_low)
    grad_qkv = attend_back(info, qkv, grad_mixed, lse, cosine, sine)
    grad_qkv, near, grad_w_down = lax.optimization_barrier((grad_qkv, near, grad_w_down))
    far = plane_reduce_far(last_low, near)
    grad_qkv_part = in_order(dot_rows(normed_all, grad_qkv).astype(LOW), True)
    back_low, back_own = project(grad_qkv[None], full_qkv, True)
    back_low, far = lax.optimization_barrier((back_low, far))
    result = attended + plane_reduced(last_own, near, far)
    output = (result * valid_rows).astype(LOW)
    grad_input, grad_gains, *last_weights = last_call(
        head_deep,
        depth,
        rows,
        width,
        [
            back_low,
            back_own,
            tokens,
            gain_one[None],
            grad_gain_mlp,
        ],
        grad_gu_rows.reshape(4, -1, grad_gu_rows.shape[1]),
        grad_qkv_part.reshape(2, depth, -1, grad_qkv_part.shape[1]),
        out_parts,
    )
    grad_w_gate, grad_w_up, grad_w_query, grad_w_key, grad_w_value = last_weights[:5]
    grad_w_gate, grad_w_up = grad_w_gate.astype(FULL), grad_w_up.astype(FULL)
    grad_input = grad_input + grad_attended
    if whole_heads:
        grad_w_out = last_weights[5]
    index = ((at_z * 2 + at_x) * 2 + at_c) * 2 + at_y
    part = width // (8 * depth)
    grad_gains = lax.dynamic_slice_in_dim(grad_gains, index * part, part, axis=1)
    return (
        output,
        grad_input,
        grad_w_query,
        grad_w_key,
        grad_w_value,
        grad_w_out,
        grad_w_gate,
        grad_w_up,
        grad_w_down,
        grad_gains[0],
        grad_gains[1],
    )


def solution(mesh):
    shape = (mesh.shape["dp"] // 4, 2, 2, mesh.shape["seq"])
    grid = Mesh(mesh.devices.reshape(shape), AXES)
    split = P(AXES, None)
    part = P(AXES)
    return jax.shard_map(
        body,
        mesh=grid,
        in_specs=(split, split, P(), P()) + (split,) * 7 + (part, part),
        out_specs=(split,) * 9 + (part, part),
        check_vma=False,
    )
```

```python
import functools

import jax
import jax.experimental.pallas as pl
import jax.experimental.pallas.tpu as pltpu
import jax.numpy as jnp
from jax import lax
from jax.sharding import Mesh, PartitionSpec as P

HEAD_DIM = 64
PAIR = 2 * HEAD_DIM
norm_eps = 1e-05
rope_base = 130000.0
AXES = ("z", "x", "c", "y")
LOW = jnp.bfloat16
FULL = jnp.float32
like = jax.ShapeDtypeStruct
in_hbm = pltpu.HBM


def hbm(*values):
    return [pltpu.with_memory_space_constraint(value, pltpu.HBM) for value in values]


def swap_x(value):
    return lax.ppermute(value, "x", [(0, 1), (1, 0)])


def swap_y(value):
    return lax.ppermute(value, "y", [(0, 1), (1, 0)])


def swap_c(value):
    return lax.ppermute(value, "c", [(0, 1), (1, 0)])


def plane_gather_near(value):
    half = value.shape[0] // 2
    return swap_y(value[:half]), swap_x(value[half:])


def plane_gather_far(value, near):
    half = value.shape[0] // 2
    return (
        swap_x(jnp.concatenate([value[:half], near[0]], axis=0)),
        swap_y(jnp.concatenate([value[half:], near[1]], axis=0)),
    )


def plane_gathered(value, near, far):
    half = value.shape[0] // 2
    top, low = far
    return jnp.concatenate(
        [value, near[0], low[:half], top[:half], near[1], top[half:], low[half:]], axis=0
    )


def plane_blocks(value):
    count = value.shape[0] // 4
    return [value[at * count : (at + 1) * count] for at in range(4)]


def plane_reduce_near(value):
    _, by_y, by_x, by_d = plane_blocks(value)
    half = by_y.shape[0] // 2
    return (
        swap_x(jnp.concatenate([by_x[:half], by_d[:half]], axis=0)),
        swap_y(jnp.concatenate([by_y[half:], by_d[half:]], axis=0)),
    )


def plane_reduce_far(value, near):
    _, by_y, by_x, _ = plane_blocks(value)
    half = by_y.shape[0] // 2
    return (
        swap_y((by_y[:half].astype(FULL) + near[0][half:].astype(FULL)).astype(LOW)),
        swap_x((by_x[half:].astype(FULL) + near[1][half:].astype(FULL)).astype(LOW)),
    )


def plane_reduced(own, near, far):
    half = own.shape[0] // 2
    return own + jnp.concatenate(
        [
            near[0][:half].astype(FULL) + far[0].astype(FULL),
            near[1][:half].astype(FULL) + far[1].astype(FULL),
        ],
        axis=0,
    )


def part_place(depth, part, block):
    return ((block // 2 * 2 + part // 2) * 2 + block % 2) * 2 + part % 2


def part_columns(width, depth, in_blocks, part, start, count):
    if not in_blocks:
        return [(0, part * (width // 4) + start, count)]
    each = width // (8 * depth)
    length = min(each, count)
    return [
        (
            at,
            part_place(depth, part, (start + at) // each) * each + (start + at) % each,
            length,
        )
        for at in range(0, count, length)
    ]


def factor_of(values):
    return lax.rsqrt(jnp.mean(values * values, axis=-1, keepdims=True) + norm_eps)


def rope_tables(positions):
    halves = HEAD_DIM // 2
    frequency = rope_base ** (-(jnp.arange(halves).astype(FULL) * 2.0 / HEAD_DIM))
    angles = positions.astype(FULL)[:, None] * frequency[None, :]
    cosine = jnp.cos(angles)
    sine = jnp.sin(angles)
    return (
        jnp.concatenate([cosine] * 4, axis=1),
        jnp.concatenate([-sine, sine, -sine, sine], axis=1),
    )


def turned(values, low_half):
    lanes = values.shape[1]
    halves = HEAD_DIM // 2
    return jnp.where(
        low_half, pltpu.roll(values, lanes - halves, 1), pltpu.roll(values, halves, 1)
    )


def lane_masks(rows):
    lane = lax.broadcasted_iota(jnp.int32, (rows, PAIR), 1)
    return lane % HEAD_DIM < HEAD_DIM // 2, lane < HEAD_DIM


def diagonal_mask(first, length, rows):
    query = lax.broadcasted_iota(jnp.int32, (rows, rows), 0)
    key = lax.broadcasted_iota(jnp.int32, (rows, rows), 1)
    return (key <= query) & (key + first < length)


def attend_kernel(info, qkv_ref, c_ref, s_ref, mixed, lse, qkv_out):
    rows = qkv_ref.shape[0] // 2
    length = info[1 + pl.program_id(0)]
    scale = HEAD_DIM ** (-0.5)
    low_half, first_head = lane_masks(rows)
    place = [pl.multiple_of(jnp.where(info[0] == at, 0, rows), rows) for at in range(2)]
    queries, keys, values = [], [], []
    for at in range(2):
        span = pl.ds(place[at], rows)
        table = pl.ds(at * rows, rows)
        for number, kept in enumerate((queries, keys, values)):
            lanes = slice(number * PAIR, (number + 1) * PAIR)
            item = qkv_ref[span, lanes]
            if number < 2:
                item = item * c_ref[table, :] + turned(item, low_half) * s_ref[table, :]
            item = item.astype(LOW)
            qkv_out[span, lanes] = item
            kept.append(item)
    for at in range(2):
        allowed = diagonal_mask(at * rows, length, rows)
        found, logs = [], []
        for head in range(2):
            only = first_head if head == 0 else jnp.logical_not(first_head)
            query = jnp.where(only, queries[at], jnp.zeros_like(queries[at]))
            scores = []
            for block in range(at + 1):
                score = dot_through(query, keys[block]) * scale
                scores.append(jnp.where(allowed, score, -1e30) if block == at else score)
            top = jnp.max(scores[0], axis=1, keepdims=True)
            for score in scores[1:]:
                top = jnp.maximum(top, jnp.max(score, axis=1, keepdims=True))
            weights = [jnp.exp(score - top) for score in scores]
            total = jnp.sum(weights[0], axis=1, keepdims=True)
            for weight in weights[1:]:
                total = total + jnp.sum(weight, axis=1, keepdims=True)
            share = 1.0 / total
            out = dot((weights[0] * share).astype(LOW), values[0])
            for block in range(1, at + 1):
                out = out + dot((weights[block] * share).astype(LOW), values[block])
            found.append(out)
            logs.append(top + jnp.log(total))
        span = pl.ds(place[at], rows)
        mixed[span, :] = jnp.where(first_head, found[0], found[1]).astype(LOW)
        lse[span, :] = jnp.where(first_head, logs[0], logs[1])


def attend_back_kernel(info, qkv_ref, g_ref, lse_ref, c_ref, s_ref, grads_out):
    rows = qkv_ref.shape[0] // 2
    length = info[1 + pl.program_id(0)]
    scale = HEAD_DIM ** (-0.5)
    low_half, first_head = lane_masks(rows)
    place = [pl.multiple_of(jnp.where(info[0] == at, 0, rows), rows) for at in range(2)]
    spans = [pl.ds(start, rows) for start in place]
    keys = [qkv_ref[span, PAIR : 2 * PAIR] for span in spans]
    values = [qkv_ref[span, 2 * PAIR :] for span in spans]
    key_sums = [[None, None], [None, None]]
    value_sums = [[None, None], [None, None]]

    def unrotated(item, at):
        table = pl.ds(at * rows, rows)
        scaled = item * s_ref[table, :]
        return (item * c_ref[table, :] + turned(scaled, low_half)).astype(LOW)

    def added(old, new):
        return new if old is None else old + new

    for at in range(2):
        allowed = diagonal_mask(at * rows, length, rows)
        query_all, grad_all, logs = qkv_ref[spans[at], :PAIR], g_ref[spans[at], :], lse_ref[spans[at], :]
        found = []
        for head in range(2):
            only = first_head if head == 0 else jnp.logical_not(first_head)
            query = jnp.where(only, query_all, jnp.zeros_like(query_all))
            grad = jnp.where(only, grad_all, jnp.zeros_like(grad_all))
            log = logs[:, head * HEAD_DIM : head * HEAD_DIM + 1]
            probs, grads = [], []
            inner = jnp.zeros((rows, 1), FULL)
            for block in range(at + 1):
                prob = jnp.exp(dot_through(query, keys[block]) * scale - log)
                if block == at:
                    prob = jnp.where(allowed, prob, 0.0)
                grad_prob = dot_through(grad, values[block])
                inner = inner + jnp.sum(prob * grad_prob, axis=1, keepdims=True)
                probs.append(prob)
                grads.append(grad_prob)
            out = None
            for block in range(at + 1):
                grad_score = (probs[block] * (grads[block] - inner)).astype(LOW)
                out = added(out, dot(grad_score, keys[block]))
                key_sums[block][head] = added(key_sums[block][head], dot_rows(grad_score, query_all))
                value_sums[block][head] = added(
                    value_sums[block][head], dot_rows(probs[block].astype(LOW), grad_all)
                )
            found.append(out)
        grads_out[spans[at], :PAIR] = unrotated(jnp.where(first_head, found[0], found[1]) * scale, at)
    for at in range(2):
        both = jnp.where(first_head, key_sums[at][0], key_sums[at][1]) * scale
        grads_out[spans[at], PAIR : 2 * PAIR] = unrotated(both, at)
        both = jnp.where(first_head, value_sums[at][0], value_sums[at][1])
        grads_out[spans[at], 2 * PAIR :] = both.astype(LOW)


def attend(info, qkv, cosine, sine):
    total, width = qkv.shape[0], qkv.shape[1] // 3
    slot_rows, pairs = total // 2, width // PAIR
    part = pl.BlockSpec((slot_rows, PAIR), lambda slot, pair, info: (slot, pair))
    three = pl.BlockSpec((slot_rows, 3 * PAIR), lambda slot, pair, info: (slot, pair))
    table = pl.BlockSpec((slot_rows, PAIR), lambda slot, pair, info: (0, 0))
    return pl.pallas_call(
        attend_kernel,
        grid_spec=pltpu.PrefetchScalarGridSpec(
            num_scalar_prefetch=1,
            grid=(2, pairs),
            in_specs=[three, table, table],
            out_specs=[part, part, three],
        ),
        out_shape=[
            in_hbm((total, width), LOW),
            in_hbm((total, width), FULL),
            in_hbm((total, 3 * width), LOW),
        ],
        compiler_params=pltpu.CompilerParams(vmem_limit_bytes=16 * 1024 * 1024),
        cost_estimate=pl.CostEstimate(
            flops=16 * total * slot_rows * width,
            bytes_accessed=total * width * 24,
            transcendentals=total * slot_rows * width // HEAD_DIM,
        ),
    )(info, qkv, cosine, sine)


def attend_back(info, qkv, grads, lse, cosine, sine):
    total, width = grads.shape
    slot_rows, pairs = total // 2, width // PAIR
    part = pl.BlockSpec((slot_rows, PAIR), lambda slot, pair, info: (slot, pair))
    three = pl.BlockSpec((slot_rows, 3 * PAIR), lambda slot, pair, info: (slot, pair))
    table = pl.BlockSpec((slot_rows, PAIR), lambda slot, pair, info: (0, 0))
    return pl.pallas_call(
        attend_back_kernel,
        grid_spec=pltpu.PrefetchScalarGridSpec(
            num_scalar_prefetch=1,
            grid=(2, pairs),
            in_specs=[three, part, part, table, table],
            out_specs=three,
        ),
        out_shape=in_hbm((total, 3 * width), LOW),
        compiler_params=pltpu.CompilerParams(vmem_limit_bytes=16 * 1024 * 1024),
        cost_estimate=pl.CostEstimate(
            flops=40 * total * slot_rows * width,
            bytes_accessed=total * width * 18,
            transcendentals=total * slot_rows * width // HEAD_DIM,
        ),
    )(info, *hbm(qkv, grads, lse), cosine, sine)


def dot(left, right):
    return jnp.dot(left, right, preferred_element_type=FULL)


def dot_rows(left, right):
    return lax.dot_general(left, right, (((0,), (0,)), ((), ())), preferred_element_type=FULL)


def dot_through(left, right):
    return lax.dot_general(left, right, (((1,), (1,)), ((), ())), preferred_element_type=FULL)


UNIT_TILE = 256
QKV_RUNS = 2


def activate_kernel(normed, weight, both_ref, active_ref):
    both = dot(normed[...], weight[...])
    both_ref[...] = both
    gate, upper = both[:, :UNIT_TILE], both[:, UNIT_TILE:]
    active_ref[...] = (gate * jax.nn.sigmoid(gate) * upper).astype(LOW)


def activate(normed, weight):
    rows, width = normed.shape
    units = weight.shape[1] // 2
    return pl.pallas_call(
        activate_kernel,
        grid=(units // UNIT_TILE,),
        in_specs=[
            pl.BlockSpec((rows, width), lambda at: (0, 0)),
            pl.BlockSpec((width, 2 * UNIT_TILE), lambda at: (0, at)),
        ],
        out_specs=[
            pl.BlockSpec((rows, 2 * UNIT_TILE), lambda at: (0, at)),
            pl.BlockSpec((rows, UNIT_TILE), lambda at: (0, at)),
        ],
        out_shape=[in_hbm((rows, 2 * units), FULL), in_hbm((rows, units), LOW)],
        compiler_params=pltpu.CompilerParams(vmem_limit_bytes=40 * 1024 * 1024),
        cost_estimate=pl.CostEstimate(
            flops=4 * rows * units * width,
            bytes_accessed=rows * units * 10 + units * width * 4,
            transcendentals=rows * units,
        ),
    )(*hbm(normed, weight))


def activate_back_kernel(grad_low, weight, both_ref, out):
    grads = dot_through(grad_low[...], weight[...])
    gate, upper = both_ref[:, :UNIT_TILE], both_ref[:, UNIT_TILE:]
    sigmoid = jax.nn.sigmoid(gate)
    out[:, :UNIT_TILE] = (grads * upper * sigmoid * (1.0 + gate * (1.0 - sigmoid))).astype(LOW)
    out[:, UNIT_TILE:] = (grads * gate * sigmoid).astype(LOW)


def activate_back(grad_low, weight, both):
    rows, units = both.shape[0], both.shape[1] // 2
    width = grad_low.shape[1]
    part = pl.BlockSpec((rows, 2 * UNIT_TILE), lambda at: (0, at))
    return pl.pallas_call(
        activate_back_kernel,
        grid=(units // UNIT_TILE,),
        in_specs=[
            pl.BlockSpec((rows, width), lambda at: (0, 0)),
            pl.BlockSpec((UNIT_TILE, width), lambda at: (at, 0)),
            part,
        ],
        out_specs=part,
        out_shape=in_hbm((rows, 2 * units), LOW),
        compiler_params=pltpu.CompilerParams(vmem_limit_bytes=40 * 1024 * 1024),
        cost_estimate=pl.CostEstimate(
            flops=2 * rows * units * width,
            bytes_accessed=rows * units * 12 + units * width * 2,
            transcendentals=rows * units,
        ),
    )(*hbm(grad_low, weight, both))


def project_kernel(through, left, weight, low, own):
    groups, total, depth = left.shape
    if through:
        found = dot_through(left[0], weight[:, :depth])
        for group in range(1, groups):
            found = found + dot_through(
                left[group], weight[:, group * depth : (group + 1) * depth]
            )
    else:
        found = dot(left[0], weight[...])
    low[...] = found.astype(LOW)
    own[...] = found[: own.shape[0], :]


def project(left, weight, through):
    groups, total, depth = left.shape
    width = weight.shape[0] if through else weight.shape[1]
    tile = 256
    block = (tile, groups * depth) if through else (depth, tile)
    return pl.pallas_call(
        functools.partial(project_kernel, through),
        grid=(width // tile,),
        in_specs=[
            pl.BlockSpec((groups, total, depth), lambda at: (0, 0, 0)),
            pl.BlockSpec(block, (lambda at: (at, 0)) if through else (lambda at: (0, at))),
        ],
        out_specs=[
            pl.BlockSpec((total, tile), lambda at: (0, at)),
            pl.BlockSpec((total // 4, tile), lambda at: (0, at)),
        ],
        out_shape=[in_hbm((total, width), LOW), in_hbm((total // 4, width), FULL)],
        compiler_params=pltpu.CompilerParams(vmem_limit_bytes=40 * 1024 * 1024),
        cost_estimate=pl.CostEstimate(
            flops=2 * groups * total * depth * width,
            bytes_accessed=2 * groups * depth * (total + width) + 3 * total * width,
            transcendentals=0,
        ),
    )(*hbm(left, weight))


AXIS_BLOCK = {"y": 1, "x": 2}
PIECES = 4
FIRST, SECOND = ("x", "y"), ("y", "x")


def peer(*axes):
    return {axis: 1 - lax.axis_index(axis) for axis in axes}


def paired(axis, step):
    index = lax.axis_index(axis)
    return {axis: index + step * (1 - 2 * ((index // step) % 2))}


def beside(step):
    count = lax.axis_size("z")
    return {"z": (lax.axis_index("z") + step + count) % count}


def signal(barrier, device):
    pl.semaphore_signal(barrier, inc=1, device_id=device, device_id_type=pl.DeviceIdType.MESH)


def greet(devices, line=False):
    barrier = pltpu.get_barrier_semaphore()
    count = len(devices)
    for device in devices:
        signal(barrier, device)
    if line:
        index, last = lax.axis_index("z"), lax.axis_size("z") - 1
        for step, there in ((1, index < last), (-1, index > 0)):

            @pl.when(there)
            def _():
                signal(barrier, beside(step))

            count = count + there.astype(jnp.int32)
    pl.semaphore_wait(barrier, count)


class PlaneSum:
    def __init__(
        self, low, own, first_in, second_out, second_in, send, recv, between, local, spread=None
    ):
        self.low, self.own, self.spread = low, own, spread
        self.first_in, self.second_out, self.second_in = first_in, second_out, second_in
        self.send, self.recv = send, recv
        self.between, self.local = between, local
        self.rows = own.shape[0]
        self.step = self.rows // (2 * PIECES)
        self.pieces = [(half, at) for at in range(PIECES) for half in range(2)]

    def span(self, block, half, at):
        return pl.ds(block * self.rows + (half * PIECES + at) * self.step, self.step)

    def copy(self, kind, half, at, source, target, axis):
        return pltpu.make_async_remote_copy(
            src_ref=source,
            dst_ref=target,
            send_sem=self.send.at[kind, half, at],
            recv_sem=self.recv.at[kind, half, at],
            device_id=peer(axis),
            device_id_type=pl.DeviceIdType.MESH,
        )

    def first(self, kind, half, at):
        block = (AXIS_BLOCK[FIRST[half]], 3)[kind]
        return self.copy(
            kind,
            half,
            at,
            self.low.at[self.span(block, half, at)],
            self.first_in.at[half, at, kind],
            FIRST[half],
        )

    def second(self, half, at):
        return self.copy(
            2, half, at, self.second_out.at[half, at], self.second_in.at[half, at], SECOND[half]
        )

    def spreading(self, axis, half, at):
        return self.copy(
            2 + AXIS_BLOCK[axis],
            half,
            at,
            self.spread.at[self.span(0, half, at)],
            self.spread.at[self.span(AXIS_BLOCK[axis], half, at)],
            axis,
        )

    def forwarding(self, half, at):
        block = AXIS_BLOCK[SECOND[half]]
        return self.copy(
            5,
            half,
            at,
            self.spread.at[self.span(block, half, at)],
            self.spread.at[self.span(3, half, at)],
            FIRST[half],
        )

    def load(self, half):
        count = self.rows // 2
        place = pl.ds(AXIS_BLOCK[SECOND[half]] * self.rows + half * count, count)
        return pltpu.make_async_copy(self.low.at[place], self.between.at[half], self.local.at[half])

    def start(self):
        for half, at in self.pieces:
            self.first(0, half, at).start()
            self.first(1, half, at).start()
        for half in range(2):
            self.load(half).start()

    def middle(self, half, at):
        if at == 0:
            self.load(half).wait()
        self.first(0, half, at).wait_recv()
        self.first(1, half, at).wait_recv()
        total = self.between[half, at * self.step : (at + 1) * self.step, :].astype(FULL)
        total = total + self.first_in[half, at, 1].astype(FULL)
        self.second_out[half, at] = total.astype(LOW)
        self.second(half, at).start()

    def total(self, half, at):
        self.second(half, at).wait_recv()
        total = self.own[self.span(0, half, at), :] + self.first_in[half, at, 0].astype(FULL)
        return total + self.second_in[half, at].astype(FULL)

    def give(self, half, at, rows):
        self.spread[self.span(0, half, at), :] = rows
        self.spreading("x", half, at).start()
        self.spreading("y", half, at).start()

    def forward(self, half, at):
        self.spreading(SECOND[half], half, at).wait_recv()
        self.forwarding(half, at).start()

    def finish(self):
        for half, at in self.pieces:
            self.first(0, half, at).wait_send()
            self.first(1, half, at).wait_send()
            self.second(half, at).wait_send()
            if self.spread is not None:
                self.close_spread(half, at)

    def close_spread(self, half, at):
        self.spreading("x", half, at).wait_send()
        self.spreading("y", half, at).wait_send()
        self.spreading(FIRST[half], half, at).wait_recv()
        self.forwarding(half, at).wait()

    def run(self, each, ready):
        count = len(self.pieces)
        self.start()
        ready()
        for turn in range(count + 3):
            if turn < count:
                self.middle(*self.pieces[turn])
            if 1 <= turn <= count:
                half, at = self.pieces[turn - 1]
                self.give(half, at, each(self.span(0, half, at), self.total(half, at)))
            if turn >= 3:
                self.forward(*self.pieces[turn - 3])
        self.finish()


def start_loads(sources, scratch):
    count = len(sources)
    rest, held, sems = scratch[: -count - 1], scratch[-count - 1 : -1], scratch[-1]
    loads = [
        pltpu.make_async_copy(source, kept, sems.at[at])
        for at, (source, kept) in enumerate(zip(sources, held))
    ]
    for load in loads:
        load.start()

    def ready():
        for load in loads:
            load.wait()

    return rest, held, ready


def forward_kernel(low, own, tokens, gain, attended, spread, *scratch):
    scratch, (own, tokens), ready = start_loads((own, tokens), scratch)
    greet([peer("x"), peer("y")])
    plane = PlaneSum(low, own, *scratch, spread)

    def each(span, total):
        values = tokens[span, :].astype(FULL) + total
        attended[span, :] = values
        return mix((values * factor_of(values) * gain[...]).astype(LOW), lax.axis_size("z"))

    plane.run(each, ready)


def norm_back(values, gain, grads):
    factor = factor_of(values)
    weighted = grads * gain
    inner = jnp.mean(weighted * values, axis=-1, keepdims=True)
    grad_gain = jnp.sum(grads * values * factor, axis=0, keepdims=True)
    return factor * weighted - values * (factor * factor * factor) * inner, grad_gain


def backward_kernel(
    low, own, attended, grad_out, gain, grad_attended, grad_gain, spread, *scratch
):
    scratch, (own, attended, grad_out), ready = start_loads((own, attended, grad_out), scratch)
    greet([peer("x"), peer("y")])
    plane = PlaneSum(low, own, *scratch, spread)
    grad_gain[...] = jnp.zeros_like(grad_gain)

    def each(span, total):
        grads, for_gain = norm_back(
            attended[span, :], gain[...], mix(total, lax.axis_size("z"), True)
        )
        grads = grads + grad_out[span, :]
        grad_attended[span, :] = grads
        grad_gain[...] += for_gain
        return grads.astype(LOW)

    plane.run(each, ready)


def blocks_align(width, depth):
    return (width // (4 * depth)) % 128 == 0


def mix(values, depth, back=False):
    if not blocks_align(values.shape[1], depth):
        return values
    block = values.shape[1] // (4 * depth)
    order = [(z * 2 + x) * 2 + c for c in range(2) for z in range(depth) for x in range(2)]
    if back:
        order = sorted(range(4 * depth), key=order.__getitem__)
    return jnp.concatenate([values[:, at * block : (at + 1) * block] for at in order], axis=1)


class LineSum:
    def __init__(self, core_first, parts, sums, line_in, last_in, ours, sems):
        self.core_first, self.parts, self.ours = core_first, parts, ours
        self.sums, self.line_in, self.last_in = sums, line_in, last_in
        self.core_send, self.core_recv, self.send, self.right_recv, self.left_recv = sems[:5]
        self.local = sems[5]
        self.depth = sums.shape[0]

    def place(self, at, core):
        return (core, at) if self.core_first else (at, core)

    def core(self, at):
        return pltpu.make_async_remote_copy(
            src_ref=self.parts.at[self.place(at, 1 - lax.axis_index("c"))],
            dst_ref=self.sums.at[at],
            send_sem=self.core_send.at[at],
            recv_sem=self.core_recv.at[at],
            device_id=peer("c"),
            device_id_type=pl.DeviceIdType.MESH,
        )

    def line(self, at, step, last=False):
        sems = self.right_recv if step == 1 else self.left_recv
        return pltpu.make_async_remote_copy(
            src_ref=self.sums.at[at],
            dst_ref=self.last_in if last else self.line_in.at[at],
            send_sem=self.send.at[at],
            recv_sem=sems.at[at],
            device_id=beside(step),
            device_id_type=pl.DeviceIdType.MESH,
        )

    def start(self):
        ends_first = sorted(range(self.depth), key=lambda at: min(at, self.depth - 1 - at))
        for at in ends_first:
            self.core(at).start()
            self.load(at).start()

    def load(self, at):
        place = self.parts.at[self.place(at, lax.axis_index("c"))]
        return pltpu.make_async_copy(place, self.ours.at[at], self.local.at[at])

    def both_cores(self, at):
        self.load(at).wait()
        self.core(at).wait_recv()
        return self.ours[at].astype(FULL) + self.sums[at].astype(FULL)

    def pass_on(self, at, step, first):
        total = self.both_cores(at)
        if not first:
            self.line(at, step).wait_recv()
            total = total + self.line_in[at].astype(FULL)
        self.sums[at] = total.astype(LOW)
        if step == 1:
            self.line(at, 1).start()
            return
        ends = at == lax.axis_index("z") - 1

        @pl.when(ends)
        def _():
            self.line(at, -1, True).start()

        @pl.when(jnp.logical_not(ends))
        def _():
            self.line(at, -1).start()

    def from_ends(self):
        index, last = lax.axis_index("z"), self.depth - 1
        for number in range(last):

            @pl.when(index == 0)
            def _():
                self.pass_on(last - number, 1, True)

            @pl.when(index == last)
            def _():
                self.pass_on(number, -1, True)

    def turn(self, time):
        index, last = lax.axis_index("z"), self.depth - 1

        @pl.when((index > 0) & (index <= time))
        def _():
            self.pass_on(index + last - time, 1, False)

        @pl.when((index < last) & (last - index <= time))
        def _():
            self.pass_on(time - (last - index), -1, False)

    def finish(self, total):
        index, last = lax.axis_index("z"), self.depth - 1
        total[...] = self.both_cores(index)

        @pl.when(index > 0)
        def _():
            self.line(index, 1).wait_recv()
            total[...] += self.line_in[index].astype(FULL)

        @pl.when(index < last)
        def _():
            self.line(index, -1, True).wait_recv()
            total[...] += self.last_in[...].astype(FULL)

    def close(self):
        index = lax.axis_index("z")
        for at in range(self.depth):
            self.core(at).wait_send()

            @pl.when(index < at)
            def _():
                self.line(at, 1).wait_send()

            @pl.when(index > at)
            def _():
                self.line(at, -1).wait_send()


def line_scratch(depth, shape):
    rows, columns = shape[2:]
    sems = [pltpu.SemaphoreType.DMA((depth,))] * 6
    buffers = [pltpu.VMEM((depth, rows, columns), LOW)] * 2
    buffers += [pltpu.VMEM((rows, columns), LOW), pltpu.VMEM((depth, rows, columns), LOW)]
    return buffers + sems


def last_kernel(deep, with_out, *refs):
    refs = list(refs)

    def take(count):
        taken, refs[:count] = refs[:count], []
        return taken

    low, own, tokens, gain, grad_gain_mlp, gu_rows, qkv_parts = take(7)
    out_parts = take(1)[0] if with_out else None
    grad_input, gains, grad_gate, grad_up, grad_query, grad_key, grad_value = take(7)
    grad_out = take(1)[0] if with_out else None
    plane_refs = take(7)
    qkv_refs, (qkv_total,) = take(10), take(1)
    if with_out:
        out_refs, (out_total,) = take(10), take(1)
    sent, back, gu_back, back_send, back_recv, own_local = take(6)
    gain_in, gain_out, gain_send, gain_recv = take(4)

    depth = qkv_parts.shape[1]
    steps = [("c", 1), ("x", 1), ("y", 1)]
    step = 1
    while step < depth:
        steps.append(("z", step))
        step *= 2
    far = [paired(axis, step) for axis, step in steps if step > 1]
    greet([peer("c"), peer("x"), peer("y"), peer("x", "y")] + far, line=True)

    plane = PlaneSum(low, own, *plane_refs)
    lines = [LineSum(True, qkv_parts, *qkv_refs[:4], qkv_refs[4:])]
    if with_out:
        lines.append(LineSum(False, out_parts, *out_refs[:4], out_refs[4:]))
    mine = lax.axis_index("x") * 2 + lax.axis_index("y")
    members = [("y",), ("x",), ("x", "y")]

    def exchange(kind, at):
        there = peer(*members[at])
        theirs = there.get("x", lax.axis_index("x")) * 2 + there.get("y", lax.axis_index("y"))
        source, target = sent.at[theirs], back.at[mine]
        if kind:
            span = pl.ds((kind - 1) * 16, 16)
            source, target = gu_rows.at[theirs, span], gu_back.at[mine, span]
        return pltpu.make_async_remote_copy(
            src_ref=source,
            dst_ref=target,
            send_sem=back_send.at[kind, at],
            recv_sem=back_recv.at[kind, at],
            device_id=there,
            device_id_type=pl.DeviceIdType.MESH,
        )

    kinds = 1 + gu_rows.shape[1] // 16

    def send_units(first, last):
        for kind in range(1 + (kinds - 1) * first // 4, 1 + (kinds - 1) * last // 4):
            for at in range(3):
                exchange(kind, at).start()

    def spread_parts(targets, source, tile, in_blocks):
        for part in range(4):
            for at in range(source.shape[2] // tile):
                target = targets[at % len(targets)]
                columns = source[part, :, at * tile : (at + 1) * tile].astype(target.dtype)
                runs = part_columns(
                    target.shape[1], depth, in_blocks, part, at // len(targets) * tile, tile
                )
                for own, place, length in runs:
                    target[:, place : place + length] = columns[:, own : own + length]

    lines[0].start()
    lines[0].from_ends()
    plane.start()
    for line in lines[1:]:
        line.start()
        line.from_ends()
    own_units = pltpu.make_async_copy(gu_rows.at[mine], gu_back.at[mine], own_local.at[0])
    own_units.start()

    grad_gain = jnp.zeros((1, own.shape[1]), FULL)
    todo = [("middle", 0)]
    for at in range(1, len(plane.pieces)):
        todo += [("middle", at), ("total", at - 1)]
    todo.append(("total", len(plane.pieces) - 1))
    share = -(-len(todo) // max(1, depth - 1))
    for number in range(depth - 1):
        if number:
            lines[0].turn(number)
        if 0 < number < 3:
            send_units(number - 1, number)
        for kind, at in todo[number * share : (number + 1) * share]:
            half, piece = plane.pieces[at]
            if kind == "middle":
                plane.middle(half, piece)
                continue
            span = plane.span(0, half, piece)
            grads, for_gain = norm_back(
                tokens[span, :].astype(FULL), gain[...], mix(plane.total(half, piece), depth, True)
            )
            grad_input[span, :] = grads
            grad_gain = grad_gain + for_gain

    gain_out[0, 0:1, :] = grad_gain
    gain_out[0, 1:2, :] = grad_gain_mlp[...]

    def swap(at):
        axis, step = steps[at]
        return pltpu.make_async_remote_copy(
            src_ref=gain_out.at[at],
            dst_ref=gain_in.at[at],
            send_sem=gain_send.at[at],
            recv_sem=gain_recv.at[at],
            device_id=paired(axis, step),
            device_id_type=pl.DeviceIdType.MESH,
        )

    def swap_on(at):
        swap(at).wait_recv()
        total = gain_out[at] + gain_in[at]
        if at + 1 < len(steps):
            gain_out[at + 1] = total
            swap(at + 1).start()
        else:
            gains[...] = total

    send_units(min(2, max(depth - 2, 0)), 4)
    swap(0).start()
    for at in range(3):
        swap_on(at)

    lines[0].finish(qkv_total)
    rows = qkv_parts.shape[2] // 4
    for at in range(4):
        sent[at] = qkv_total[at * rows : (at + 1) * rows, :].astype(LOW)
    for at in range(3):
        exchange(0, at).start()
    back[mine] = sent[mine]
    if with_out:
        for number in range(1, depth - 1):
            lines[1].turn(number)
    swap_on(3)
    for kind in range(1, kinds):
        for at in range(3):
            exchange(kind, at).wait_recv()
    own_units.wait()
    spread_parts((grad_gate, grad_up), gu_back, UNIT_TILE, True)
    for at in range(4, len(steps)):
        swap_on(at)
    for at in range(3):
        exchange(0, at).wait_recv()
    spread_parts((grad_query, grad_key, grad_value), back, PAIR, deep)
    if with_out:
        lines[1].finish(out_total)
        grad_out[...] = out_total[...]

    for at in range(3):
        for kind in range(kinds):
            exchange(kind, at).wait_send()
    for at in range(len(steps)):
        swap(at).wait_send()
    plane.finish()
    for line in lines:
        line.close()


def last_call(deep, depth, rows, width, plane_operands, gu_rows, qkv_parts, out_parts):
    whole = pl.BlockSpec(memory_space=pltpu.VMEM)
    with_out = out_parts is not None
    there = pl.BlockSpec(memory_space=pl.ANY)
    parts = [gu_rows, qkv_parts] + ([out_parts] if with_out else [])
    operands = hbm(plane_operands[0]) + list(plane_operands[1:]) + hbm(*parts)
    in_specs = [there] + [whole] * (len(plane_operands) - 1) + [there] * len(parts)
    part_rows, part_width = qkv_parts.shape[2] // 4, qkv_parts.shape[3]
    outs = [like((rows, width), FULL), like((2, width), FULL)]
    outs += [like((part_rows, 2 * gu_rows.shape[2]), LOW)] * 2
    outs += [like((part_rows, 4 * part_width // 3), FULL)] * 3
    scratch = plane_scratch(rows, width) + line_scratch(depth, qkv_parts.shape)
    scratch.append(pltpu.VMEM(qkv_parts.shape[2:], FULL))
    if with_out:
        outs.append(like(out_parts.shape[2:], FULL))
        scratch += line_scratch(depth, out_parts.shape)
        scratch.append(pltpu.VMEM(out_parts.shape[2:], FULL))
    swaps = 3 + (depth - 1).bit_length()
    scratch += [
        pltpu.VMEM((4, part_rows, part_width), LOW),
        pltpu.VMEM((4, part_rows, part_width), LOW),
        pltpu.VMEM(gu_rows.shape, LOW),
        pltpu.SemaphoreType.DMA((1 + part_rows // 16, 3)),
        pltpu.SemaphoreType.DMA((1 + part_rows // 16, 3)),
        pltpu.SemaphoreType.DMA((1,)),
        pltpu.VMEM((swaps, 2, width), FULL),
        pltpu.VMEM((swaps, 2, width), FULL),
        pltpu.SemaphoreType.DMA((swaps,)),
        pltpu.SemaphoreType.DMA((swaps,)),
    ]
    return pl.pallas_call(
        functools.partial(last_kernel, deep, with_out),
        out_shape=outs,
        in_specs=in_specs,
        out_specs=[whole] * len(outs),
        scratch_shapes=scratch,
        compiler_params=pltpu.CompilerParams(
            collective_id=3, has_side_effects=True, vmem_limit_bytes=50 * 1024 * 1024
        ),
        cost_estimate=pl.CostEstimate(
            flops=rows * width * 100, bytes_accessed=rows * width * 400, transcendentals=0
        ),
    )(*operands)


class LineGather:
    def __init__(self, core_first, full, sems, columns=slice(None)):
        self.core_first, self.full, self.columns = core_first, full, columns
        self.right_send, self.right_recv, self.left_send, self.left_recv = sems[:4]
        self.core_send, self.core_recv = sems[4:]
        self.depth = full.shape[1 if core_first else 0]

    def copy(self, at, send, recv, device):
        core = lax.axis_index("c")
        block = (core, at) if self.core_first else (at, core)
        place = self.full.at[block + (slice(None), self.columns)]
        return pltpu.make_async_remote_copy(
            src_ref=place,
            dst_ref=place,
            send_sem=send.at[at],
            recv_sem=recv.at[at],
            device_id=device,
            device_id_type=pl.DeviceIdType.MESH,
        )

    def right(self, at):
        return self.copy(at, self.right_send, self.right_recv, beside(1))

    def left(self, at):
        return self.copy(at, self.left_send, self.left_recv, beside(-1))

    def core(self, at):
        return self.copy(at, self.core_send, self.core_recv, peer("c"))

    def pass_on(self, number):
        index, last = lax.axis_index("z"), self.depth - 1
        for step, move in ((1, self.right), (-1, self.left)):
            at = index - number * step
            inside = (at >= 0) & (at <= last)

            @pl.when(inside)
            def _():
                if number:
                    move(at).wait_recv()

                @pl.when((index < last) if step == 1 else (index > 0))
                def _():
                    move(at).start()

                if number or step == 1:
                    self.core(at).start()

    def close(self):
        index, last = lax.axis_index("z"), self.depth - 1
        for at in range(self.depth):
            self.core(at).wait()

            @pl.when((index < last) & (at <= index))
            def _():
                self.right(at).wait_send()

            @pl.when((index > 0) & (at >= index))
            def _():
                self.left(at).wait_send()


def first_kernel(with_out, *refs):
    refs = list(refs)

    def take(count):
        taken, refs[:count] = refs[:count], []
        return taken

    weights, (tokens, gain_parts) = take(5), take(2)
    w_out = take(1)[0] if with_out else None
    full_qkv, gu_rows, spread, gains = take(4)
    full_out = take(1)[0] if with_out else None
    spread_send, spread_recv, gain_all, gain_send, gain_recv = take(5)
    swap_send, swap_recv, local, qkv_parts, gu_parts = take(5)
    held, held_sems = take(5), take(1)[0]
    runs = full_qkv.shape[3] // QKV_RUNS
    runs = [pl.ds(at * runs, runs) for at in range(QKV_RUNS)]
    lines = [LineGather(True, full_qkv, take(6), run) for run in runs]
    if with_out:
        lines.insert(0, LineGather(False, full_out, take(6)))

    loads = [
        pltpu.make_async_copy(weight, kept, held_sems.at[at])
        for at, (weight, kept) in enumerate(zip(weights, held))
    ]
    for load in loads:
        load.start()
    depth = full_qkv.shape[1]
    at_z, at_x, at_c, at_y = (lax.axis_index(axis) for axis in AXES)
    mine = at_x * 2 + at_y
    steps = []
    step = 1
    while step < depth:
        steps.append(("z", step))
        step *= 2
    steps += [("c", 1), ("y", 1), ("x", 1)]
    index = ((at_x * 2 + at_y) * 2 + at_c) * depth + at_z
    far = [paired(axis, step) for axis, step in steps if step > 1]
    greet([peer("c"), peer("x"), peer("y"), peer("x", "y")] + far, line=True)

    def gather_parts(target, sources, tile, in_blocks):
        for part in range(4):
            for at in range(target.shape[2] // tile):
                source = sources[at % len(sources)]
                runs = part_columns(
                    source.shape[1], depth, in_blocks, part, at // len(sources) * tile, tile
                )
                pieces = [source[:, place : place + length] for _, place, length in runs]
                whole = pieces[0] if len(pieces) == 1 else jnp.concatenate(pieces, axis=1)
                target[part, :, at * tile : (at + 1) * tile] = whole

    for load in loads[:3]:
        load.wait()
    gather_parts(qkv_parts, held[:3], PAIR, with_out)
    members = [("y",), ("x",), ("x", "y")]
    part_rows = qkv_parts.shape[1]

    def exchange(kind, at):
        there = peer(*members[at])
        theirs = there.get("x", at_x) * 2 + there.get("y", at_y)
        source, target = gu_parts.at[theirs], gu_rows.at[mine]
        if kind < QKV_RUNS:
            source = qkv_parts.at[theirs, :, runs[kind]]
            target = full_qkv.at[at_c, at_z, pl.ds(mine * part_rows, part_rows), runs[kind]]
        return pltpu.make_async_remote_copy(
            src_ref=source,
            dst_ref=target,
            send_sem=swap_send.at[kind, at],
            recv_sem=swap_recv.at[kind, at],
            device_id=there,
            device_id_type=pl.DeviceIdType.MESH,
        )

    own_qkv = pltpu.make_async_copy(
        qkv_parts.at[mine],
        full_qkv.at[at_c, at_z, pl.ds(mine * part_rows, part_rows)],
        local.at[0],
    )
    own_gu = pltpu.make_async_copy(gu_parts.at[mine], gu_rows.at[mine], local.at[1])
    for kind in range(QKV_RUNS):
        for at in (2, 0, 1):
            exchange(kind, at).start()
    own_qkv.start()
    if with_out:
        own_out = pltpu.make_async_copy(w_out, full_out.at[at_z, at_c], local.at[2])
        own_out.start()

    def swap(at):
        axis, step = steps[at]
        count = 2**at
        place = gain_all.at[pl.ds((index // count) * count, count)]
        return pltpu.make_async_remote_copy(
            src_ref=place,
            dst_ref=place,
            send_sem=gain_send.at[at],
            recv_sem=gain_recv.at[at],
            device_id=paired(axis, step),
            device_id_type=pl.DeviceIdType.MESH,
        )

    gain_all[index] = gain_parts[0]
    for at in range(len(steps)):
        swap(at).start()
        if at == 1:
            for load in loads[3:]:
                load.wait()
            gather_parts(gu_parts, held[3:], UNIT_TILE, True)
            own_gu.start()
        swap(at).wait_recv()
        if at == len(steps) - 3:
            own_qkv.wait()
        kind = at - (len(steps) - 3)
        if 0 <= kind < QKV_RUNS:
            for other in range(3):
                exchange(kind, other).wait_recv()
            lines[kind - QKV_RUNS].pass_on(0)
        if at == len(steps) - 4 and with_out:
            own_out.wait()
            lines[0].pass_on(0)
    each = gain_parts.shape[2]
    for at in range(8 * depth):
        x, y, c, z = at // (4 * depth), at // (2 * depth) % 2, at // depth % 2, at % depth
        place = (((z * 2 + x) * 2 + c) * 2 + y) * each
        gains[:, place : place + each] = gain_all[at]

    plane = PlaneSum(None, tokens, None, None, None, spread_send, spread_recv, None, None, spread)
    gain = gains[0:1, :]
    for half, at in plane.pieces:
        values = tokens[plane.span(0, half, at), :].astype(FULL)
        plane.give(half, at, mix((values * factor_of(values) * gain).astype(LOW), depth))
    for at in range(3):
        exchange(QKV_RUNS, at).start()

    todo = list(plane.pieces)
    share = -(-len(todo) // max(1, depth - 1))
    for number in range(1, depth):
        for line in lines:
            line.pass_on(number)
        for half, at in todo[(number - 1) * share : number * share]:
            plane.forward(half, at)
    for half, at in plane.pieces:
        plane.close_spread(half, at)
    own_gu.wait()
    for at in range(3):
        for kind in range(QKV_RUNS):
            exchange(kind, at).wait_send()
        exchange(QKV_RUNS, at).wait()
    for at in range(len(steps)):
        swap(at).wait_send()
    for line in lines:
        line.close()


def first_call(depth, weights, tokens, gain_parts, w_out):
    rows, width = tokens.shape
    whole = pl.BlockSpec(memory_space=pltpu.VMEM)
    there = pl.BlockSpec(memory_space=pl.ANY)
    operands = hbm(*weights) + [tokens, gain_parts]
    in_specs = [there] * len(weights) + [whole, whole]
    part_rows, part_width, part_units = weights[0].shape[0], 3 * width // 4, weights[3].shape[1] // 2
    outs = [
        in_hbm((2, depth, 4 * part_rows, part_width), LOW),
        in_hbm((4, part_rows, part_units), LOW),
        in_hbm((4 * rows, width), LOW),
        like((2, width), FULL),
    ]
    out_specs = [there, there, whole, whole]
    swaps = 3 + (depth - 1).bit_length()
    scratch = [
        pltpu.SemaphoreType.DMA((6, 2, PIECES)),
        pltpu.SemaphoreType.DMA((6, 2, PIECES)),
        pltpu.VMEM((8 * depth, 2, width // (8 * depth)), FULL),
        pltpu.SemaphoreType.DMA((swaps,)),
        pltpu.SemaphoreType.DMA((swaps,)),
        pltpu.SemaphoreType.DMA((QKV_RUNS + 1, 3)),
        pltpu.SemaphoreType.DMA((QKV_RUNS + 1, 3)),
        pltpu.SemaphoreType.DMA((3,)),
        pltpu.VMEM((4, part_rows, part_width), LOW),
        pltpu.VMEM((4, part_rows, part_units), LOW),
    ]
    scratch += [pltpu.VMEM(weight.shape, LOW) for weight in weights]
    scratch.append(pltpu.SemaphoreType.DMA((len(weights),)))
    scratch += [pltpu.SemaphoreType.DMA((depth,))] * (6 * QKV_RUNS)
    if w_out is not None:
        operands.append(w_out)
        in_specs.append(there)
        outs.append(in_hbm((depth, 2) + w_out.shape, LOW))
        out_specs.append(there)
        scratch += [pltpu.SemaphoreType.DMA((depth,))] * 6
    return pl.pallas_call(
        functools.partial(first_kernel, w_out is not None),
        out_shape=outs,
        in_specs=in_specs,
        out_specs=out_specs,
        scratch_shapes=scratch,
        compiler_params=pltpu.CompilerParams(
            collective_id=4, has_side_effects=True, vmem_limit_bytes=24 * 1024 * 1024
        ),
        cost_estimate=pl.CostEstimate(
            flops=rows * width * 100, bytes_accessed=rows * width * 200, transcendentals=0
        ),
    )(*operands)


def plane_scratch(rows, width):
    step = rows // (2 * PIECES)
    return [
        pltpu.VMEM((2, PIECES, 2, step, width), LOW),
        pltpu.VMEM((2, PIECES, step, width), LOW),
        pltpu.VMEM((2, PIECES, step, width), LOW),
        pltpu.SemaphoreType.DMA((6, 2, PIECES)),
        pltpu.SemaphoreType.DMA((6, 2, PIECES)),
        pltpu.VMEM((2, rows // 2, width), LOW),
        pltpu.SemaphoreType.DMA((2,)),
    ]


def plane_call(kernel, number, rows, width, outs, gain, *operands):
    whole = pl.BlockSpec(memory_space=pltpu.VMEM)
    there = pl.BlockSpec(memory_space=pl.ANY)
    loaded = operands[1:]
    return pl.pallas_call(
        kernel,
        out_shape=outs,
        in_specs=[there] * len(operands) + [whole],
        out_specs=[whole] * len(outs),
        scratch_shapes=plane_scratch(rows, width)
        + [pltpu.VMEM(item.shape, item.dtype) for item in loaded]
        + [pltpu.SemaphoreType.DMA((len(loaded),))],
        compiler_params=pltpu.CompilerParams(
            collective_id=number, has_side_effects=True, vmem_limit_bytes=32 * 1024 * 1024
        ),
        cost_estimate=pl.CostEstimate(
            flops=rows * width * 100, bytes_accessed=rows * width * 200, transcendentals=0
        ),
    )(*hbm(*operands), gain)


def body(
    tokens,
    cotangent,
    seq_lengths,
    assignment,
    w_query,
    w_key,
    w_value,
    w_out,
    w_gate,
    w_up,
    w_down,
    gain_attn,
    gain_mlp,
):
    rows, width = tokens.shape
    depth = lax.axis_size("z")
    at_z, at_x, at_c, at_y = (lax.axis_index(axis) for axis in AXES)
    mine = at_x * 2 + at_y
    whole_heads = w_out.shape[0] % HEAD_DIM == 0
    head_deep = depth if whole_heads else 0
    head_width = width // 4

    def in_order(weight, back=False):
        if blocks_align(width, depth):
            return weight
        order = (2, 0, 1, 3, 4) if back else (1, 2, 0, 3, 4)
        shape = (depth, 2, 2) if back else (2, depth, 2)
        apart = weight.reshape(shape + (-1, weight.shape[1]))
        return apart.transpose(order).reshape(weight.shape)

    def core_columns(values, core):
        if blocks_align(width, depth):
            return lax.dynamic_slice_in_dim(values, core * (width // 2), width // 2, axis=1)
        apart = values.reshape(values.shape[0], depth, 2, 2, -1)
        part = lax.dynamic_index_in_dim(apart, core, 3, keepdims=False)
        return part.reshape(values.shape[0], -1)

    slot_at = [(at_z * 2 + x) * 2 + at_c for x in (at_x, 1 - at_x)]
    slot_length = [seq_lengths[assignment[slot]] for slot in slot_at]
    row = jnp.arange(rows)
    valid_rows = (at_y * rows + row < slot_length[0]).astype(FULL)[:, None]

    full_qkv, gu_rows, normed_all, gains, *rest = first_call(
        depth,
        (w_query, w_key, w_value, w_gate, w_up),
        tokens,
        jnp.stack([gain_attn, gain_mlp])[None].astype(FULL),
        w_out if whole_heads else None,
    )
    full_qkv = in_order(full_qkv.reshape(width, -1))
    gain_one, gain_two = gains[0], gains[1]
    full_gu = lax.all_gather(
        gu_rows.reshape(-1, gu_rows.shape[2]), ("c", "z"), axis=0, tiled=True
    )
    full_gu = in_order(full_gu)
    if whole_heads:
        full_out = rest[0].reshape(-1, width)
    else:
        every = lax.all_gather(w_out, AXES, axis=0, tiled=True)
        full_out = lax.dynamic_slice_in_dim(every, mine * head_width, head_width, axis=0)
    w_down, normed_all = lax.optimization_barrier((w_down, normed_all))

    grad_out = cotangent.astype(FULL) * valid_rows
    grad_low = grad_out.astype(LOW)
    normed_all, grad_low = lax.optimization_barrier((normed_all, grad_low))
    near = plane_gather_near(grad_low)
    qkv = dot(normed_all, full_qkv)
    qkv, near = lax.optimization_barrier((qkv, near))
    far = plane_gather_far(grad_low, near)
    cosine, sine = rope_tables(jnp.arange(2 * rows))
    info = jnp.stack([at_y.astype(jnp.int32)] + slot_length)
    heads_out, lse, qkv = attend(info, qkv, cosine, sine)
    w_down, heads_out, far = lax.optimization_barrier((w_down, heads_out, far))
    grad_low_all = plane_gathered(grad_low, near, far)
    full_down = lax.all_gather(w_down, ("z", "c"), axis=0, tiled=True)
    branch_low, branch_own = project(heads_out[None], full_out, False)
    attended, normed2_all = plane_call(
        forward_kernel,
        1,
        rows,
        width,
        [like((rows, width), FULL), in_hbm((4 * rows, width), LOW)],
        gain_two[None],
        branch_low,
        branch_own,
        tokens,
    )
    both, active = activate(normed2_all, full_gu)

    down_part = dot_rows(active, grad_low_all).astype(LOW)
    grad_w_down = lax.psum_scatter(down_part, ("z", "c"), scatter_dimension=0, tiled=True)
    grad_w_down = grad_w_down.astype(FULL)
    down_part, grad_low_all = lax.optimization_barrier((down_part, grad_low_all))
    grad_gu = activate_back(grad_low_all, full_down, both)
    theirs = dot_rows(core_columns(normed2_all, 1 - at_c), grad_gu).astype(LOW)
    from_core = swap_c(theirs)
    theirs, grad_gu = lax.optimization_barrier((theirs, grad_gu))
    back_low, back_own = project(grad_gu[None], full_gu, True)
    back_low, from_core, grad_gu = lax.optimization_barrier((back_low, from_core, grad_gu))
    ours = dot_rows(core_columns(normed2_all, at_c), grad_gu) + from_core.astype(FULL)
    grad_gu_rows = lax.psum_scatter(ours.astype(LOW), "z", scatter_dimension=0, tiled=True)
    ours, back_low = lax.optimization_barrier((ours, back_low))
    grad_attended, grad_gain_mlp, grad_branch = plane_call(
        backward_kernel,
        2,
        rows,
        width,
        [like((rows, width), FULL), like((1, width), FULL), in_hbm((4 * rows, width), LOW)],
        gain_two[None],
        back_low,
        back_own,
        attended,
        grad_out,
    )
    grad_branch, active = lax.optimization_barrier((grad_branch, active))

    grad_w_out = dot_rows(heads_out, grad_branch)
    out_parts = None
    if whole_heads:
        out_parts = grad_w_out.astype(LOW).reshape(depth, 2, -1, width)
    else:
        spread = lax.dynamic_update_slice_in_dim(
            jnp.zeros((width, width), FULL), grad_w_out, mine * head_width, axis=0
        )
        grad_w_out = lax.psum_scatter(spread, AXES, scatter_dimension=0, tiled=True)
    grad_mixed = dot_through(grad_branch, full_out).astype(LOW)
    last_low, last_own = project(active[None], full_down, False)
    last_low, grad_mixed = lax.optimization_barrier((last_low, grad_mixed))
    near = plane_reduce_near(last_low)
    grad_qkv = attend_back(info, qkv, grad_mixed, lse, cosine, sine)
    grad_qkv, near, grad_w_down = lax.optimization_barrier((grad_qkv, near, grad_w_down))
    far = plane_reduce_far(last_low, near)
    grad_qkv_part = in_order(dot_rows(normed_all, grad_qkv).astype(LOW), True)
    back_low, back_own = project(grad_qkv[None], full_qkv, True)
    back_low, far = lax.optimization_barrier((back_low, far))
    result = attended + plane_reduced(last_own, near, far)
    output = (result * valid_rows).astype(LOW)
    grad_input, grad_gains, *last_weights = last_call(
        head_deep,
        depth,
        rows,
        width,
        [
            back_low,
            back_own,
            tokens,
            gain_one[None],
            grad_gain_mlp,
        ],
        grad_gu_rows.reshape(4, -1, grad_gu_rows.shape[1]),
        grad_qkv_part.reshape(2, depth, -1, grad_qkv_part.shape[1]),
        out_parts,
    )
    grad_w_gate, grad_w_up, grad_w_query, grad_w_key, grad_w_value = last_weights[:5]
    grad_w_gate, grad_w_up = grad_w_gate.astype(FULL), grad_w_up.astype(FULL)
    grad_input = grad_input + grad_attended
    if whole_heads:
        grad_w_out = last_weights[5]
    index = ((at_z * 2 + at_x) * 2 + at_c) * 2 + at_y
    part = width // (8 * depth)
    grad_gains = lax.dynamic_slice_in_dim(grad_gains, index * part, part, axis=1)
    return (
        output,
        grad_input,
        grad_w_query,
        grad_w_key,
        grad_w_value,
        grad_w_out,
        grad_w_gate,
        grad_w_up,
        grad_w_down,
        grad_gains[0],
        grad_gains[1],
    )


def solution(mesh):
    shape = (mesh.shape["dp"] // 4, 2, 2, mesh.shape["seq"])
    grid = Mesh(mesh.devices.reshape(shape), AXES)
    split = P(AXES, None)
    part = P(AXES)
    return jax.shard_map(
        body,
        mesh=grid,
        in_specs=(split, split, P(), P()) + (split,) * 7 + (part, part),
        out_specs=(split,) * 9 + (part, part),
        check_vma=False,
    )
```

```python
import functools

import jax
import jax.experimental.pallas as pl
import jax.experimental.pallas.tpu as pltpu
import jax.numpy as jnp
from jax import lax
from jax.sharding import Mesh, PartitionSpec as P

HEAD_DIM = 64
PAIR = 2 * HEAD_DIM
norm_eps = 1e-05
rope_base = 130000.0
AXES = ("z", "x", "c", "y")
LOW = jnp.bfloat16
FULL = jnp.float32
like = jax.ShapeDtypeStruct
in_hbm = pltpu.HBM


def hbm(*values):
    return [pltpu.with_memory_space_constraint(value, pltpu.HBM) for value in values]


def swap_x(value):
    return lax.ppermute(value, "x", [(0, 1), (1, 0)])


def swap_y(value):
    return lax.ppermute(value, "y", [(0, 1), (1, 0)])


def swap_c(value):
    return lax.ppermute(value, "c", [(0, 1), (1, 0)])


def plane_gather_near(value):
    half = value.shape[0] // 2
    return swap_y(value[:half]), swap_x(value[half:])


def plane_gather_far(value, near):
    half = value.shape[0] // 2
    return (
        swap_x(jnp.concatenate([value[:half], near[0]], axis=0)),
        swap_y(jnp.concatenate([value[half:], near[1]], axis=0)),
    )


def plane_gathered(value, near, far):
    half = value.shape[0] // 2
    top, low = far
    return jnp.concatenate(
        [value, near[0], low[:half], top[:half], near[1], top[half:], low[half:]], axis=0
    )


def plane_blocks(value):
    count = value.shape[0] // 4
    return [value[at * count : (at + 1) * count] for at in range(4)]


def plane_reduce_near(value):
    _, by_y, by_x, by_d = plane_blocks(value)
    half = by_y.shape[0] // 2
    return (
        swap_x(jnp.concatenate([by_x[:half], by_d[:half]], axis=0)),
        swap_y(jnp.concatenate([by_y[half:], by_d[half:]], axis=0)),
    )


def plane_reduce_far(value, near):
    _, by_y, by_x, _ = plane_blocks(value)
    half = by_y.shape[0] // 2
    return (
        swap_y((by_y[:half].astype(FULL) + near[0][half:].astype(FULL)).astype(LOW)),
        swap_x((by_x[half:].astype(FULL) + near[1][half:].astype(FULL)).astype(LOW)),
    )


def plane_reduced(own, near, far):
    half = own.shape[0] // 2
    return own + jnp.concatenate(
        [
            near[0][:half].astype(FULL) + far[0].astype(FULL),
            near[1][:half].astype(FULL) + far[1].astype(FULL),
        ],
        axis=0,
    )


def part_place(depth, part, block):
    return ((block // 2 * 2 + part // 2) * 2 + block % 2) * 2 + part % 2


def part_columns(width, depth, in_blocks, part, start, count):
    if not in_blocks:
        return [(0, part * (width // 4) + start, count)]
    each = width // (8 * depth)
    length = min(each, count)
    return [
        (
            at,
            part_place(depth, part, (start + at) // each) * each + (start + at) % each,
            length,
        )
        for at in range(0, count, length)
    ]


def factor_of(values):
    return lax.rsqrt(jnp.mean(values * values, axis=-1, keepdims=True) + norm_eps)


def rope_tables(positions):
    halves = HEAD_DIM // 2
    frequency = rope_base ** (-(jnp.arange(halves).astype(FULL) * 2.0 / HEAD_DIM))
    angles = positions.astype(FULL)[:, None] * frequency[None, :]
    cosine = jnp.cos(angles)
    sine = jnp.sin(angles)
    return (
        jnp.concatenate([cosine] * 4, axis=1),
        jnp.concatenate([-sine, sine, -sine, sine], axis=1),
    )


def turned(values, low_half):
    lanes = values.shape[1]
    halves = HEAD_DIM // 2
    return jnp.where(
        low_half, pltpu.roll(values, lanes - halves, 1), pltpu.roll(values, halves, 1)
    )


def lane_masks(rows):
    lane = lax.broadcasted_iota(jnp.int32, (rows, PAIR), 1)
    return lane % HEAD_DIM < HEAD_DIM // 2, lane < HEAD_DIM


def diagonal_mask(first, length, rows):
    query = lax.broadcasted_iota(jnp.int32, (rows, rows), 0)
    key = lax.broadcasted_iota(jnp.int32, (rows, rows), 1)
    return (key <= query) & (key + first < length)


def attend_kernel(info, qkv_ref, c_ref, s_ref, mixed, lse, qkv_out):
    rows = qkv_ref.shape[0] // 2
    length = info[1 + pl.program_id(0)]
    scale = HEAD_DIM ** (-0.5)
    low_half, first_head = lane_masks(rows)
    place = [pl.multiple_of(jnp.where(info[0] == at, 0, rows), rows) for at in range(2)]
    queries, keys, values = [], [], []
    for at in range(2):
        span = pl.ds(place[at], rows)
        table = pl.ds(at * rows, rows)
        for number, kept in enumerate((queries, keys, values)):
            lanes = slice(number * PAIR, (number + 1) * PAIR)
            item = qkv_ref[span, lanes]
            if number < 2:
                item = item * c_ref[table, :] + turned(item, low_half) * s_ref[table, :]
            item = item.astype(LOW)
            qkv_out[span, lanes] = item
            kept.append(item)
    for at in range(2):
        allowed = diagonal_mask(at * rows, length, rows)
        found, logs = [], []
        for head in range(2):
            only = first_head if head == 0 else jnp.logical_not(first_head)
            query = jnp.where(only, queries[at], jnp.zeros_like(queries[at]))
            scores = []
            for block in range(at + 1):
                score = dot_through(query, keys[block]) * scale
                scores.append(jnp.where(allowed, score, -1e30) if block == at else score)
            top = jnp.max(scores[0], axis=1, keepdims=True)
            for score in scores[1:]:
                top = jnp.maximum(top, jnp.max(score, axis=1, keepdims=True))
            weights = [jnp.exp(score - top) for score in scores]
            total = jnp.sum(weights[0], axis=1, keepdims=True)
            for weight in weights[1:]:
                total = total + jnp.sum(weight, axis=1, keepdims=True)
            share = 1.0 / total
            out = dot((weights[0] * share).astype(LOW), values[0])
            for block in range(1, at + 1):
                out = out + dot((weights[block] * share).astype(LOW), values[block])
            found.append(out)
            logs.append(top + jnp.log(total))
        span = pl.ds(place[at], rows)
        mixed[span, :] = jnp.where(first_head, found[0], found[1]).astype(LOW)
        lse[span, :] = jnp.where(first_head, logs[0], logs[1])


def attend_back_kernel(info, qkv_ref, g_ref, lse_ref, c_ref, s_ref, grads_out):
    rows = qkv_ref.shape[0] // 2
    length = info[1 + pl.program_id(0)]
    scale = HEAD_DIM ** (-0.5)
    low_half, first_head = lane_masks(rows)
    place = [pl.multiple_of(jnp.where(info[0] == at, 0, rows), rows) for at in range(2)]
    spans = [pl.ds(start, rows) for start in place]
    keys = [qkv_ref[span, PAIR : 2 * PAIR] for span in spans]
    values = [qkv_ref[span, 2 * PAIR :] for span in spans]
    key_sums = [[None, None], [None, None]]
    value_sums = [[None, None], [None, None]]

    def unrotated(item, at):
        table = pl.ds(at * rows, rows)
        scaled = item * s_ref[table, :]
        return (item * c_ref[table, :] + turned(scaled, low_half)).astype(LOW)

    def added(old, new):
        return new if old is None else old + new

    for at in range(2):
        allowed = diagonal_mask(at * rows, length, rows)
        query_all, grad_all, logs = qkv_ref[spans[at], :PAIR], g_ref[spans[at], :], lse_ref[spans[at], :]
        found = []
        for head in range(2):
            only = first_head if head == 0 else jnp.logical_not(first_head)
            query = jnp.where(only, query_all, jnp.zeros_like(query_all))
            grad = jnp.where(only, grad_all, jnp.zeros_like(grad_all))
            log = logs[:, head * HEAD_DIM : head * HEAD_DIM + 1]
            probs, grads = [], []
            inner = jnp.zeros((rows, 1), FULL)
            for block in range(at + 1):
                prob = jnp.exp(dot_through(query, keys[block]) * scale - log)
                if block == at:
                    prob = jnp.where(allowed, prob, 0.0)
                grad_prob = dot_through(grad, values[block])
                inner = inner + jnp.sum(prob * grad_prob, axis=1, keepdims=True)
                probs.append(prob)
                grads.append(grad_prob)
            out = None
            for block in range(at + 1):
                grad_score = (probs[block] * (grads[block] - inner)).astype(LOW)
                out = added(out, dot(grad_score, keys[block]))
                key_sums[block][head] = added(key_sums[block][head], dot_rows(grad_score, query_all))
                value_sums[block][head] = added(
                    value_sums[block][head], dot_rows(probs[block].astype(LOW), grad_all)
                )
            found.append(out)
        grads_out[spans[at], :PAIR] = unrotated(jnp.where(first_head, found[0], found[1]) * scale, at)
    for at in range(2):
        both = jnp.where(first_head, key_sums[at][0], key_sums[at][1]) * scale
        grads_out[spans[at], PAIR : 2 * PAIR] = unrotated(both, at)
        both = jnp.where(first_head, value_sums[at][0], value_sums[at][1])
        grads_out[spans[at], 2 * PAIR :] = both.astype(LOW)


def attend(info, qkv, cosine, sine):
    total, width = qkv.shape[0], qkv.shape[1] // 3
    slot_rows, pairs = total // 2, width // PAIR
    part = pl.BlockSpec((slot_rows, PAIR), lambda slot, pair, info: (slot, pair))
    three = pl.BlockSpec((slot_rows, 3 * PAIR), lambda slot, pair, info: (slot, pair))
    table = pl.BlockSpec((slot_rows, PAIR), lambda slot, pair, info: (0, 0))
    return pl.pallas_call(
        attend_kernel,
        grid_spec=pltpu.PrefetchScalarGridSpec(
            num_scalar_prefetch=1,
            grid=(2, pairs),
            in_specs=[three, table, table],
            out_specs=[part, part, three],
        ),
        out_shape=[
            in_hbm((total, width), LOW),
            in_hbm((total, width), FULL),
            in_hbm((total, 3 * width), LOW),
        ],
        compiler_params=pltpu.CompilerParams(vmem_limit_bytes=16 * 1024 * 1024),
        cost_estimate=pl.CostEstimate(
            flops=16 * total * slot_rows * width,
            bytes_accessed=total * width * 24,
            transcendentals=total * slot_rows * width // HEAD_DIM,
        ),
    )(info, qkv, cosine, sine)


def attend_back(info, qkv, grads, lse, cosine, sine):
    total, width = grads.shape
    slot_rows, pairs = total // 2, width // PAIR
    part = pl.BlockSpec((slot_rows, PAIR), lambda slot, pair, info: (slot, pair))
    three = pl.BlockSpec((slot_rows, 3 * PAIR), lambda slot, pair, info: (slot, pair))
    table = pl.BlockSpec((slot_rows, PAIR), lambda slot, pair, info: (0, 0))
    return pl.pallas_call(
        attend_back_kernel,
        grid_spec=pltpu.PrefetchScalarGridSpec(
            num_scalar_prefetch=1,
            grid=(2, pairs),
            in_specs=[three, part, part, table, table],
            out_specs=three,
        ),
        out_shape=in_hbm((total, 3 * width), LOW),
        compiler_params=pltpu.CompilerParams(vmem_limit_bytes=16 * 1024 * 1024),
        cost_estimate=pl.CostEstimate(
            flops=40 * total * slot_rows * width,
            bytes_accessed=total * width * 18,
            transcendentals=total * slot_rows * width // HEAD_DIM,
        ),
    )(info, *hbm(qkv, grads, lse), cosine, sine)


def dot(left, right):
    return jnp.dot(left, right, preferred_element_type=FULL)


def dot_rows(left, right):
    return lax.dot_general(left, right, (((0,), (0,)), ((), ())), preferred_element_type=FULL)


def dot_through(left, right):
    return lax.dot_general(left, right, (((1,), (1,)), ((), ())), preferred_element_type=FULL)


UNIT_TILE = 256
QKV_RUNS = 2


def activate_kernel(normed, weight, both_ref, active_ref):
    both = dot(normed[...], weight[...])
    both_ref[...] = both
    gate, upper = both[:, :UNIT_TILE], both[:, UNIT_TILE:]
    active_ref[...] = (gate * jax.nn.sigmoid(gate) * upper).astype(LOW)


def activate(normed, weight):
    rows, width = normed.shape
    units = weight.shape[1] // 2
    return pl.pallas_call(
        activate_kernel,
        grid=(units // UNIT_TILE,),
        in_specs=[
            pl.BlockSpec((rows, width), lambda at: (0, 0)),
            pl.BlockSpec((width, 2 * UNIT_TILE), lambda at: (0, at)),
        ],
        out_specs=[
            pl.BlockSpec((rows, 2 * UNIT_TILE), lambda at: (0, at)),
            pl.BlockSpec((rows, UNIT_TILE), lambda at: (0, at)),
        ],
        out_shape=[in_hbm((rows, 2 * units), FULL), in_hbm((rows, units), LOW)],
        compiler_params=pltpu.CompilerParams(vmem_limit_bytes=40 * 1024 * 1024),
        cost_estimate=pl.CostEstimate(
            flops=4 * rows * units * width,
            bytes_accessed=rows * units * 10 + units * width * 4,
            transcendentals=rows * units,
        ),
    )(*hbm(normed, weight))


def activate_back_kernel(grad_low, weight, both_ref, out):
    grads = dot_through(grad_low[...], weight[...])
    gate, upper = both_ref[:, :UNIT_TILE], both_ref[:, UNIT_TILE:]
    sigmoid = jax.nn.sigmoid(gate)
    out[:, :UNIT_TILE] = (grads * upper * sigmoid * (1.0 + gate * (1.0 - sigmoid))).astype(LOW)
    out[:, UNIT_TILE:] = (grads * gate * sigmoid).astype(LOW)


def activate_back(grad_low, weight, both):
    rows, units = both.shape[0], both.shape[1] // 2
    width = grad_low.shape[1]
    part = pl.BlockSpec((rows, 2 * UNIT_TILE), lambda at: (0, at))
    return pl.pallas_call(
        activate_back_kernel,
        grid=(units // UNIT_TILE,),
        in_specs=[
            pl.BlockSpec((rows, width), lambda at: (0, 0)),
            pl.BlockSpec((UNIT_TILE, width), lambda at: (at, 0)),
            part,
        ],
        out_specs=part,
        out_shape=in_hbm((rows, 2 * units), LOW),
        compiler_params=pltpu.CompilerParams(vmem_limit_bytes=40 * 1024 * 1024),
        cost_estimate=pl.CostEstimate(
            flops=2 * rows * units * width,
            bytes_accessed=rows * units * 12 + units * width * 2,
            transcendentals=rows * units,
        ),
    )(*hbm(grad_low, weight, both))


def project_kernel(through, left, weight, low, own):
    groups, total, depth = left.shape
    if through:
        found = dot_through(left[0], weight[:, :depth])
        for group in range(1, groups):
            found = found + dot_through(
                left[group], weight[:, group * depth : (group + 1) * depth]
            )
    else:
        found = dot(left[0], weight[...])
    low[...] = found.astype(LOW)
    own[...] = found[: own.shape[0], :]


def project(left, weight, through):
    groups, total, depth = left.shape
    width = weight.shape[0] if through else weight.shape[1]
    tile = 256
    block = (tile, groups * depth) if through else (depth, tile)
    return pl.pallas_call(
        functools.partial(project_kernel, through),
        grid=(width // tile,),
        in_specs=[
            pl.BlockSpec((groups, total, depth), lambda at: (0, 0, 0)),
            pl.BlockSpec(block, (lambda at: (at, 0)) if through else (lambda at: (0, at))),
        ],
        out_specs=[
            pl.BlockSpec((total, tile), lambda at: (0, at)),
            pl.BlockSpec((total // 4, tile), lambda at: (0, at)),
        ],
        out_shape=[in_hbm((total, width), LOW), in_hbm((total // 4, width), FULL)],
        compiler_params=pltpu.CompilerParams(vmem_limit_bytes=40 * 1024 * 1024),
        cost_estimate=pl.CostEstimate(
            flops=2 * groups * total * depth * width,
            bytes_accessed=2 * groups * depth * (total + width) + 3 * total * width,
            transcendentals=0,
        ),
    )(*hbm(left, weight))


AXIS_BLOCK = {"y": 1, "x": 2}
PIECES = 2
FIRST, SECOND = ("x", "y"), ("y", "x")


def peer(*axes):
    return {axis: 1 - lax.axis_index(axis) for axis in axes}


def paired(axis, step):
    index = lax.axis_index(axis)
    return {axis: index + step * (1 - 2 * ((index // step) % 2))}


def beside(step):
    count = lax.axis_size("z")
    return {"z": (lax.axis_index("z") + step + count) % count}


def signal(barrier, device):
    pl.semaphore_signal(barrier, inc=1, device_id=device, device_id_type=pl.DeviceIdType.MESH)


def greet(devices, line=False):
    barrier = pltpu.get_barrier_semaphore()
    count = len(devices)
    for device in devices:
        signal(barrier, device)
    if line:
        index, last = lax.axis_index("z"), lax.axis_size("z") - 1
        for step, there in ((1, index < last), (-1, index > 0)):

            @pl.when(there)
            def _():
                signal(barrier, beside(step))

            count = count + there.astype(jnp.int32)
    pl.semaphore_wait(barrier, count)


class PlaneSum:
    def __init__(
        self, low, own, first_in, second_out, second_in, send, recv, between, local, spread=None
    ):
        self.low, self.own, self.spread = low, own, spread
        self.first_in, self.second_out, self.second_in = first_in, second_out, second_in
        self.send, self.recv = send, recv
        self.between, self.local = between, local
        self.rows = own.shape[0]
        self.step = self.rows // (2 * PIECES)
        self.pieces = [(half, at) for at in range(PIECES) for half in range(2)]

    def span(self, block, half, at):
        return pl.ds(block * self.rows + (half * PIECES + at) * self.step, self.step)

    def copy(self, kind, half, at, source, target, axis):
        return pltpu.make_async_remote_copy(
            src_ref=source,
            dst_ref=target,
            send_sem=self.send.at[kind, half, at],
            recv_sem=self.recv.at[kind, half, at],
            device_id=peer(axis),
            device_id_type=pl.DeviceIdType.MESH,
        )

    def first(self, kind, half, at):
        block = (AXIS_BLOCK[FIRST[half]], 3)[kind]
        return self.copy(
            kind,
            half,
            at,
            self.low.at[self.span(block, half, at)],
            self.first_in.at[half, at, kind],
            FIRST[half],
        )

    def second(self, half, at):
        return self.copy(
            2, half, at, self.second_out.at[half, at], self.second_in.at[half, at], SECOND[half]
        )

    def spreading(self, axis, half, at):
        return self.copy(
            2 + AXIS_BLOCK[axis],
            half,
            at,
            self.spread.at[self.span(0, half, at)],
            self.spread.at[self.span(AXIS_BLOCK[axis], half, at)],
            axis,
        )

    def forwarding(self, half, at):
        block = AXIS_BLOCK[SECOND[half]]
        return self.copy(
            5,
            half,
            at,
            self.spread.at[self.span(block, half, at)],
            self.spread.at[self.span(3, half, at)],
            FIRST[half],
        )

    def load(self, half):
        count = self.rows // 2
        place = pl.ds(AXIS_BLOCK[SECOND[half]] * self.rows + half * count, count)
        return pltpu.make_async_copy(self.low.at[place], self.between.at[half], self.local.at[half])

    def start(self):
        for half, at in self.pieces:
            self.first(0, half, at).start()
            self.first(1, half, at).start()
        for half in range(2):
            self.load(half).start()

    def middle(self, half, at):
        if at == 0:
            self.load(half).wait()
        self.first(0, half, at).wait_recv()
        self.first(1, half, at).wait_recv()
        total = self.between[half, at * self.step : (at + 1) * self.step, :].astype(FULL)
        total = total + self.first_in[half, at, 1].astype(FULL)
        self.second_out[half, at] = total.astype(LOW)
        self.second(half, at).start()

    def total(self, half, at):
        self.second(half, at).wait_recv()
        total = self.own[self.span(0, half, at), :] + self.first_in[half, at, 0].astype(FULL)
        return total + self.second_in[half, at].astype(FULL)

    def give(self, half, at, rows):
        self.spread[self.span(0, half, at), :] = rows
        self.spreading("x", half, at).start()
        self.spreading("y", half, at).start()

    def forward(self, half, at):
        self.spreading(SECOND[half], half, at).wait_recv()
        self.forwarding(half, at).start()

    def finish(self):
        for half, at in self.pieces:
            self.first(0, half, at).wait_send()
            self.first(1, half, at).wait_send()
            self.second(half, at).wait_send()
            if self.spread is not None:
                self.close_spread(half, at)

    def close_spread(self, half, at):
        self.spreading("x", half, at).wait_send()
        self.spreading("y", half, at).wait_send()
        self.spreading(FIRST[half], half, at).wait_recv()
        self.forwarding(half, at).wait()

    def run(self, each, ready):
        count = len(self.pieces)
        self.start()
        ready()
        for turn in range(count + 3):
            if turn < count:
                self.middle(*self.pieces[turn])
            if 1 <= turn <= count:
                half, at = self.pieces[turn - 1]
                self.give(half, at, each(self.span(0, half, at), self.total(half, at)))
            if turn >= 3:
                self.forward(*self.pieces[turn - 3])
        self.finish()


def start_loads(sources, scratch):
    count = len(sources)
    rest, held, sems = scratch[: -count - 1], scratch[-count - 1 : -1], scratch[-1]
    loads = [
        pltpu.make_async_copy(source, kept, sems.at[at])
        for at, (source, kept) in enumerate(zip(sources, held))
    ]
    for load in loads:
        load.start()

    def ready():
        for load in loads:
            load.wait()

    return rest, held, ready


def forward_kernel(low, own, tokens, gain, attended, spread, *scratch):
    scratch, (own, tokens), ready = start_loads((own, tokens), scratch)
    greet([peer("x"), peer("y")])
    plane = PlaneSum(low, own, *scratch, spread)

    def each(span, total):
        values = tokens[span, :].astype(FULL) + total
        attended[span, :] = values
        return mix((values * factor_of(values) * gain[...]).astype(LOW), lax.axis_size("z"))

    plane.run(each, ready)


def norm_back(values, gain, grads):
    factor = factor_of(values)
    weighted = grads * gain
    inner = jnp.mean(weighted * values, axis=-1, keepdims=True)
    grad_gain = jnp.sum(grads * values * factor, axis=0, keepdims=True)
    return factor * weighted - values * (factor * factor * factor) * inner, grad_gain


def backward_kernel(
    low, own, attended, grad_out, gain, grad_attended, grad_gain, spread, *scratch
):
    scratch, (own, attended, grad_out), ready = start_loads((own, attended, grad_out), scratch)
    greet([peer("x"), peer("y")])
    plane = PlaneSum(low, own, *scratch, spread)
    grad_gain[...] = jnp.zeros_like(grad_gain)

    def each(span, total):
        grads, for_gain = norm_back(
            attended[span, :], gain[...], mix(total, lax.axis_size("z"), True)
        )
        grads = grads + grad_out[span, :]
        grad_attended[span, :] = grads
        grad_gain[...] += for_gain
        return grads.astype(LOW)

    plane.run(each, ready)


def blocks_align(width, depth):
    return (width // (4 * depth)) % 128 == 0


def mix(values, depth, back=False):
    if not blocks_align(values.shape[1], depth):
        return values
    block = values.shape[1] // (4 * depth)
    order = [(z * 2 + x) * 2 + c for c in range(2) for z in range(depth) for x in range(2)]
    if back:
        order = sorted(range(4 * depth), key=order.__getitem__)
    return jnp.concatenate([values[:, at * block : (at + 1) * block] for at in order], axis=1)


class LineSum:
    def __init__(self, core_first, parts, sums, line_in, last_in, ours, sems):
        self.core_first, self.parts, self.ours = core_first, parts, ours
        self.sums, self.line_in, self.last_in = sums, line_in, last_in
        self.core_send, self.core_recv, self.send, self.right_recv, self.left_recv = sems[:5]
        self.local = sems[5]
        self.depth = sums.shape[0]

    def place(self, at, core):
        return (core, at) if self.core_first else (at, core)

    def core(self, at):
        return pltpu.make_async_remote_copy(
            src_ref=self.parts.at[self.place(at, 1 - lax.axis_index("c"))],
            dst_ref=self.sums.at[at],
            send_sem=self.core_send.at[at],
            recv_sem=self.core_recv.at[at],
            device_id=peer("c"),
            device_id_type=pl.DeviceIdType.MESH,
        )

    def line(self, at, step, last=False):
        sems = self.right_recv if step == 1 else self.left_recv
        return pltpu.make_async_remote_copy(
            src_ref=self.sums.at[at],
            dst_ref=self.last_in if last else self.line_in.at[at],
            send_sem=self.send.at[at],
            recv_sem=sems.at[at],
            device_id=beside(step),
            device_id_type=pl.DeviceIdType.MESH,
        )

    def start(self):
        ends_first = sorted(range(self.depth), key=lambda at: min(at, self.depth - 1 - at))
        for at in ends_first:
            self.core(at).start()
            self.load(at).start()

    def load(self, at):
        place = self.parts.at[self.place(at, lax.axis_index("c"))]
        return pltpu.make_async_copy(place, self.ours.at[at], self.local.at[at])

    def both_cores(self, at):
        self.load(at).wait()
        self.core(at).wait_recv()
        return self.ours[at].astype(FULL) + self.sums[at].astype(FULL)

    def pass_on(self, at, step, first):
        total = self.both_cores(at)
        if not first:
            self.line(at, step).wait_recv()
            total = total + self.line_in[at].astype(FULL)
        self.sums[at] = total.astype(LOW)
        if step == 1:
            self.line(at, 1).start()
            return
        ends = at == lax.axis_index("z") - 1

        @pl.when(ends)
        def _():
            self.line(at, -1, True).start()

        @pl.when(jnp.logical_not(ends))
        def _():
            self.line(at, -1).start()

    def from_ends(self):
        index, last = lax.axis_index("z"), self.depth - 1
        for number in range(last):

            @pl.when(index == 0)
            def _():
                self.pass_on(last - number, 1, True)

            @pl.when(index == last)
            def _():
                self.pass_on(number, -1, True)

    def turn(self, time):
        index, last = lax.axis_index("z"), self.depth - 1

        @pl.when((index > 0) & (index <= time))
        def _():
            self.pass_on(index + last - time, 1, False)

        @pl.when((index < last) & (last - index <= time))
        def _():
            self.pass_on(time - (last - index), -1, False)

    def finish(self, total):
        index, last = lax.axis_index("z"), self.depth - 1
        total[...] = self.both_cores(index)

        @pl.when(index > 0)
        def _():
            self.line(index, 1).wait_recv()
            total[...] += self.line_in[index].astype(FULL)

        @pl.when(index < last)
        def _():
            self.line(index, -1, True).wait_recv()
            total[...] += self.last_in[...].astype(FULL)

    def close(self):
        index = lax.axis_index("z")
        for at in range(self.depth):
            self.core(at).wait_send()

            @pl.when(index < at)
            def _():
                self.line(at, 1).wait_send()

            @pl.when(index > at)
            def _():
                self.line(at, -1).wait_send()


def line_scratch(depth, shape):
    rows, columns = shape[2:]
    sems = [pltpu.SemaphoreType.DMA((depth,))] * 6
    buffers = [pltpu.VMEM((depth, rows, columns), LOW)] * 2
    buffers += [pltpu.VMEM((rows, columns), LOW), pltpu.VMEM((depth, rows, columns), LOW)]
    return buffers + sems


def last_kernel(deep, with_out, *refs):
    refs = list(refs)

    def take(count):
        taken, refs[:count] = refs[:count], []
        return taken

    low, own, tokens, gain, grad_gain_mlp, gu_rows, qkv_parts = take(7)
    out_parts = take(1)[0] if with_out else None
    grad_input, gains, grad_gate, grad_up, grad_query, grad_key, grad_value = take(7)
    grad_out = take(1)[0] if with_out else None
    plane_refs = take(7)
    qkv_refs, (qkv_total,) = take(10), take(1)
    if with_out:
        out_refs, (out_total,) = take(10), take(1)
    sent, back, gu_back, back_send, back_recv, own_local = take(6)
    gain_in, gain_out, gain_send, gain_recv = take(4)

    depth = qkv_parts.shape[1]
    steps = [("c", 1), ("x", 1), ("y", 1)]
    step = 1
    while step < depth:
        steps.append(("z", step))
        step *= 2
    far = [paired(axis, step) for axis, step in steps if step > 1]
    greet([peer("c"), peer("x"), peer("y"), peer("x", "y")] + far, line=True)

    plane = PlaneSum(low, own, *plane_refs)
    lines = [LineSum(True, qkv_parts, *qkv_refs[:4], qkv_refs[4:])]
    if with_out:
        lines.append(LineSum(False, out_parts, *out_refs[:4], out_refs[4:]))
    mine = lax.axis_index("x") * 2 + lax.axis_index("y")
    members = [("y",), ("x",), ("x", "y")]

    def exchange(kind, at):
        there = peer(*members[at])
        theirs = there.get("x", lax.axis_index("x")) * 2 + there.get("y", lax.axis_index("y"))
        source, target = sent.at[theirs], back.at[mine]
        if kind:
            span = pl.ds((kind - 1) * 16, 16)
            source, target = gu_rows.at[theirs, span], gu_back.at[mine, span]
        return pltpu.make_async_remote_copy(
            src_ref=source,
            dst_ref=target,
            send_sem=back_send.at[kind, at],
            recv_sem=back_recv.at[kind, at],
            device_id=there,
            device_id_type=pl.DeviceIdType.MESH,
        )

    kinds = 1 + gu_rows.shape[1] // 16

    def send_units(first, last):
        for kind in range(1 + (kinds - 1) * first // 4, 1 + (kinds - 1) * last // 4):
            for at in range(3):
                exchange(kind, at).start()

    def spread_parts(targets, source, tile, in_blocks):
        for part in range(4):
            for at in range(source.shape[2] // tile):
                target = targets[at % len(targets)]
                columns = source[part, :, at * tile : (at + 1) * tile].astype(target.dtype)
                runs = part_columns(
                    target.shape[1], depth, in_blocks, part, at // len(targets) * tile, tile
                )
                for own, place, length in runs:
                    target[:, place : place + length] = columns[:, own : own + length]

    lines[0].start()
    lines[0].from_ends()
    plane.start()
    for line in lines[1:]:
        line.start()
        line.from_ends()
    own_units = pltpu.make_async_copy(gu_rows.at[mine], gu_back.at[mine], own_local.at[0])
    own_units.start()

    grad_gain = jnp.zeros((1, own.shape[1]), FULL)
    todo = [("middle", 0)]
    for at in range(1, len(plane.pieces)):
        todo += [("middle", at), ("total", at - 1)]
    todo.append(("total", len(plane.pieces) - 1))
    share = -(-len(todo) // max(1, depth - 1))
    for number in range(depth - 1):
        if number:
            lines[0].turn(number)
        if 0 < number < 3:
            send_units(number - 1, number)
        for kind, at in todo[number * share : (number + 1) * share]:
            half, piece = plane.pieces[at]
            if kind == "middle":
                plane.middle(half, piece)
                continue
            span = plane.span(0, half, piece)
            grads, for_gain = norm_back(
                tokens[span, :].astype(FULL), gain[...], mix(plane.total(half, piece), depth, True)
            )
            grad_input[span, :] = grads
            grad_gain = grad_gain + for_gain

    gain_out[0, 0:1, :] = grad_gain
    gain_out[0, 1:2, :] = grad_gain_mlp[...]

    def swap(at):
        axis, step = steps[at]
        return pltpu.make_async_remote_copy(
            src_ref=gain_out.at[at],
            dst_ref=gain_in.at[at],
            send_sem=gain_send.at[at],
            recv_sem=gain_recv.at[at],
            device_id=paired(axis, step),
            device_id_type=pl.DeviceIdType.MESH,
        )

    def swap_on(at):
        swap(at).wait_recv()
        total = gain_out[at] + gain_in[at]
        if at + 1 < len(steps):
            gain_out[at + 1] = total
            swap(at + 1).start()
        else:
            gains[...] = total

    send_units(min(2, max(depth - 2, 0)), 4)
    swap(0).start()
    for at in range(3):
        swap_on(at)

    lines[0].finish(qkv_total)
    rows = qkv_parts.shape[2] // 4
    for at in range(4):
        sent[at] = qkv_total[at * rows : (at + 1) * rows, :].astype(LOW)
    for at in range(3):
        exchange(0, at).start()
    back[mine] = sent[mine]
    if with_out:
        for number in range(1, depth - 1):
            lines[1].turn(number)
    swap_on(3)
    for kind in range(1, kinds):
        for at in range(3):
            exchange(kind, at).wait_recv()
    own_units.wait()
    spread_parts((grad_gate, grad_up), gu_back, UNIT_TILE, True)
    for at in range(4, len(steps)):
        swap_on(at)
    for at in range(3):
        exchange(0, at).wait_recv()
    spread_parts((grad_query, grad_key, grad_value), back, PAIR, deep)
    if with_out:
        lines[1].finish(out_total)
        grad_out[...] = out_total[...]

    for at in range(3):
        for kind in range(kinds):
            exchange(kind, at).wait_send()
    for at in range(len(steps)):
        swap(at).wait_send()
    plane.finish()
    for line in lines:
        line.close()


def last_call(deep, depth, rows, width, plane_operands, gu_rows, qkv_parts, out_parts):
    whole = pl.BlockSpec(memory_space=pltpu.VMEM)
    with_out = out_parts is not None
    there = pl.BlockSpec(memory_space=pl.ANY)
    parts = [gu_rows, qkv_parts] + ([out_parts] if with_out else [])
    operands = hbm(plane_operands[0]) + list(plane_operands[1:]) + hbm(*parts)
    in_specs = [there] + [whole] * (len(plane_operands) - 1) + [there] * len(parts)
    part_rows, part_width = qkv_parts.shape[2] // 4, qkv_parts.shape[3]
    outs = [like((rows, width), FULL), like((2, width), FULL)]
    outs += [like((part_rows, 2 * gu_rows.shape[2]), LOW)] * 2
    outs += [like((part_rows, 4 * part_width // 3), FULL)] * 3
    scratch = plane_scratch(rows, width) + line_scratch(depth, qkv_parts.shape)
    scratch.append(pltpu.VMEM(qkv_parts.shape[2:], FULL))
    if with_out:
        outs.append(like(out_parts.shape[2:], FULL))
        scratch += line_scratch(depth, out_parts.shape)
        scratch.append(pltpu.VMEM(out_parts.shape[2:], FULL))
    swaps = 3 + (depth - 1).bit_length()
    scratch += [
        pltpu.VMEM((4, part_rows, part_width), LOW),
        pltpu.VMEM((4, part_rows, part_width), LOW),
        pltpu.VMEM(gu_rows.shape, LOW),
        pltpu.SemaphoreType.DMA((1 + part_rows // 16, 3)),
        pltpu.SemaphoreType.DMA((1 + part_rows // 16, 3)),
        pltpu.SemaphoreType.DMA((1,)),
        pltpu.VMEM((swaps, 2, width), FULL),
        pltpu.VMEM((swaps, 2, width), FULL),
        pltpu.SemaphoreType.DMA((swaps,)),
        pltpu.SemaphoreType.DMA((swaps,)),
    ]
    return pl.pallas_call(
        functools.partial(last_kernel, deep, with_out),
        out_shape=outs,
        in_specs=in_specs,
        out_specs=[whole] * len(outs),
        scratch_shapes=scratch,
        compiler_params=pltpu.CompilerParams(
            collective_id=3, has_side_effects=True, vmem_limit_bytes=50 * 1024 * 1024
        ),
        cost_estimate=pl.CostEstimate(
            flops=rows * width * 100, bytes_accessed=rows * width * 400, transcendentals=0
        ),
    )(*operands)


class LineGather:
    def __init__(self, core_first, full, sems, columns=slice(None)):
        self.core_first, self.full, self.columns = core_first, full, columns
        self.right_send, self.right_recv, self.left_send, self.left_recv = sems[:4]
        self.core_send, self.core_recv = sems[4:]
        self.depth = full.shape[1 if core_first else 0]

    def copy(self, at, send, recv, device):
        core = lax.axis_index("c")
        block = (core, at) if self.core_first else (at, core)
        place = self.full.at[block + (slice(None), self.columns)]
        return pltpu.make_async_remote_copy(
            src_ref=place,
            dst_ref=place,
            send_sem=send.at[at],
            recv_sem=recv.at[at],
            device_id=device,
            device_id_type=pl.DeviceIdType.MESH,
        )

    def right(self, at):
        return self.copy(at, self.right_send, self.right_recv, beside(1))

    def left(self, at):
        return self.copy(at, self.left_send, self.left_recv, beside(-1))

    def core(self, at):
        return self.copy(at, self.core_send, self.core_recv, peer("c"))

    def pass_on(self, number):
        index, last = lax.axis_index("z"), self.depth - 1
        for step, move in ((1, self.right), (-1, self.left)):
            at = index - number * step
            inside = (at >= 0) & (at <= last)

            @pl.when(inside)
            def _():
                if number:
                    move(at).wait_recv()

                @pl.when((index < last) if step == 1 else (index > 0))
                def _():
                    move(at).start()

                if number or step == 1:
                    self.core(at).start()

    def close(self):
        index, last = lax.axis_index("z"), self.depth - 1
        for at in range(self.depth):
            self.core(at).wait()

            @pl.when((index < last) & (at <= index))
            def _():
                self.right(at).wait_send()

            @pl.when((index > 0) & (at >= index))
            def _():
                self.left(at).wait_send()


def first_kernel(with_out, *refs):
    refs = list(refs)

    def take(count):
        taken, refs[:count] = refs[:count], []
        return taken

    weights, (tokens, gain_parts) = take(5), take(2)
    w_out = take(1)[0] if with_out else None
    full_qkv, gu_rows, spread, gains = take(4)
    full_out = take(1)[0] if with_out else None
    spread_send, spread_recv, gain_all, gain_send, gain_recv = take(5)
    swap_send, swap_recv, local, qkv_parts, gu_parts = take(5)
    held, held_sems = take(5), take(1)[0]
    runs = full_qkv.shape[3] // QKV_RUNS
    runs = [pl.ds(at * runs, runs) for at in range(QKV_RUNS)]
    lines = [LineGather(True, full_qkv, take(6), run) for run in runs]
    if with_out:
        lines.insert(0, LineGather(False, full_out, take(6)))

    loads = [
        pltpu.make_async_copy(weight, kept, held_sems.at[at])
        for at, (weight, kept) in enumerate(zip(weights, held))
    ]
    for load in loads:
        load.start()
    depth = full_qkv.shape[1]
    at_z, at_x, at_c, at_y = (lax.axis_index(axis) for axis in AXES)
    mine = at_x * 2 + at_y
    steps = []
    step = 1
    while step < depth:
        steps.append(("z", step))
        step *= 2
    steps += [("c", 1), ("y", 1), ("x", 1)]
    index = ((at_x * 2 + at_y) * 2 + at_c) * depth + at_z
    far = [paired(axis, step) for axis, step in steps if step > 1]
    greet([peer("c"), peer("x"), peer("y"), peer("x", "y")] + far, line=True)

    def gather_parts(target, sources, tile, in_blocks):
        for part in range(4):
            for at in range(target.shape[2] // tile):
                source = sources[at % len(sources)]
                runs = part_columns(
                    source.shape[1], depth, in_blocks, part, at // len(sources) * tile, tile
                )
                pieces = [source[:, place : place + length] for _, place, length in runs]
                whole = pieces[0] if len(pieces) == 1 else jnp.concatenate(pieces, axis=1)
                target[part, :, at * tile : (at + 1) * tile] = whole

    for load in loads[:3]:
        load.wait()
    gather_parts(qkv_parts, held[:3], PAIR, with_out)
    members = [("y",), ("x",), ("x", "y")]
    part_rows = qkv_parts.shape[1]

    def exchange(kind, at):
        there = peer(*members[at])
        theirs = there.get("x", at_x) * 2 + there.get("y", at_y)
        source, target = gu_parts.at[theirs], gu_rows.at[mine]
        if kind < QKV_RUNS:
            source = qkv_parts.at[theirs, :, runs[kind]]
            target = full_qkv.at[at_c, at_z, pl.ds(mine * part_rows, part_rows), runs[kind]]
        return pltpu.make_async_remote_copy(
            src_ref=source,
            dst_ref=target,
            send_sem=swap_send.at[kind, at],
            recv_sem=swap_recv.at[kind, at],
            device_id=there,
            device_id_type=pl.DeviceIdType.MESH,
        )

    own_qkv = pltpu.make_async_copy(
        qkv_parts.at[mine],
        full_qkv.at[at_c, at_z, pl.ds(mine * part_rows, part_rows)],
        local.at[0],
    )
    own_gu = pltpu.make_async_copy(gu_parts.at[mine], gu_rows.at[mine], local.at[1])
    for kind in range(QKV_RUNS):
        for at in (2, 0, 1):
            exchange(kind, at).start()
    own_qkv.start()
    if with_out:
        own_out = pltpu.make_async_copy(w_out, full_out.at[at_z, at_c], local.at[2])
        own_out.start()

    def swap(at):
        axis, step = steps[at]
        count = 2**at
        place = gain_all.at[pl.ds((index // count) * count, count)]
        return pltpu.make_async_remote_copy(
            src_ref=place,
            dst_ref=place,
            send_sem=gain_send.at[at],
            recv_sem=gain_recv.at[at],
            device_id=paired(axis, step),
            device_id_type=pl.DeviceIdType.MESH,
        )

    gain_all[index] = gain_parts[0]
    for at in range(len(steps)):
        swap(at).start()
        if at == 1:
            for load in loads[3:]:
                load.wait()
            gather_parts(gu_parts, held[3:], UNIT_TILE, True)
            own_gu.start()
        swap(at).wait_recv()
        if at == len(steps) - 3:
            own_qkv.wait()
        kind = at - (len(steps) - 3)
        if 0 <= kind < QKV_RUNS:
            for other in range(3):
                exchange(kind, other).wait_recv()
            lines[kind - QKV_RUNS].pass_on(0)
        if at == len(steps) - 4 and with_out:
            own_out.wait()
            lines[0].pass_on(0)
    each = gain_parts.shape[2]
    for at in range(8 * depth):
        x, y, c, z = at // (4 * depth), at // (2 * depth) % 2, at // depth % 2, at % depth
        place = (((z * 2 + x) * 2 + c) * 2 + y) * each
        gains[:, place : place + each] = gain_all[at]

    plane = PlaneSum(None, tokens, None, None, None, spread_send, spread_recv, None, None, spread)
    gain = gains[0:1, :]
    for half, at in plane.pieces:
        values = tokens[plane.span(0, half, at), :].astype(FULL)
        plane.give(half, at, mix((values * factor_of(values) * gain).astype(LOW), depth))
    for at in range(3):
        exchange(QKV_RUNS, at).start()

    todo = list(plane.pieces)
    share = -(-len(todo) // max(1, depth - 1))
    for number in range(1, depth):
        for line in lines:
            line.pass_on(number)
        for half, at in todo[(number - 1) * share : number * share]:
            plane.forward(half, at)
    for half, at in plane.pieces:
        plane.close_spread(half, at)
    own_gu.wait()
    for at in range(3):
        for kind in range(QKV_RUNS):
            exchange(kind, at).wait_send()
        exchange(QKV_RUNS, at).wait()
    for at in range(len(steps)):
        swap(at).wait_send()
    for line in lines:
        line.close()


def first_call(depth, weights, tokens, gain_parts, w_out):
    rows, width = tokens.shape
    whole = pl.BlockSpec(memory_space=pltpu.VMEM)
    there = pl.BlockSpec(memory_space=pl.ANY)
    operands = hbm(*weights) + [tokens, gain_parts]
    in_specs = [there] * len(weights) + [whole, whole]
    part_rows, part_width, part_units = weights[0].shape[0], 3 * width // 4, weights[3].shape[1] // 2
    outs = [
        in_hbm((2, depth, 4 * part_rows, part_width), LOW),
        in_hbm((4, part_rows, part_units), LOW),
        in_hbm((4 * rows, width), LOW),
        like((2, width), FULL),
    ]
    out_specs = [there, there, whole, whole]
    swaps = 3 + (depth - 1).bit_length()
    scratch = [
        pltpu.SemaphoreType.DMA((6, 2, PIECES)),
        pltpu.SemaphoreType.DMA((6, 2, PIECES)),
        pltpu.VMEM((8 * depth, 2, width // (8 * depth)), FULL),
        pltpu.SemaphoreType.DMA((swaps,)),
        pltpu.SemaphoreType.DMA((swaps,)),
        pltpu.SemaphoreType.DMA((QKV_RUNS + 1, 3)),
        pltpu.SemaphoreType.DMA((QKV_RUNS + 1, 3)),
        pltpu.SemaphoreType.DMA((3,)),
        pltpu.VMEM((4, part_rows, part_width), LOW),
        pltpu.VMEM((4, part_rows, part_units), LOW),
    ]
    scratch += [pltpu.VMEM(weight.shape, LOW) for weight in weights]
    scratch.append(pltpu.SemaphoreType.DMA((len(weights),)))
    scratch += [pltpu.SemaphoreType.DMA((depth,))] * (6 * QKV_RUNS)
    if w_out is not None:
        operands.append(w_out)
        in_specs.append(there)
        outs.append(in_hbm((depth, 2) + w_out.shape, LOW))
        out_specs.append(there)
        scratch += [pltpu.SemaphoreType.DMA((depth,))] * 6
    return pl.pallas_call(
        functools.partial(first_kernel, w_out is not None),
        out_shape=outs,
        in_specs=in_specs,
        out_specs=out_specs,
        scratch_shapes=scratch,
        compiler_params=pltpu.CompilerParams(
            collective_id=4, has_side_effects=True, vmem_limit_bytes=24 * 1024 * 1024
        ),
        cost_estimate=pl.CostEstimate(
            flops=rows * width * 100, bytes_accessed=rows * width * 200, transcendentals=0
        ),
    )(*operands)


def plane_scratch(rows, width):
    step = rows // (2 * PIECES)
    return [
        pltpu.VMEM((2, PIECES, 2, step, width), LOW),
        pltpu.VMEM((2, PIECES, step, width), LOW),
        pltpu.VMEM((2, PIECES, step, width), LOW),
        pltpu.SemaphoreType.DMA((6, 2, PIECES)),
        pltpu.SemaphoreType.DMA((6, 2, PIECES)),
        pltpu.VMEM((2, rows // 2, width), LOW),
        pltpu.SemaphoreType.DMA((2,)),
    ]


def plane_call(kernel, number, rows, width, outs, gain, *operands):
    whole = pl.BlockSpec(memory_space=pltpu.VMEM)
    there = pl.BlockSpec(memory_space=pl.ANY)
    loaded = operands[1:]
    return pl.pallas_call(
        kernel,
        out_shape=outs,
        in_specs=[there] * len(operands) + [whole],
        out_specs=[whole] * len(outs),
        scratch_shapes=plane_scratch(rows, width)
        + [pltpu.VMEM(item.shape, item.dtype) for item in loaded]
        + [pltpu.SemaphoreType.DMA((len(loaded),))],
        compiler_params=pltpu.CompilerParams(
            collective_id=number, has_side_effects=True, vmem_limit_bytes=32 * 1024 * 1024
        ),
        cost_estimate=pl.CostEstimate(
            flops=rows * width * 100, bytes_accessed=rows * width * 200, transcendentals=0
        ),
    )(*hbm(*operands), gain)


def body(
    tokens,
    cotangent,
    seq_lengths,
    assignment,
    w_query,
    w_key,
    w_value,
    w_out,
    w_gate,
    w_up,
    w_down,
    gain_attn,
    gain_mlp,
):
    rows, width = tokens.shape
    depth = lax.axis_size("z")
    at_z, at_x, at_c, at_y = (lax.axis_index(axis) for axis in AXES)
    mine = at_x * 2 + at_y
    whole_heads = w_out.shape[0] % HEAD_DIM == 0
    head_deep = depth if whole_heads else 0
    head_width = width // 4

    def in_order(weight, back=False):
        if blocks_align(width, depth):
            return weight
        order = (2, 0, 1, 3, 4) if back else (1, 2, 0, 3, 4)
        shape = (depth, 2, 2) if back else (2, depth, 2)
        apart = weight.reshape(shape + (-1, weight.shape[1]))
        return apart.transpose(order).reshape(weight.shape)

    def core_columns(values, core):
        if blocks_align(width, depth):
            return lax.dynamic_slice_in_dim(values, core * (width // 2), width // 2, axis=1)
        apart = values.reshape(values.shape[0], depth, 2, 2, -1)
        part = lax.dynamic_index_in_dim(apart, core, 3, keepdims=False)
        return part.reshape(values.shape[0], -1)

    slot_at = [(at_z * 2 + x) * 2 + at_c for x in (at_x, 1 - at_x)]
    slot_length = [seq_lengths[assignment[slot]] for slot in slot_at]
    row = jnp.arange(rows)
    valid_rows = (at_y * rows + row < slot_length[0]).astype(FULL)[:, None]

    full_qkv, gu_rows, normed_all, gains, *rest = first_call(
        depth,
        (w_query, w_key, w_value, w_gate, w_up),
        tokens,
        jnp.stack([gain_attn, gain_mlp])[None].astype(FULL),
        w_out if whole_heads else None,
    )
    full_qkv = in_order(full_qkv.reshape(width, -1))
    gain_one, gain_two = gains[0], gains[1]
    full_gu = lax.all_gather(
        gu_rows.reshape(-1, gu_rows.shape[2]), ("c", "z"), axis=0, tiled=True
    )
    full_gu = in_order(full_gu)
    if whole_heads:
        full_out = rest[0].reshape(-1, width)
    else:
        every = lax.all_gather(w_out, AXES, axis=0, tiled=True)
        full_out = lax.dynamic_slice_in_dim(every, mine * head_width, head_width, axis=0)
    w_down, normed_all = lax.optimization_barrier((w_down, normed_all))

    grad_out = cotangent.astype(FULL) * valid_rows
    grad_low = grad_out.astype(LOW)
    normed_all, grad_low = lax.optimization_barrier((normed_all, grad_low))
    near = plane_gather_near(grad_low)
    qkv = dot(normed_all, full_qkv)
    qkv, near = lax.optimization_barrier((qkv, near))
    far = plane_gather_far(grad_low, near)
    cosine, sine = rope_tables(jnp.arange(2 * rows))
    info = jnp.stack([at_y.astype(jnp.int32)] + slot_length)
    heads_out, lse, qkv = attend(info, qkv, cosine, sine)
    w_down, heads_out, far = lax.optimization_barrier((w_down, heads_out, far))
    grad_low_all = plane_gathered(grad_low, near, far)
    full_down = lax.all_gather(w_down, ("z", "c"), axis=0, tiled=True)
    branch_low, branch_own = project(heads_out[None], full_out, False)
    attended, normed2_all = plane_call(
        forward_kernel,
        1,
        rows,
        width,
        [like((rows, width), FULL), in_hbm((4 * rows, width), LOW)],
        gain_two[None],
        branch_low,
        branch_own,
        tokens,
    )
    both, active = activate(normed2_all, full_gu)

    down_part = dot_rows(active, grad_low_all).astype(LOW)
    grad_w_down = lax.psum_scatter(down_part, ("z", "c"), scatter_dimension=0, tiled=True)
    grad_w_down = grad_w_down.astype(FULL)
    down_part, grad_low_all = lax.optimization_barrier((down_part, grad_low_all))
    grad_gu = activate_back(grad_low_all, full_down, both)
    theirs = dot_rows(core_columns(normed2_all, 1 - at_c), grad_gu).astype(LOW)
    from_core = swap_c(theirs)
    theirs, grad_gu = lax.optimization_barrier((theirs, grad_gu))
    back_low, back_own = project(grad_gu[None], full_gu, True)
    back_low, from_core, grad_gu = lax.optimization_barrier((back_low, from_core, grad_gu))
    ours = dot_rows(core_columns(normed2_all, at_c), grad_gu) + from_core.astype(FULL)
    grad_gu_rows = lax.psum_scatter(ours.astype(LOW), "z", scatter_dimension=0, tiled=True)
    ours, back_low = lax.optimization_barrier((ours, back_low))
    grad_attended, grad_gain_mlp, grad_branch = plane_call(
        backward_kernel,
        2,
        rows,
        width,
        [like((rows, width), FULL), like((1, width), FULL), in_hbm((4 * rows, width), LOW)],
        gain_two[None],
        back_low,
        back_own,
        attended,
        grad_out,
    )
    grad_branch, active = lax.optimization_barrier((grad_branch, active))

    grad_w_out = dot_rows(heads_out, grad_branch)
    out_parts = None
    if whole_heads:
        out_parts = grad_w_out.astype(LOW).reshape(depth, 2, -1, width)
    else:
        spread = lax.dynamic_update_slice_in_dim(
            jnp.zeros((width, width), FULL), grad_w_out, mine * head_width, axis=0
        )
        grad_w_out = lax.psum_scatter(spread, AXES, scatter_dimension=0, tiled=True)
    grad_mixed = dot_through(grad_branch, full_out).astype(LOW)
    last_low, last_own = project(active[None], full_down, False)
    last_low, grad_mixed = lax.optimization_barrier((last_low, grad_mixed))
    near = plane_reduce_near(last_low)
    grad_qkv = attend_back(info, qkv, grad_mixed, lse, cosine, sine)
    grad_qkv, near, grad_w_down = lax.optimization_barrier((grad_qkv, near, grad_w_down))
    far = plane_reduce_far(last_low, near)
    grad_qkv_part = in_order(dot_rows(normed_all, grad_qkv).astype(LOW), True)
    back_low, back_own = project(grad_qkv[None], full_qkv, True)
    back_low, far = lax.optimization_barrier((back_low, far))
    result = attended + plane_reduced(last_own, near, far)
    output = (result * valid_rows).astype(LOW)
    grad_input, grad_gains, *last_weights = last_call(
        head_deep,
        depth,
        rows,
        width,
        [
            back_low,
            back_own,
            tokens,
            gain_one[None],
            grad_gain_mlp,
        ],
        grad_gu_rows.reshape(4, -1, grad_gu_rows.shape[1]),
        grad_qkv_part.reshape(2, depth, -1, grad_qkv_part.shape[1]),
        out_parts,
    )
    grad_w_gate, grad_w_up, grad_w_query, grad_w_key, grad_w_value = last_weights[:5]
    grad_w_gate, grad_w_up = grad_w_gate.astype(FULL), grad_w_up.astype(FULL)
    grad_input = grad_input + grad_attended
    if whole_heads:
        grad_w_out = last_weights[5]
    index = ((at_z * 2 + at_x) * 2 + at_c) * 2 + at_y
    part = width // (8 * depth)
    grad_gains = lax.dynamic_slice_in_dim(grad_gains, index * part, part, axis=1)
    return (
        output,
        grad_input,
        grad_w_query,
        grad_w_key,
        grad_w_value,
        grad_w_out,
        grad_w_gate,
        grad_w_up,
        grad_w_down,
        grad_gains[0],
        grad_gains[1],
    )


def solution(mesh):
    shape = (mesh.shape["dp"] // 4, 2, 2, mesh.shape["seq"])
    grid = Mesh(mesh.devices.reshape(shape), AXES)
    split = P(AXES, None)
    part = P(AXES)
    return jax.shard_map(
        body,
        mesh=grid,
        in_specs=(split, split, P(), P()) + (split,) * 7 + (part, part),
        out_specs=(split,) * 9 + (part, part),
        check_vma=False,
    )
```
